32 devices in a mesh: rows: 8 (over z, x), head: 4 (over y, core).
Axes of the slice: x: 2, y: 2, z: 4, core: 2. Of those that a mesh axis runs over, the one named last changes fastest.
Arguments:
- media: bfloat16 [32, 256, 1536], P('rows', 'head'), may hold values from -6 to 6
- latents: bfloat16 [32, 64, 1536], P('rows', 'head'), may hold values from -6 to 6
- counts: int32 [4], replicated, may hold values from 1 to 8, 20 in all
- media_gain: float32 [1536], replicated, may hold values from 0.1 to 1.9
- media_shift: float32 [1536], replicated, may hold values from -1.5 to 1.5
- latent_gain: float32 [1536], replicated, may hold values from 0.1 to 1.9
- latent_shift: float32 [1536], replicated, may hold values from -1.5 to 1.5
- w_query: bfloat16 [1536, 1536], replicated, may hold values from -0.15625 to 0.15625
- w_key: bfloat16 [1536, 1536], replicated, may hold values from -0.15625 to 0.15625
- w_value: bfloat16 [1536, 1536], replicated, may hold values from -0.15625 to 0.15625
- w_out: bfloat16 [1536, 1536], replicated, may hold values from -1.25 to 1.25
- ffn_gain: float32 [1536], replicated, may hold values from 0.1 to 1.9
- ffn_shift: float32 [1536], replicated, may hold values from -1.5 to 1.5
- w_up: bfloat16 [1536, 6144], replicated, may hold values from -0.15625 to 0.15625
- w_down: bfloat16 [6144, 1536], replicated, may hold values from -0.078125 to 0.078125
- cotangent: bfloat16 [32, 64, 1536], P('rows', 'head'), may hold values from -6 to 6
Outputs:
- latents_out: float32 [32, 64, 1536], P('rows', 'head')
- media_grad: float32 [32, 256, 1536], P('rows', 'head')
- latents_grad: float32 [32, 64, 1536], P('rows', 'head')
- media_gain_grad: float32 [1536], P(('rows', 'head'))
- media_shift_grad: float32 [1536], P(('rows', 'head'))
- latent_gain_grad: float32 [1536], P(('rows', 'head'))
- latent_shift_grad: float32 [1536], P(('rows', 'head'))
- query_grad: float32 [1536, 1536], P('rows', 'head')
- key_grad: float32 [1536, 1536], P('rows', 'head')
- value_grad: float32 [1536, 1536], P('rows', 'head')
- out_grad: float32 [1536, 1536], P('rows', 'head')
- ffn_gain_grad: float32 [1536], P(('rows', 'head'))
- ffn_shift_grad: float32 [1536], P(('rows', 'head'))
- up_grad: float32 [1536, 6144], P('rows', 'head')
- down_grad: float32 [6144, 1536], P('head', 'rows')
The draws below stay inside these ranges and needn't reach their ends.
Inputs may be any that keep to these rules, and one draw needn't show every extreme that they name: At most 8 images in a sequence, and some sequence has exactly 8; the counts sum to 20.
All inputs are finite; a program needn't handle non-finite values.
Results may differ from the reference program's by a relative error of at most 0.017.
Values may be sent and summed in bfloat16 or wider, within the bound.
A program may use at most 192 MiB of HBM per device.

```python
import math
import jax
import jax.numpy as jnp
import numpy as np
from jax import lax

D = 1536
HEADS = 16
HEAD_DIM = 96
FF = 6144
LAT = 64
PATCH = 256
MAX_IMG = 8
IMAGES = 32
SEQS = 4


def level_of(key, extent, split, smallest, top_value):
    level = 1.0
    for position, shards_of in split:
        steps = jax.random.uniform(jax.random.fold_in(jax.random.fold_in(key, 6), position), (shards_of,), jnp.float32, smallest / len(split), top_value / len(split))
        level = level * jnp.repeat(jnp.exp(steps), extent[position] // shards_of).reshape((-1,) + (1,) * (len(extent) - 1 - position))
    return level


def length_profile(count, total, bound, slope):
    weights = [(1 << 20) // math.isqrt(standing ** slope) + 1 for standing in range(2, count + 1)]
    spare, given = total - bound - (count - 1), [1] * (count - 1)
    while spare > 0:
        candidates = [i for i in range(count - 1) if given[i] < bound]
        whole, remaining = sum([weights[i] for i in candidates]), spare
        for i in candidates:
            extra = min(bound - given[i], max(1, remaining * weights[i] // whole), spare)
            given[i] = given[i] + extra
            spare = spare - extra
    return np.array([bound] + given)


def uneven_parts(key, count, total, limit, skew):
    if count == 2:
        one = jax.random.randint(key, (), max(1, total - limit), min(limit, total - 1) + 1)
        return jnp.stack([one, total - one])
    sizes = jnp.asarray(length_profile(count, total, limit, skew), jnp.int32)
    pairs = (count - 1) // 2
    giver, taker = sizes[1:1 + 2 * pairs:2], sizes[2:2 + 2 * pairs:2]
    margin = jnp.minimum(giver - 1, limit - taker)
    shifted = jax.random.randint(jax.random.fold_in(key, 1), (pairs,), 0, 1 << 20) % (margin + 1)
    sizes = sizes.at[1:1 + 2 * pairs:2].set(giver - shifted).at[2:2 + 2 * pairs:2].set(taker + shifted)
    return sizes[jax.random.permutation(jax.random.fold_in(key, 2), count)]


def gaussian(stream_key, dims, scale, limit, split=(), held_as=jnp.bfloat16):
    level = level_of(stream_key, dims, split, -0.22, 0.18) if split else 1.0
    drawn = jax.random.normal(stream_key, dims, jnp.float32) * scale * level
    return jnp.minimum(jnp.maximum(drawn, -limit), limit).astype(held_as)


def setup_inputs(seed: int = 0) -> dict:
    arg_keys = jax.random.split(jax.random.key(seed), 17)
    return {
        "media": gaussian(arg_keys[0], (IMAGES, PATCH, D), 1.0, 6.0, ((0, 8), (1, 4))),
        "latents": gaussian(arg_keys[1], (IMAGES, LAT, D), 1.0, 6.0, ((0, 8), (1, 4))),
        "counts": uneven_parts(arg_keys[2], SEQS, IMAGES * 5 // 8, MAX_IMG, 1).astype(jnp.int32),
        "media_gain": jnp.clip(1.0 + 0.18 * jax.random.normal(arg_keys[3], (D,), jnp.float32), 0.1, 1.9),
        "media_shift": gaussian(arg_keys[4], (D,), 0.3, 1.5, (), jnp.float32),
        "latent_gain": jnp.clip(1.0 + 0.18 * jax.random.normal(arg_keys[5], (D,), jnp.float32), 0.1, 1.9),
        "latent_shift": gaussian(arg_keys[6], (D,), 0.3, 1.5, (), jnp.float32),
        "w_query": gaussian(arg_keys[7], (D, D), D ** -0.5, 0.15625),
        "w_key": gaussian(arg_keys[8], (D, D), D ** -0.5, 0.15625),
        "w_value": gaussian(arg_keys[9], (D, D), D ** -0.5, 0.15625),
        "w_out": gaussian(arg_keys[10], (D, D), (D // 64) ** -0.5, 1.25),
        "ffn_gain": jnp.clip(1.0 + 0.18 * jax.random.normal(arg_keys[11], (D,), jnp.float32), 0.1, 1.9),
        "ffn_shift": gaussian(arg_keys[12], (D,), 0.3, 1.5, (), jnp.float32),
        "w_up": gaussian(arg_keys[13], (D, FF), D ** -0.5, 0.15625),
        "w_down": gaussian(arg_keys[14], (FF, D), FF ** -0.5, 0.078125),
        "cotangent": gaussian(arg_keys[15], (IMAGES, LAT, D), 1.0, 6.0, ((0, 8), (1, 4))),
    }


@jax.custom_vjp
def low(v):
    return lax.optimization_barrier(v.astype(jnp.bfloat16)).astype(jnp.float32)

@jax.custom_vjp
def low_back(v):
    return v

def low_keep(v):
    return (low(v), None)

def low_pass(kept, grad):
    return (grad,)

def back_keep(v):
    return (v, None)

def back_low(kept, grad):
    return (low(grad),)
low.defvjp(low_keep, low_pass)
low_back.defvjp(back_keep, back_low)
epsilon = 1e-05
highest = lax.Precision.HIGHEST

def normalize(values, norm_gain, norm_shift):
    row_mean = lax.optimization_barrier(jnp.mean(values, axis=-1, keepdims=True))
    centered = values - row_mean
    variance = lax.optimization_barrier(jnp.mean(centered * centered, axis=-1, keepdims=True))
    return centered * lax.rsqrt(variance + epsilon) * norm_gain + norm_shift

def layer(media, latents, media_gain, media_shift, latent_gain, latent_shift, w_query, w_key, w_value, w_out, ffn_gain, ffn_shift, w_up, w_down):
    images = latents.shape[0]
    score_scale = 1.0 / math.sqrt(HEAD_DIM)
    media_norm = low(normalize(media, media_gain, media_shift))
    latent_norm = low(normalize(latents, latent_gain, latent_shift))
    query = low_back(low(jnp.einsum('ild,de->ile', latent_norm, w_query, precision=highest)))
    key_rows = jnp.concatenate([media_norm, latent_norm], axis=1)
    keys = low_back(low(jnp.einsum('ikd,de->ike', key_rows, w_key, precision=highest)))
    values = low_back(low(jnp.einsum('ikd,de->ike', key_rows, w_value, precision=highest)))
    query_heads = query.reshape(images, LAT, HEADS, HEAD_DIM)
    key_heads = keys.reshape(images, PATCH + LAT, HEADS, HEAD_DIM)
    value_heads = values.reshape(images, PATCH + LAT, HEADS, HEAD_DIM)
    scores = low_back(jnp.einsum('iqhe,ikhe->ihqk', query_heads, key_heads, precision=highest) * score_scale)
    attn_probs = low(jax.nn.softmax(scores, axis=-1))
    mixed = jnp.einsum('ihqk,ikhe->iqhe', attn_probs, value_heads, precision=highest).reshape(images, LAT, D)
    mixed = low_back(low(mixed))
    residual = latents + low_back(jnp.einsum('ild,de->ile', mixed, w_out, precision=highest))
    ffn_norm = low(normalize(residual, ffn_gain, ffn_shift))
    hidden = low_back(jnp.einsum('ild,df->ilf', ffn_norm, w_up, precision=highest))
    activated = low(jax.nn.gelu(hidden))
    return residual + jnp.einsum('ilf,fd->ild', activated, w_down, precision=highest)

def image_mask(counts):
    image_ids = jnp.arange(IMAGES, dtype=jnp.int32)
    sequence = image_ids // MAX_IMG
    slot_ids = image_ids % MAX_IMG
    seq_table = jnp.arange(counts.shape[0], dtype=jnp.int32)
    seq_limit = lax.optimization_barrier(jnp.sum(jnp.where(sequence[:, None] == seq_table[None, :], counts[None, :], 0), axis=1))
    return (slot_ids < seq_limit).astype(jnp.float32)

def reference(media, latents, counts, media_gain, media_shift, latent_gain, latent_shift, w_query, w_key, w_value, w_out, ffn_gain, ffn_shift, w_up, w_down, cotangent):
    inputs = [operand.astype(jnp.float32) for operand in (media, latents, media_gain, media_shift, latent_gain, latent_shift, w_query, w_key, w_value, w_out, ffn_gain, ffn_shift, w_up, w_down)]
    output, pullback = jax.vjp(layer, *inputs)
    live_mask = image_mask(counts)
    gradients = pullback(cotangent.astype(jnp.float32) * live_mask[:, None, None])
    return (output, gradients[0], gradients[1], gradients[2], gradients[3], gradients[4], gradients[5], gradients[6], gradients[7], gradients[8], gradients[9], gradients[10], gradients[11], gradients[12], gradients[13])
```

```python
import functools
import math

import jax
import jax.numpy as jnp
from jax import lax
from jax.experimental import pallas as pl
from jax.experimental.pallas import tpu as pltpu
from jax.sharding import PartitionSpec as P

HEAD_DIM = 96
MAX_IMG = 8
EPSILON = 1e-05
BF = jnp.bfloat16
F32 = jnp.float32
MESH = pl.DeviceIdType.MESH
ANY = pl.BlockSpec(memory_space=pl.ANY)


def factor_rows(count):
    nz = 4 if count % 4 == 0 else 1
    return nz, count // nz


def factor_head(count):
    nc = 2 if count % 2 == 0 else 1
    return count // nc, nc


def standardize(values):
    row_mean = jnp.mean(values, axis=-1, keepdims=True)
    centered = values - row_mean
    variance = jnp.mean(centered * centered, axis=-1, keepdims=True)
    inv_scale = lax.rsqrt(variance + EPSILON)
    return centered * inv_scale, inv_scale


def norm_back(d_scaled, normed, inv_scale):
    first_mean = jnp.mean(d_scaled, axis=-1, keepdims=True)
    second_mean = jnp.mean(d_scaled * normed, axis=-1, keepdims=True)
    return inv_scale * (d_scaled - first_mean - normed * second_mean)


def dot(a, b, dims):
    return lax.dot_general(a, b, (dims, ((), ())), preferred_element_type=F32)


class Place:
    def __init__(self, rows, heads):
        self.rows, self.heads = rows, heads
        self.nz, self.nx = factor_rows(rows)
        self.ny, self.nc = factor_head(heads)
        self.r = lax.axis_index("rows")
        self.h = lax.axis_index("head")
        self.z, self.x = self.r // self.nx, self.r % self.nx
        self.y, self.c = self.h // self.nc, self.h % self.nc

    def head_peers(self):
        return [(self.r, lax.rem(self.h + d, self.heads)) for d in range(1, self.heads)]

    def x_peer(self, d):
        return lax.rem(self.x + d, self.nx)

    def z_peer(self, d):
        return lax.rem(self.z + d, self.nz)

    def y_peer(self, d):
        return lax.rem(self.y + d, self.ny)


def greet(peers):
    barrier = pltpu.get_barrier_semaphore()
    for peer in peers:
        pl.semaphore_signal(barrier, inc=1, device_id=peer, device_id_type=MESH)
    pl.semaphore_wait(barrier, len(peers))


def remote(src, dst, sems, slot, peer):
    return pltpu.make_async_remote_copy(
        src_ref=src,
        dst_ref=dst,
        send_sem=sems[0].at[slot],
        recv_sem=sems[1].at[slot],
        device_id=peer,
        device_id_type=MESH,
    )


def run_kernel(kernel, name, ident, out_shapes, semaphores, *operands, scratch=()):
    return pl.pallas_call(
        kernel,
        name=name,
        out_shape=out_shapes,
        in_specs=[ANY] * len(operands),
        out_specs=jax.tree.map(lambda _: ANY, out_shapes),
        scratch_shapes=[pltpu.SemaphoreType.DMA((semaphores,))] * 2
        + [pltpu.SemaphoreType.DMA((len(operands),))]
        + list(scratch),
        compiler_params=pltpu.CompilerParams(collective_id=ident, has_side_effects=True),
    )(*operands)


def gather_head_kernel(rows, heads, count, put_second, *refs):
    ins, outs = refs[:count], refs[count : 2 * count]
    sems, local = refs[2 * count : 2 * count + 2], refs[2 * count + 2]
    at = Place(rows, heads)

    def slot(ref, head):
        return ref.at[:, head] if put_second else ref.at[head]

    greet(at.head_peers())
    partner = (at.r, at.y * at.nc + (at.nc - 1 - at.c))
    own, far, near, relay = [], [], [], []
    per = 2 * at.ny
    for i in range(count):
        for d in range(1, at.ny):
            peer = (at.r, at.y_peer(d) * at.nc + at.c)
            copy = remote(ins[i], slot(outs[i], at.h), sems, i * per + d, peer)
            copy.start()
            far.append((i, d, copy))
        if at.nc > 1:
            copy = remote(ins[i], slot(outs[i], at.h), sems, i * per, partner)
            copy.start()
            near.append(copy)
        copy = pltpu.make_async_copy(ins[i], slot(outs[i], at.h), local.at[i])
        copy.start()
        own.append(copy)
    for i, d, copy in far:
        copy.wait_recv()
        source = at.y_peer(at.ny - d) * at.nc + at.c
        if at.nc > 1:
            block = slot(outs[i], source)
            hop = remote(block, block, sems, i * per + at.ny + d, partner)
            hop.start()
            relay.append(hop)
    for copy in near:
        copy.wait_recv()
    for copy in relay:
        copy.wait_recv()
    for copy in own:
        copy.wait()
    for _, _, copy in far:
        copy.wait_send()
    for copy in near + relay:
        copy.wait_send()


def gather_head(name, ident, rows, heads, put_second, *operands):
    shapes = []
    for array in operands:
        shape = array.shape
        shape = shape[:1] + (heads,) + shape[1:] if put_second else (heads,) + shape
        shapes.append(jax.ShapeDtypeStruct(shape, array.dtype))
    ny, _ = factor_head(heads)
    kernel = functools.partial(gather_head_kernel, rows, heads, len(operands), put_second)
    return run_kernel(kernel, name, ident, shapes, len(operands) * 2 * ny, *operands)


def exchange_kernel(rows, heads, axis, ways, count, *refs):
    ins, outs = refs[:count], refs[count : 2 * count]
    sems = refs[2 * count : 2 * count + 2]
    at = Place(rows, heads)
    peers = []
    for a in ways:
        peers += exchange_peers(at, a)
    greet([peer for peer, _ in peers])
    copies = []
    slot = 0
    for i in range(count):
        for d, (peer, index) in enumerate(exchange_peers(at, axis[i])):
            copy = remote(ins[i].at[index], outs[i].at[d], sems, slot, peer)
            copy.start()
            copies.append(copy)
            slot += 1
    for copy in copies:
        copy.wait()


def exchange_peers(at, axis):
    if axis == "head":
        return [((at.r, lax.rem(at.h + d, at.heads)), lax.rem(at.h + d, at.heads)) for d in range(1, at.heads)]
    if axis == "x":
        return [((at.z * at.nx + at.x_peer(d), at.h), at.x_peer(d)) for d in range(1, at.nx)]
    if axis == "z":
        return [((at.z_peer(d) * at.nx + at.x, at.h), at.z_peer(d)) for d in range(1, at.nz)]
    if axis == "y":
        return [((at.r, at.y_peer(d) * at.nc + at.c), at.y_peer(d)) for d in range(1, at.ny)]
    return [((at.r, at.y * at.nc + (at.nc - 1 - at.c)), at.nc - 1 - at.c)]


def exchange(name, ident, rows, heads, axis, *operands):
    shapes = [jax.ShapeDtypeStruct((a.shape[0] - 1,) + a.shape[1:], a.dtype) for a in operands]
    ways = sorted(set(axis))
    total = sum(a.shape[0] - 1 for a in operands)
    kernel = functools.partial(exchange_kernel, rows, heads, axis, ways, len(operands))
    return run_kernel(kernel, name, ident, shapes, total, *operands)


def attend_kernel(q_ref, k_ref, v_ref, o_ref):
    width = q_ref.shape[-1]
    scale = 1.0 / math.sqrt(HEAD_DIM)
    for n in range(width // HEAD_DIM):
        part = slice(n * HEAD_DIM, (n + 1) * HEAD_DIM)
        q, k, v = q_ref[0, :, part], k_ref[0, :, part], v_ref[0, :, part]
        scores = dot(q, k, ((1,), (1,))) * scale
        top = jnp.max(scores, axis=-1, keepdims=True)
        powers = jnp.exp(scores - top)
        total = jnp.sum(powers, axis=-1, keepdims=True)
        probs = (powers * (1.0 / total)).astype(BF)
        o_ref[0, :, part] = dot(probs, v, ((1,), (0,))).astype(BF)


def attend_back_kernel(q_ref, k_ref, v_ref, d_ref, dq_ref, dk_ref, dv_ref):
    width = q_ref.shape[-1]
    scale = 1.0 / math.sqrt(HEAD_DIM)
    for n in range(width // HEAD_DIM):
        part = slice(n * HEAD_DIM, (n + 1) * HEAD_DIM)
        q, k, v, d = q_ref[0, :, part], k_ref[0, :, part], v_ref[0, :, part], d_ref[0, :, part]
        scores = dot(q, k, ((1,), (1,))) * scale
        top = jnp.max(scores, axis=-1, keepdims=True)
        powers = jnp.exp(scores - top)
        probs = powers * (1.0 / jnp.sum(powers, axis=-1, keepdims=True))
        d_probs = dot(d, v, ((1,), (1,)))
        inner = jnp.sum(probs * d_probs, axis=-1, keepdims=True)
        d_scores = (probs * (d_probs - inner)).astype(BF)
        dq_ref[0, :, part] = (dot(d_scores, k, ((1,), (0,))) * scale).astype(BF)
        dk_ref[0, :, part] = (dot(d_scores, q, ((0,), (0,))) * scale).astype(BF)
        dv_ref[0, :, part] = dot(probs.astype(BF), d, ((0,), (0,))).astype(BF)


def per_image(kernel, name, outs, *operands):
    def spec(array):
        return pl.BlockSpec((1,) + array.shape[1:], lambda i: (i, 0, 0))

    return pl.pallas_call(
        kernel,
        name=name,
        grid=(operands[0].shape[0],),
        in_specs=[spec(a) for a in operands],
        out_specs=[spec(a) for a in outs],
        out_shape=outs,
    )(*operands)


def body(
    media, latents, counts, media_gain, media_shift, latent_gain, latent_shift, w_query, w_key, w_value, w_out,
    ffn_gain, ffn_shift, w_up, w_down, cotangent,
):
    rows, heads = lax.axis_size("rows"), lax.axis_size("head")
    at = Place(rows, heads)
    nz, nx, ny, nc = at.nz, at.nx, at.ny, at.nc
    images, patch, width = media.shape
    lat = latents.shape[1]
    hidden_width = w_up.shape[1]
    cols = width // heads
    mine = hidden_width // heads
    lat_rows = heads * lat
    key_count = heads * (patch + lat)

    media_all, lat_all, cot_all = gather_head("gather_inputs", 1, rows, heads, True, media, latents, cotangent)
    wide_all = lat_all.astype(F32)
    media_hat_all, _ = standardize(media_all.astype(F32))
    latent_hat_all, _ = standardize(wide_all)
    media_norm = (media_hat_all * media_gain + media_shift).astype(BF)
    latent_norm = (latent_hat_all * latent_gain + latent_shift).astype(BF)
    key_rows = jnp.concatenate([media_norm, latent_norm], axis=2).reshape(images * key_count, width)
    latent_rows = latent_norm.reshape(images * lat_rows, width)

    def columns(weight):
        return lax.dynamic_slice_in_dim(weight, at.h * cols, cols, 1)

    query = dot(latent_rows, columns(w_query), ((1,), (0,))).astype(BF).reshape(images, lat_rows, cols)
    keys = dot(key_rows, columns(w_key), ((1,), (0,))).astype(BF).reshape(images, key_count, cols)
    values = dot(key_rows, columns(w_value), ((1,), (0,))).astype(BF).reshape(images, key_count, cols)
    q_shape = jax.ShapeDtypeStruct(query.shape, BF)
    k_shape = jax.ShapeDtypeStruct(keys.shape, BF)
    (mixed_mine,) = per_image(attend_kernel, "attend", [q_shape], query, keys, values)
    (mixed_heads,) = gather_head("gather_mixed", 2, rows, heads, False, mixed_mine.reshape(images * lat_rows, cols))
    mixed = jnp.swapaxes(mixed_heads, 0, 1).reshape(images * lat_rows, width)

    residual = wide_all.reshape(images * lat_rows, width) + dot(mixed, w_out, ((1,), (0,)))
    ffn_hat, ffn_scale = standardize(residual)
    ffn_norm = (ffn_hat * ffn_gain + ffn_shift).astype(BF)
    image_ids = at.r * images + jnp.arange(images, dtype=jnp.int32)
    seq_table = jnp.arange(counts.shape[0], dtype=jnp.int32)
    limit = jnp.sum(jnp.where((image_ids // MAX_IMG)[:, None] == seq_table[None, :], counts[None, :], 0), axis=1)
    live = (image_ids % MAX_IMG) < limit
    d_out = jnp.where(live[:, None, None, None], cot_all, jnp.zeros((), BF)).reshape(images * lat_rows, width)

    def gather_rows(array):
        half = array.reshape(nc, array.shape[0] // nc, width)
        part = lax.dynamic_index_in_dim(half, at.c, 0, keepdims=False)
        line = [part]
        for d in range(1, nz):
            line.append(lax.ppermute(part, "rows", [(z * nx + x, (z + d) % nz * nx + x) for z in range(nz) for x in range(nx)]))
        plane = list(line)
        for d in range(1, nx):
            for block in line:
                plane.append(lax.ppermute(block, "rows", [(z * nx + x, z * nx + (x + d) % nx) for z in range(nz) for x in range(nx)]))
        mine_all = jnp.stack(plane)
        if nc == 1:
            return mine_all.reshape(-1, width)
        other = lax.ppermute(mine_all, "head", [(y * nc + c, y * nc + nc - 1 - c) for y in range(ny) for c in range(nc)])
        first = jnp.where(at.c == 0, mine_all, other)
        second = jnp.where(at.c == 0, other, mine_all)
        return jnp.concatenate([first, second], axis=0).reshape(-1, width)

    d_out_rows = gather_rows(d_out)
    ffn_rows = gather_rows(ffn_norm)
    up_mine = lax.dynamic_slice_in_dim(w_up, at.h * mine, mine, 1)
    down_mine = lax.dynamic_slice_in_dim(w_down, at.h * mine, mine, 0)
    hidden = dot(ffn_norm, up_mine, ((1,), (0,)))
    activated_wide, gelu_pull = jax.vjp(jax.nn.gelu, hidden)
    activated = activated_wide.astype(BF)
    out_part = dot(activated, down_mine, ((1,), (0,)))
    d_hidden = gelu_pull(dot(d_out, down_mine, ((1,), (1,))))[0].astype(BF)
    d_ffn_part = dot(d_hidden, up_mine, ((1,), (1,)))

    def by_core(array):
        return jnp.transpose(array.reshape(images, ny, nc, lat, width), (2, 1, 0, 3, 4))

    d_ffn_core, out_core = by_core(d_ffn_part), by_core(out_part)
    if nc > 1:
        d_ffn_other, out_other = exchange("sum_core", 3, rows, heads, ["core", "core"], d_ffn_core, out_core)
        d_ffn_half = lax.dynamic_index_in_dim(d_ffn_core, at.c, 0, keepdims=False) + d_ffn_other[0]
        out_half = lax.dynamic_index_in_dim(out_core, at.c, 0, keepdims=False) + out_other[0]
    else:
        d_ffn_half, out_half = d_ffn_core[0], out_core[0]
    if ny > 1:
        send = d_ffn_half.astype(BF)
        out_send = out_half.astype(BF)
        copies = jnp.broadcast_to(send[None], (ny,) + send.shape)
        d_ffn_far, out_far = exchange("sum_y", 4, rows, heads, ["y", "y"], copies, out_send)
        d_ffn_half = send.astype(F32) + jnp.sum(d_ffn_far.astype(F32), axis=0)
        out_own = lax.dynamic_index_in_dim(out_half, at.y, 0, keepdims=False) + jnp.sum(out_far.astype(F32), axis=0)
    else:
        out_own = out_half[0]
    if nc > 1:
        pair = jnp.broadcast_to(d_ffn_half[None], (nc,) + d_ffn_half.shape)
        (d_ffn_pair,) = exchange("share_core", 5, rows, heads, ["core"], pair)
        first = jnp.where(at.c == 0, d_ffn_half, d_ffn_pair[0])
        second = jnp.where(at.c == 0, d_ffn_pair[0], d_ffn_half)
        both = jnp.stack([first, second])
    else:
        both = d_ffn_half[None]
    d_ffn_norm = jnp.transpose(both, (2, 1, 0, 3, 4)).reshape(images * lat_rows, width)

    def own_rows(array):
        return lax.dynamic_index_in_dim(array.reshape(images, heads, lat, width), at.h, 1, keepdims=False)

    output = own_rows(residual) + jnp.swapaxes(out_own, 0, 0).reshape(images, lat, width)
    d_ffn_own = own_rows(d_ffn_norm)
    ffn_gain_part = jnp.sum(d_ffn_own * own_rows(ffn_hat), axis=(0, 1))
    ffn_shift_part = jnp.sum(d_ffn_own, axis=(0, 1))
    d_residual = d_out.astype(F32) + norm_back(d_ffn_norm * ffn_gain, ffn_hat, ffn_scale)
    d_attn = d_residual.astype(BF)
    out_rows = lax.dynamic_slice_in_dim(w_out, at.h * cols, cols, 0)
    d_mixed = dot(d_attn, out_rows, ((1,), (1,))).astype(BF).reshape(images, lat_rows, cols)
    d_query, d_keys, d_values = per_image(
        attend_back_kernel, "attend_back", [q_shape, k_shape, k_shape], query, keys, values, d_mixed
    )

    d_attn_cols = lax.dynamic_slice_in_dim(d_attn, at.h * cols, cols, 1)
    parts = [
        dot(latent_rows, d_query.reshape(-1, cols), ((0,), (0,))),
        dot(key_rows, d_keys.reshape(-1, cols), ((0,), (0,))),
        dot(key_rows, d_values.reshape(-1, cols), ((0,), (0,))),
        dot(mixed, d_attn_cols, ((0,), (0,))),
    ]
    block = width // rows
    parts = [jnp.swapaxes(p.astype(BF).reshape(nz, nx, block, cols), 0, 1) for p in parts]

    def to_heads(array, count):
        return jnp.swapaxes(array.reshape(images, heads, count, cols), 0, 1)

    turned = [to_heads(d_query, lat), to_heads(d_keys, patch + lat), to_heads(d_values, patch + lat)]
    moved = exchange("turn_and_sum_x", 6, rows, heads, ["head"] * 3 + ["x"] * 4, *turned, *parts)
    full = []
    for array, far in zip(turned, moved[:3]):
        own = lax.dynamic_index_in_dim(array, at.h, 0, keepdims=True)
        stacked = jnp.concatenate([own, far], axis=0)
        stacked = jnp.take(stacked, (at.h - jnp.arange(heads)) % heads, axis=0)
        full.append(jnp.transpose(stacked, (1, 2, 0, 3)).reshape(-1, width))
    d_query_own, d_keys_own, d_values_own = full
    sums = [
        (lax.dynamic_index_in_dim(p, at.x, 0, keepdims=False).astype(F32) + jnp.sum(far.astype(F32), axis=0)).astype(BF)
        for p, far in zip(parts, moved[3:])
    ]

    d_key_rows = (dot(d_keys_own, w_key, ((1,), (1,))) + dot(d_values_own, w_value, ((1,), (1,)))).reshape(
        images, patch + lat, width
    )
    d_media_norm = d_key_rows[:, :patch]
    d_latent_norm = d_key_rows[:, patch:] + dot(d_query_own, w_query, ((1,), (1,))).reshape(images, lat, width)
    media_hat, media_scale = standardize(media.astype(F32))
    latent_hat, latent_scale = standardize(latents.astype(F32))
    media_grad = norm_back(d_media_norm * media_gain, media_hat, media_scale)
    latents_grad = own_rows(d_residual) + norm_back(d_latent_norm * latent_gain, latent_hat, latent_scale)
    vectors = jnp.stack(
        [
            jnp.sum(d_media_norm * media_hat, axis=(0, 1)),
            jnp.sum(d_media_norm, axis=(0, 1)),
            jnp.sum(d_latent_norm * latent_hat, axis=(0, 1)),
            jnp.sum(d_latent_norm, axis=(0, 1)),
            ffn_gain_part,
            ffn_shift_part,
        ]
    )
    share = width // (rows * heads)
    tiles = jnp.transpose(vectors.reshape(6, rows, heads, share), (2, 1, 0, 3))
    tiles = jnp.pad(tiles, ((0, 0), (0, 0), (0, 2), (0, 128 - share)))
    moved = exchange("sum_z", 7, rows, heads, ["z"] * 4 + ["head"], *sums, tiles)
    grads = [
        lax.dynamic_index_in_dim(s, at.z, 0, keepdims=False).astype(F32) + jnp.sum(far.astype(F32), axis=0)
        for s, far in zip(sums, moved[:4])
    ]
    tiles = lax.dynamic_index_in_dim(tiles, at.h, 0, keepdims=False) + jnp.sum(moved[4], axis=0)
    tiles = tiles.reshape(nz, nx, 8, 128)
    (far,) = exchange("vectors_z", 8, rows, heads, ["z"], tiles)
    tiles = lax.dynamic_index_in_dim(tiles, at.z, 0, keepdims=False) + jnp.sum(far, axis=0)
    if nx > 1:
        (far,) = exchange("vectors_x", 9, rows, heads, ["x"], tiles)
        tiles = lax.dynamic_index_in_dim(tiles, at.x, 0, keepdims=False) + jnp.sum(far, axis=0)
    else:
        tiles = tiles[0]
    vector_sums = tiles[:6, :share]

    hidden_rows = dot(ffn_rows, up_mine, ((1,), (0,)))
    activated_rows, gelu_pull = jax.vjp(jax.nn.gelu, hidden_rows)
    d_hidden_rows = gelu_pull(dot(d_out_rows, down_mine, ((1,), (1,))))[0].astype(BF)
    ffn_cols = lax.dynamic_slice_in_dim(ffn_rows, at.r * block, block, 1)
    d_out_cols = lax.dynamic_slice_in_dim(d_out_rows, at.r * block, block, 1)
    up_grad = dot(ffn_cols, d_hidden_rows, ((0,), (0,)))
    down_grad = dot(activated_rows.astype(BF), d_out_cols, ((0,), (0,)))
    return (
        output, media_grad, latents_grad, vector_sums[0], vector_sums[1], vector_sums[2], vector_sums[3],
        grads[0], grads[1], grads[2], grads[3], vector_sums[4], vector_sums[5], up_grad, down_grad,
    )


def solution(mesh):
    row = P("rows", "head", None)
    whole = P()
    vector = P(("rows", "head"))
    grid = P("rows", "head")
    return jax.shard_map(
        body,
        mesh=mesh,
        in_specs=(row, row) + (whole,) * 13 + (row,),
        out_specs=(row, row, row, vector, vector, vector, vector, grid, grid, grid, grid, vector, vector, grid, P("head", "rows")),
        check_vma=False,
    )
```

```python
import functools
import math
import types

import jax
import jax.numpy as jnp
from jax import lax
from jax.experimental import pallas as pl
from jax.experimental.pallas import tpu as pltpu
from jax.sharding import PartitionSpec as P

HEAD_DIM = 96
MAX_IMG = 8
EPSILON = 1e-05
BF = jnp.bfloat16
F32 = jnp.float32
MESH = pl.DeviceIdType.MESH
ANY = pl.BlockSpec(memory_space=pl.ANY)


def factor_rows(count):
    nz = 4 if count % 4 == 0 else 1
    return nz, count // nz


def factor_head(count):
    nc = 2 if count % 2 == 0 else 1
    return count // nc, nc


def standardize(values):
    row_mean = jnp.mean(values, axis=-1, keepdims=True)
    centered = values - row_mean
    variance = jnp.mean(centered * centered, axis=-1, keepdims=True)
    inv_scale = lax.rsqrt(variance + EPSILON)
    return centered * inv_scale, inv_scale


def norm_back(d_scaled, normed, inv_scale):
    first_mean = jnp.mean(d_scaled, axis=-1, keepdims=True)
    second_mean = jnp.mean(d_scaled * normed, axis=-1, keepdims=True)
    return inv_scale * (d_scaled - first_mean - normed * second_mean)


def dot(a, b, dims):
    return lax.dot_general(a, b, (dims, ((), ())), preferred_element_type=F32)


class Place:
    def __init__(self, rows, heads):
        self.rows, self.heads = rows, heads
        self.nz, self.nx = factor_rows(rows)
        self.ny, self.nc = factor_head(heads)
        self.r = lax.axis_index("rows")
        self.h = lax.axis_index("head")
        self.z, self.x = self.r // self.nx, self.r % self.nx
        self.y, self.c = self.h // self.nc, self.h % self.nc

    def head_peers(self):
        return [(self.r, lax.rem(self.h + d, self.heads)) for d in range(1, self.heads)]

    def x_peer(self, d):
        return lax.rem(self.x + d, self.nx)

    def z_peer(self, d):
        return lax.rem(self.z + d, self.nz)

    def y_peer(self, d):
        return lax.rem(self.y + d, self.ny)


def greet(peers):
    barrier = pltpu.get_barrier_semaphore()
    for peer in peers:
        pl.semaphore_signal(barrier, inc=1, device_id=peer, device_id_type=MESH)
    pl.semaphore_wait(barrier, len(peers))


def remote(src, dst, sems, slot, peer):
    return pltpu.make_async_remote_copy(
        src_ref=src,
        dst_ref=dst,
        send_sem=sems[0].at[slot],
        recv_sem=sems[1].at[slot],
        device_id=peer,
        device_id_type=MESH,
    )


class Copies:
    def __init__(self, at, send, recv):
        self.at, self.send, self.recv, self.used = at, send, recv, 0
        self.unsent = []

    def put(self, src, dst, peer):
        copy = pltpu.make_async_remote_copy(
            src_ref=src,
            dst_ref=dst,
            send_sem=self.send.at[self.used],
            recv_sem=self.recv.at[self.used],
            device_id=peer,
            device_id_type=MESH,
        )
        self.used += 1
        copy.start()
        self.unsent.append(copy)
        return copy

    def sent(self, copy):
        copy.wait_send()
        self.unsent = [c for c in self.unsent if c is not copy]

    def finish(self):
        for copy in self.unsent:
            copy.wait_send()


def norm_rows(block):
    mean = jnp.mean(block, axis=-1, keepdims=True)
    centered = block - mean
    scale = lax.rsqrt(jnp.mean(centered * centered, axis=-1, keepdims=True) + EPSILON)
    return centered * scale, scale


def mm(a, b):
    return dot(a, b, ((1,), (0,)))


def mt(a, b):
    return dot(a, b, ((1,), (1,)))


def tm(a, b):
    return dot(a, b, ((0,), (0,)))


def gelu_pair(v):
    c = math.sqrt(2.0 / math.pi)
    square = v * v
    t = jnp.tanh(c * v * (1.0 + 0.044715 * square))
    half = 0.5 * (1.0 + t)
    slope = half + 0.5 * v * (1.0 - t * t) * (c * (1.0 + 3.0 * 0.044715 * square))
    return v * half, slope


def loop(count, step):
    def run(i, carry):
        step(i)
        return carry

    lax.fori_loop(0, count, run, 0)


def tile_of(extent, most):
    size = most
    while extent % size:
        size -= 128
    return size


def forward_kernel(s, *refs):
    refs = dict(zip(s.names, refs, strict=True))
    n = types.SimpleNamespace(**refs)
    at = Place(s.rows, s.heads)
    ny, nc, nz, nx = at.ny, at.nc, at.nz, at.nx
    G, pl_rows, ll, D, E, F = s.images, s.patch, s.lat, s.width, s.cols, s.mine
    M, L, LR = G * pl_rows, G * ll, s.heads * ll
    GL = G * LR
    copies = Copies(at, n.send, n.recv)
    partner = (at.r, at.y * nc + (nc - 1 - at.c))
    loads = []

    def load(src, dst):
        copy = pltpu.make_async_copy(src, dst, n.local.at[len(loads)])
        copy.start()
        loads.append(copy)
        return copy

    load_cot = load(n.cot, n.cot_v)
    load_media = load(n.media, n.raw_m.at[0])
    load_lat = load(n.lat, n.raw_l.at[0])

    def columns(weight):
        if weight.shape[1] == E:
            return weight
        return weight.at[:, pl.ds(pl.multiple_of(at.h * E, 128), E)]

    load_qkv = [load(columns(w), v) for w, v in ((n.wk, n.wk_v), (n.wv, n.wv_v), (n.wq, n.wq_v))]

    greet(at.head_peers() + [(at.z * nx + at.x_peer(d), at.h) for d in range(1, nx)] + [(at.z_peer(d) * nx + at.x, at.h) for d in range(1, nz)])
    load_cot.wait()
    masked = n.cot_v[...].astype(F32) * n.mask[...]
    n.dslot[at.y, at.c] = masked.astype(BF)

    def y_send(src, dst):
        return [copies.put(src, dst(d), (at.r, at.y_peer(d) * nc + at.c)) for d in range(1, ny)]

    def slot(ref):
        return lambda d: ref.at[(ny - d) % ny * nc]

    cot_far = y_send(n.dslot.at[at.y, at.c], lambda d: n.dslot.at[at.y, at.c])
    lat_far = y_send(n.lat, slot(n.raw_l))
    media_far = y_send(n.media, slot(n.raw_m))
    near = []
    if nc > 1:
        lat_near = copies.put(n.lat, n.raw_l.at[1], partner)
        media_near = copies.put(n.media, n.raw_m.at[1], partner)
        cot_near = copies.put(n.dslot.at[at.y, at.c], n.dslot.at[at.y, at.c], partner)
    here = at.r

    def z_send(src, dst):
        return [copies.put(src, dst, (at.z_peer(d) * nx + at.x, at.h)) for d in range(1, nz)]

    def x_send(src, dst):
        return [copies.put(src, dst, (at.z * nx + at.x_peer(d), at.h)) for d in range(1, nx)]

    def quarter(ref, r, d):
        return ref.at[r, pl.ds(pl.multiple_of((at.c * ny + at.y_peer(d)) * L, 16), L)]

    own = n.dslot.at[at.y, at.c]
    z_far = {0: z_send(own, quarter(n.dall, here, 0))}
    x_far = x_send(own, quarter(n.dall, here, 0))
    load_out = load(n.wout, n.wout_v)
    load_up = load(n.wup.at[:, pl.ds(pl.multiple_of(at.h * F, 128), F)], n.wup_v)
    load_down = load(n.wdown.at[pl.ds(pl.multiple_of(at.h * F, 16), F)], n.wdown_v)

    def x_forward(d):
        for dz, copy in enumerate(z_far[d], 1):
            copy.wait_recv()
            block = quarter(n.dall, at.z_peer(nz - dz) * nx + at.x, d)
            x_far.extend(x_send(block, block))

    stores, kept = [], [0]

    def store(src, dst):
        copy = pltpu.make_async_copy(src, dst, n.out_sem.at[kept[0]])
        kept[0] += 1
        copy.start()
        stores.append(copy)
        return copy

    busy = {}

    def patches(k, place):
        buf = place % 2
        if buf in busy:
            busy[buf].wait()
            stores[:] = [c for c in stores if c is not busy[buf]]

        def step(i):
            rows = pl.ds(pl.multiple_of(i * 32, 32), 32)
            hat, _ = norm_rows(n.raw_m[k, rows].astype(F32))
            n.norm[buf, rows] = (hat * n.vecs[0:1] + n.vecs[1:2]).astype(BF)

        loop(M // 32, step)
        n.keys[k] = mm(n.norm[buf], n.wk_v[...]).astype(BF)
        n.values[k] = mm(n.norm[buf], n.wv_v[...]).astype(BF)
        busy[buf] = store(n.norm.at[buf], n.key_norm_o.at[k, 0:M])

    load_media.wait()
    for copy in load_qkv:
        copy.wait()
    patches(0, 0)
    order = 1
    if nc > 1:
        media_near.wait_recv()
        patches(1, order)
        order += 1
    relays = []
    cot_relay, lat_relay, media_relay = [], [], []
    for d, copy in zip(range(1, ny), cot_far):
        copy.wait_recv()
        y = at.y_peer(ny - d)
        if nc > 1:
            cot_relay.append(copies.put(n.dslot.at[y, at.c], n.dslot.at[y, at.c], partner))
    for d, copy in zip(range(1, ny), lat_far):
        copy.wait_recv()
        k = (ny - d) * nc
        if nc > 1:
            lat_relay.append(copies.put(n.raw_l.at[k], n.raw_l.at[k + 1], partner))
    load_lat.wait()
    if nc > 1:
        lat_near.wait_recv()
    for copy in lat_relay:
        copy.wait_recv()
    for d in range(ny):
        for e in range(nc):
            head = at.y_peer(d) * nc + (at.c if e == 0 else nc - 1 - at.c)
            wide = n.raw_l[d * nc + e].astype(F32)
            for i in range(G):
                n.resid[pl.ds(pl.multiple_of(i * LR + head * ll, 8), ll)] = wide[i * ll : (i + 1) * ll]

    for k in range(s.heads):

        def latent_step(i):
            rows = pl.ds(pl.multiple_of(i * 32, 32), 32)
            hat, _ = norm_rows(n.raw_l[k, rows].astype(F32))
            n.lnorm[pl.ds(pl.multiple_of(k * L + i * 32, 32), 32)] = (hat * n.vecs[2:3] + n.vecs[3:4]).astype(BF)

        loop(L // 32, latent_step)
        store(n.lnorm.at[k * L : (k + 1) * L], n.key_norm_o.at[k, M : M + L])
    for weight, result in ((n.wq_v, n.query), (n.wk_v, n.lkeys), (n.wv_v, n.lvalues)):
        wide = mm(n.lnorm[...], weight[...])
        for d in range(ny):
            for e in range(nc):
                head = at.y_peer(d) * nc + (at.c if e == 0 else nc - 1 - at.c)
                for i in range(G):
                    base = (d * nc + e) * L + i * ll
                    n.turn[pl.ds(pl.multiple_of(i * LR + head * ll, 8), ll)] = wide[base : base + ll]
        result[...] = n.turn[...].astype(BF)
    for copy in [load_out, load_up, load_down]:
        copy.wait()
    if nc > 1:
        cot_near.wait_recv()
    for copy in cot_relay:
        copy.wait_recv()
    for y in range(ny):
        for c in range(nc):
            wide = n.dslot[y, c].astype(F32)
            for i in range(G):
                n.part[pl.ds(i * LR + (y * nc + c) * ll, ll)] = wide[i * ll : (i + 1) * ll]
    n.dout[...] = n.part[...].astype(BF)
    store(n.dout, n.dout_o)
    for d in range(1, ny):
        block = n.dslot.at[at.y_peer(d), at.c]
        z_far[d] = z_send(block, quarter(n.dall, here, d))
        x_far.extend(x_send(block, quarter(n.dall, here, d)))
    for d, copy in zip(range(1, ny), media_far):
        copy.wait_recv()
        k = (ny - d) * nc
        if nc > 1:
            media_relay.append(copies.put(n.raw_m.at[k], n.raw_m.at[k + 1], partner))
        patches(k, order)
        order += 1
    for d, copy in zip(range(1, ny), media_relay):
        copy.wait_recv()
        patches((ny - d) * nc + 1, order)
        order += 1
    x_forward(0)
    store(n.keys, n.keys_o)
    store(n.values, n.values_o)
    store(n.lkeys, n.lkeys_o)
    store(n.lvalues, n.lvalues_o)
    store(n.query, n.query_o)

    scale = 1.0 / math.sqrt(HEAD_DIM)

    def attend_image(i):
        q_rows = pl.ds(pl.multiple_of(i * LR, 16), LR)
        m_rows = pl.ds(pl.multiple_of(i * pl_rows, 16), pl_rows)
        q_all = n.query[q_rows]
        k_all = jnp.concatenate([n.keys[k, m_rows] for k in range(s.heads)] + [n.lkeys[q_rows]], axis=0)
        v_all = jnp.concatenate([n.values[k, m_rows] for k in range(s.heads)] + [n.lvalues[q_rows]], axis=0)
        mixed = []
        for j in range(E // HEAD_DIM):
            part = slice(j * HEAD_DIM, (j + 1) * HEAD_DIM)
            scores = mt(q_all[:, part], k_all[:, part]) * scale
            powers = jnp.exp(scores - jnp.max(scores, axis=-1, keepdims=True))
            probs = (powers * (1.0 / jnp.sum(powers, axis=-1, keepdims=True))).astype(BF)
            mixed.append(mm(probs, v_all[:, part]))
        n.mix[at.h, q_rows] = jnp.concatenate(mixed, axis=-1).astype(BF)

    loop(G, attend_image)
    mix_far = y_send(n.mix.at[at.h], lambda d: n.mix.at[at.h])
    mix_near = [copies.put(n.mix.at[at.h], n.mix.at[at.h], partner)] if nc > 1 else []
    wide_tile = tile_of(D, 512)

    def add_mixed(head):
        w_rows = pl.ds(pl.multiple_of(head * E, 16), E)

        def step(t):
            lanes = pl.ds(pl.multiple_of(t * wide_tile, 128), wide_tile)
            n.resid[:, lanes] += mm(n.mix[head], n.wout_v[w_rows, lanes])

        loop(D // wide_tile, step)

    add_mixed(at.h)
    for copy in mix_near:
        copy.wait_recv()
        add_mixed(at.y * nc + (nc - 1 - at.c))
    mix_relay = []
    for d, copy in zip(range(1, ny), mix_far):
        copy.wait_recv()
        y = at.y_peer(ny - d)
        block = n.mix.at[y * nc + at.c]
        if nc > 1:
            mix_relay.append((y, copies.put(block, block, partner)))
        add_mixed(y * nc + at.c)
    for y, copy in mix_relay:
        copy.wait_recv()
        add_mixed(y * nc + (nc - 1 - at.c))
    store(n.mix, n.mixed_o)

    def ffn_step(i):
        rows = pl.ds(pl.multiple_of(i * 32, 32), 32)
        hat, inv = norm_rows(n.resid[rows])
        n.hat[rows] = hat
        n.inv[rows] = jnp.broadcast_to(inv, (32, 128))
        n.ffn[rows] = (hat * n.vecs[4:5] + n.vecs[5:6]).astype(BF)

    loop(GL // 32, ffn_step)
    store(n.ffn, n.ffn_o)

    def own_rows(i):
        return pl.ds(pl.multiple_of(i * LR + at.h * ll, 8), ll)

    quarter_rows = jnp.concatenate([n.hat[own_rows(i)] for i in range(G)], axis=0)
    n.fq[...] = (quarter_rows * n.vecs[4:5] + n.vecs[5:6]).astype(BF)
    ffn_far = z_send(n.fq, quarter(n.fall, here, 0))
    store(n.fq, quarter(n.fall, here, 0))
    hid_tile = 256

    def hidden_step(t):
        lanes = pl.ds(pl.multiple_of(t * hid_tile, 128), hid_tile)
        value, slope = gelu_pair(mm(n.ffn[...], n.wup_v[:, lanes]))
        n.act[:, lanes] = value.astype(BF)
        n.dhid[:, lanes] = (mt(n.dout[...], n.wdown_v[lanes, :]) * slope).astype(BF)

    loop(F // hid_tile, hidden_step)
    store(n.act, n.act_o)
    store(n.dhid, n.dhid_o)

    def back_step(t):
        lanes = pl.ds(pl.multiple_of(t * wide_tile, 128), wide_tile)
        n.part[:, lanes] = mt(n.dhid[...], n.wup_v[lanes, :])

    loop(D // wide_tile, back_step)
    half = GL // nc
    mine_half = pl.ds(pl.multiple_of(at.c * half, 16), half)
    other_half = pl.ds(pl.multiple_of((nc - 1 - at.c) * half, 16), half)
    if nc > 1:
        swap = copies.put(n.part.at[other_half], n.c_recv, partner)

    def out_step(t):
        lanes = pl.ds(pl.multiple_of(t * wide_tile, 128), wide_tile)
        tile = mm(n.act[...], n.wdown_v[:, lanes])
        for i in range(G):
            for head in range(s.heads):
                base = i * LR + head * ll
                n.outp[head % nc, head // nc, i * ll : (i + 1) * ll, lanes] = tile[base : base + ll]

    loop(D // wide_tile, out_step)
    if nc > 1:
        out_swap = copies.put(n.outp.at[nc - 1 - at.c], n.oc_recv, partner)
        swap.wait_recv()
    chunk = 64

    def rows_of(base, i):
        return pl.ds(pl.multiple_of(base + i * chunk, 8), chunk)

    def half_step(i):
        rows = rows_of(at.c * half, i)
        total = n.part[rows]
        if nc > 1:
            total = total + n.c_recv[rows_of(0, i)]
        n.y_send[rows_of(0, i)] = total.astype(BF)

    loop(half // chunk, half_step)
    sum_far = [copies.put(n.y_send, n.y_recv.at[d - 1], (at.r, at.y_peer(d) * nc + at.c)) for d in range(1, ny)]
    if nc > 1:
        out_swap.wait_recv()
    for y in range(ny):
        total = n.outp[at.c, y]
        if nc > 1:
            total = total + n.oc_recv[y]
        n.outp[at.c, y] = total
        n.oy_send[y] = total.astype(BF)
    out_far = [
        copies.put(n.oy_send.at[at.y_peer(d)], n.oy_recv.at[d - 1], (at.r, at.y_peer(d) * nc + at.c)) for d in range(1, ny)
    ]
    for d in range(1, ny):
        x_forward(d)
    for copy in sum_far:
        copy.wait_recv()

    def total_step(i):
        rows = rows_of(0, i)
        total = n.y_send[rows].astype(F32)
        for d in range(1, ny):
            total = total + n.y_recv[d - 1, rows].astype(F32)
        n.share[rows] = total

    loop(half // chunk, total_step)
    if nc > 1:
        share = copies.put(n.share, n.s_recv, partner)

    def residual_back(ref, base):
        def step(i):
            rows = pl.ds(pl.multiple_of(base + i * 32, 8), 32)
            grad = ref[pl.ds(pl.multiple_of(i * 32, 8), 32)]
            hat, inv = n.hat[rows], n.inv[rows, 0:1]
            n.part[rows] = grad
            scaled = grad * n.vecs[4:5]
            first = jnp.mean(scaled, axis=-1, keepdims=True)
            second = jnp.mean(scaled * hat, axis=-1, keepdims=True)
            d_res = n.dout[rows].astype(F32) + inv * (scaled - first - hat * second)
            n.resid[rows] = d_res
            n.dattn[rows] = d_res.astype(BF)

        loop(half // 32, step)

    if nc > 1:
        copies.sent(swap)
    for copy in out_far:
        copy.wait_recv()
    total = n.outp[at.c, at.y]
    for d in range(1, ny):
        total = total + n.oy_recv[d - 1].astype(F32)
    n.own[0] = total + jnp.concatenate([n.resid[own_rows(i)] for i in range(G)], axis=0)
    store(n.own.at[0], n.out_o)
    residual_back(n.share, at.c * half)
    if nc > 1:
        share.wait_recv()
        residual_back(n.s_recv, (nc - 1 - at.c) * half)
    store(n.dattn, n.dattn_o)
    n.own[1] = jnp.concatenate([n.resid[own_rows(i)] for i in range(G)], axis=0)
    store(n.own.at[1], n.dres_o)
    grad = jnp.concatenate([n.part[own_rows(i)] for i in range(G)], axis=0)
    n.fvec[...] = jnp.concatenate(
        [
            jnp.sum(grad * jnp.concatenate([n.hat[own_rows(i)] for i in range(G)], axis=0), axis=0, keepdims=True),
            jnp.sum(grad, axis=0, keepdims=True),
            jnp.zeros((6, D), F32),
        ],
        axis=0,
    )
    store(n.fvec, n.fvec_o)
    for copy in x_far:
        copy.wait_recv()
    if nc > 1:
        spread = []
        for r in range(1, s.rows):
            block = n.dall.at[lax.rem(here + r, s.rows), pl.ds(pl.multiple_of(at.c * ny * L, 16), ny * L)]
            spread.append(copies.put(block, block, partner))
        for copy in spread:
            copy.wait_recv()
    for copy in ffn_far:
        copy.wait_recv()
    copies.finish()
    for copy in stores:
        copy.wait()


def forward(s, media, lat, cot, mask, vecs, wq, wk, wv, wout, wup, wdown):
    ny, nc = factor_head(s.heads)
    G, L, D, E, F = s.images, s.images * s.lat, s.width, s.cols, s.mine
    M, GL, H = s.images * s.patch, s.images * s.lat * s.heads, s.heads
    half = GL // nc
    outs = dict(
        out_o=((L, D), F32), dres_o=((L, D), F32), fvec_o=((8, D), F32), key_norm_o=((H, M + L, D), BF), keys_o=((H, M, E), BF), values_o=((H, M, E), BF), lkeys_o=((GL, E), BF),
        lvalues_o=((GL, E), BF), query_o=((GL, E), BF), mixed_o=((H, GL, E), BF), dattn_o=((GL, D), BF),
        ffn_o=((GL, D), BF), dout_o=((GL, D), BF), act_o=((GL, F), BF), dhid_o=((GL, F), BF),
        dall=((s.rows, GL, D), BF), fall=((s.rows, GL, D), BF),
    )
    scratch = dict(
        cot_v=((L, D), BF), raw_m=((H, M, D), BF), raw_l=((H, L, D), BF), dslot=((ny, nc, L, D), BF),
        norm=((2, M, D), BF), lnorm=((GL, D), BF), turn=((GL, E), F32), keys=((H, M, E), BF), values=((H, M, E), BF), lkeys=((GL, E), BF),
        lvalues=((GL, E), BF), query=((GL, E), BF), mix=((H, GL, E), BF), resid=((GL, D), F32), hat=((GL, D), F32),
        inv=((GL, 128), F32), ffn=((GL, D), BF), dout=((GL, D), BF), act=((GL, F), BF), dhid=((GL, F), BF),
        part=((GL, D), F32), outp=((nc, ny, L, D), F32), c_recv=((half, D), F32), oc_recv=((ny, L, D), F32),
        y_send=((half, D), BF), y_recv=((max(ny - 1, 1), half, D), BF), oy_send=((ny, L, D), BF),
        oy_recv=((max(ny - 1, 1), L, D), BF), share=((half, D), F32), s_recv=((half, D), F32), fq=((L, D), BF),
        own=((2, L, D), F32), dattn=((GL, D), BF), fvec=((8, D), F32),
        wq_v=((D, E), BF), wk_v=((D, E), BF), wv_v=((D, E), BF), wout_v=((D, D), BF), wup_v=((D, F), BF), wdown_v=((F, D), BF),
    )
    ins = dict(media=media, lat=lat, cot=cot, mask=mask, vecs=vecs, wq=wq, wk=wk, wv=wv, wout=wout, wup=wup, wdown=wdown)
    vmem = pl.BlockSpec(memory_space=pltpu.VMEM)
    s.names = list(ins) + list(outs) + list(scratch) + ["send", "recv", "local", "out_sem"]
    result = pl.pallas_call(
        functools.partial(forward_kernel, s),
        name="forward",
        out_shape=[jax.ShapeDtypeStruct(*o) for o in outs.values()],
        in_specs=[vmem if k in ("mask", "vecs") else ANY for k in ins],
        out_specs=[ANY] * len(outs),
        scratch_shapes=[pltpu.VMEM(*v) for v in scratch.values()]
        + [pltpu.SemaphoreType.DMA((200,)), pltpu.SemaphoreType.DMA((200,)), pltpu.SemaphoreType.DMA((16,)), pltpu.SemaphoreType.DMA((40,))],
        compiler_params=pltpu.CompilerParams(collective_id=1, has_side_effects=True, vmem_limit_bytes=60 << 20),
        cost_estimate=pl.CostEstimate(flops=8 * 10**9, bytes_accessed=4 * 10**7, transcendentals=10**6),
    )(*ins.values())
    return dict(zip(outs, result, strict=True))


def window_of(position, block, width):
    base = jnp.minimum(position * block // 128 * 128, width - 256)
    return pl.multiple_of(base, 128), position * block - base


def backward_kernel(s, *refs):
    n = types.SimpleNamespace(**dict(zip(s.names, refs, strict=True)))
    at = Place(s.rows, s.heads)
    ny, nc, nz, nx, H = at.ny, at.nc, at.nz, at.nx, s.heads
    G, pl_rows, ll, D, E, F = s.images, s.patch, s.lat, s.width, s.cols, s.mine
    M, L, LR = G * pl_rows, G * ll, H * ll
    GL, ML, B = G * LR, M + L, s.width // s.rows
    here = at.r
    copies = Copies(at, n.send, n.recv)
    other = nc - 1 - at.c
    partner = (at.r, at.y * nc + other)
    count = [0]

    def load(src, dst):
        copy = pltpu.make_async_copy(src, dst, n.local.at[count[0]])
        count[0] += 1
        copy.start()
        return copy

    def head_of(k):
        d, e = divmod(k, nc)
        return at.y_peer(d) * nc + (at.c if e == 0 else other)

    def quarter(r, y):
        return r, pl.ds(pl.multiple_of((at.c * ny + y) * L, 16), L)

    def group(dz, dx):
        return lax.rem(at.z + dz, nz) * nx + lax.rem(at.x + dx, nx)

    aligned = E % 128 == 0
    first_loads = [load(n.dattn, n.dattn_v), load(n.mixed, n.mix_v)]
    head_lanes = pl.ds(pl.multiple_of(at.h * E, 128), E) if aligned else None
    first_loads.append(load(n.wout.at[pl.ds(pl.multiple_of(at.h * E, 16), E)], n.wout_v))
    if aligned:
        first_loads.append(load(n.dattn.at[:, head_lanes], n.dcols_v))
    else:
        first_loads.append(load(n.dattn_cols, n.dcols_v))
    attend_loads = [load(getattr(n, k), getattr(n, k + "_v")) for k in ("keys", "values", "lkeys", "lvalues", "query")]
    norm_load = load(n.key_norm, n.norm_v)
    own_quarters = [load(n.fall.at[quarter(group(dz, 0), at.y)], n.fall_b.at[quarter(group(dz, 0), at.y)]) for dz in range(1, nz)]
    ffn_loads = [load(getattr(n, k), getattr(n, k + "_v")) for k in ("ffn", "dout", "act", "dhid")]
    ffn_loads.append(load(n.wup.at[:, pl.ds(pl.multiple_of(at.h * F, 128), F)], n.wup_v))
    ffn_loads.append(load(n.wdown.at[pl.ds(pl.multiple_of(at.h * F, 16), F)], n.wdown_v))
    key_load = load(n.wk, n.w_v.at[0])
    value_load = load(n.wv, n.w_v.at[1])
    media_load = load(n.media, n.media_v)
    lat_load = load(n.lat, n.lat_v)
    dres_load = load(n.dres, n.dres_v)

    greet(at.head_peers() + [(at.z * nx + at.x_peer(d), at.h) for d in range(1, nx)] + [(at.z_peer(d) * nx + at.x, at.h) for d in range(1, nz)])

    def y_send(src, dst):
        return [copies.put(src, dst, (at.r, at.y_peer(d) * nc + at.c)) for d in range(1, ny)]

    def x_send(src, dst):
        return [copies.put(src, dst, (at.z * nx + at.x_peer(d), at.h)) for d in range(1, nx)]

    x_quarters = []
    for dz in range(nz):
        block = quarter(group(dz, 0), at.y)
        x_quarters.append(x_send(n.fall.at[block], n.fall_b.at[block]))
    y_quarters = {}
    for dz in range(1, nz):
        block = quarter(group(dz, 0), at.y)
        y_quarters[dz, 0] = y_send(n.fall.at[block], n.fall_b.at[block])

    def spread(dz, dx):
        for copy in y_quarters[dz, dx]:
            copy.wait_recv()
        if nc == 1:
            return None
        block = group(dz, dx), pl.ds(pl.multiple_of(at.c * ny * L, 16), ny * L)
        return copies.put(n.fall_b.at[block], n.fall_b.at[block], partner)

    wide_tile = tile_of(D, 512)
    for copy in first_loads:
        copy.wait()
    n.dmixed[...] = mt(n.dattn_v[...], n.wout_v[...]).astype(BF)

    def put_part(w, z, tile):
        for x in range(nx):
            n.parts[w, x, z] = tile[x * B : (x + 1) * B].astype(BF)

    tiles_per_head = E // (nx * B) if E % (nx * B) == 0 else 0
    if tiles_per_head:
        for head in range(H):
            put_part(3, head, tm(n.mix_v[head], n.dcols_v[...]))
    else:
        whole = jnp.concatenate([n.mix_v[head] for head in range(H)], axis=-1)
        for z in range(nz):
            put_part(3, z, tm(whole[:, z * nx * B : (z + 1) * nx * B], n.dcols_v[...]))
    x_parts, z_parts = {}, {}

    def rs_start(w):
        x_parts[w] = [
            copies.put(n.parts.at[w, at.x_peer(d)], n.x_recv.at[w, d - 1], (at.z * nx + at.x_peer(d), at.h)) for d in range(1, nx)
        ]

    def rs_middle(w):
        for copy in x_parts[w]:
            copy.wait_recv()

        def step(z):
            total = n.parts[w, at.x, z].astype(F32)
            for d in range(1, nx):
                total = total + n.x_recv[w, d - 1, z].astype(F32)
            n.sums[w, z] = total.astype(BF)

        loop(nz, step)
        z_parts[w] = [
            copies.put(n.sums.at[w, at.z_peer(d)], n.z_recv.at[w, d - 1], (at.z_peer(d) * nx + at.x, at.h)) for d in range(1, nz)
        ]

    def rs_end(w):
        for copy in z_parts[w]:
            copy.wait_recv()
        total = n.sums[w, at.z].astype(F32)
        for d in range(1, nz):
            total = total + n.z_recv[w, d - 1].astype(F32)
        n.grad_v[w] = total

    rs_start(3)
    for copy in attend_loads:
        copy.wait()
    scale = 1.0 / math.sqrt(HEAD_DIM)

    def back_image(i):
        q_rows = pl.ds(pl.multiple_of(i * LR, 16), LR)
        m_rows = pl.ds(pl.multiple_of(i * pl_rows, 16), pl_rows)
        q_all, d_all = n.query_v[q_rows], n.dmixed[q_rows]
        k_all = jnp.concatenate([n.keys_v[k, m_rows] for k in range(H)] + [n.lkeys_v[q_rows]], axis=0)
        v_all = jnp.concatenate([n.values_v[k, m_rows] for k in range(H)] + [n.lvalues_v[q_rows]], axis=0)
        dq, dk, dv = [], [], []
        for j in range(E // HEAD_DIM):
            part = slice(j * HEAD_DIM, (j + 1) * HEAD_DIM)
            q, k, v, d = q_all[:, part], k_all[:, part], v_all[:, part], d_all[:, part]
            scores = mt(q, k) * scale
            powers = jnp.exp(scores - jnp.max(scores, axis=-1, keepdims=True))
            probs = powers * (1.0 / jnp.sum(powers, axis=-1, keepdims=True))
            d_probs = mt(d, v)
            inner = jnp.sum(probs * d_probs, axis=-1, keepdims=True)
            d_scores = (probs * (d_probs - inner)).astype(BF)
            dq.append(mm(d_scores, k) * scale)
            dk.append(tm(d_scores, q) * scale)
            dv.append(tm(probs.astype(BF), d))
        dq, dk, dv = [jnp.concatenate(p, axis=-1) for p in (dq, dk, dv)]
        for j, grad in enumerate((dk, dv)):
            for k in range(H):
                n.dkv[j, k, m_rows] = grad[k * pl_rows : (k + 1) * pl_rows].astype(BF)
        for j, grad in enumerate((dk[H * pl_rows :], dv[H * pl_rows :], dq)):
            for head in range(H):
                n.turn[j, head, pl.ds(pl.multiple_of(i * ll, 8), ll)] = grad[head * ll : (head + 1) * ll]

    loop(G, back_image)
    for k in range(H):
        head = head_of(k)
        n.dkv[0, k, M:ML] = n.turn[0, head].astype(BF)
        n.dkv[1, k, M:ML] = n.turn[1, head].astype(BF)
        n.dqs[k] = n.turn[2, head].astype(BF)
    turned = {}
    for d in range(ny):
        for e in range(nc):
            k = d * nc + e
            if k == 0:
                continue
            peer = (at.r, head_of(k))
            to = (ny - d) % ny * nc + e
            turned[to] = [copies.put(n.dkv.at[j, k], n.dkv_recv.at[j, to], peer) for j in range(2)]
            turned[to].append(copies.put(n.dqs.at[k], n.dqs_recv.at[to], peer))
    for copy in own_quarters:
        copy.wait()
    near_blocks = [spread(dz, 0) for dz in range(1, nz)]
    norm_load.wait()
    for w in (1, 2, 0):

        def tile_step(z):
            lanes = pl.ds(pl.multiple_of(z * nx * B, 128), nx * B)
            if w == 0:
                total = sum(tm(n.norm_v[k, M:ML, lanes], n.dqs[k]) for k in range(H))
            else:
                total = sum(tm(n.norm_v[k, :, lanes], n.dkv[w - 1, k]) for k in range(H))
            put_part(w, z, total)

        loop(nz, tile_step)
        rs_start(w)
    for dx in range(1, nx):
        for dz in range(nz):
            x_quarters[dz][dx - 1].wait_recv()
            block = quarter(group(dz, nx - dx), at.y)
            y_quarters[dz, nx - dx] = y_send(n.fall_b.at[block], n.fall_b.at[block])
    rs_middle(3)
    for copy in ffn_loads:
        copy.wait()
    base, offset = window_of(here, B, D)
    window = pl.ds(base, 256)
    hid_tile = 256

    def own_step(t):
        lanes = pl.ds(pl.multiple_of(t * hid_tile, 128), hid_tile)
        n.up_acc[:, lanes] = tm(n.ffn_v[:, window], n.dhid_v[:, lanes])
        n.down_acc[:, lanes] = tm(n.dout_v[:, window], n.act_v[:, lanes])

    loop(F // hid_tile, own_step)

    def other_group(dz, dx, arrival):
        for copy in arrival:
            if copy is not None:
                copy.wait_recv()
        r = group(dz, dx)
        loads = [load(n.fall_b.at[r], n.ffn_v), load(n.dall.at[r], n.dout_v)]
        for copy in loads:
            copy.wait()

        def step(t):
            lanes = pl.ds(pl.multiple_of(t * hid_tile, 128), hid_tile)
            value, slope = gelu_pair(mm(n.ffn_v[...], n.wup_v[:, lanes]))
            d_act = mt(n.dout_v[...], n.wdown_v[lanes, :])
            n.up_acc[:, lanes] += tm(n.ffn_v[:, window], (d_act * slope).astype(BF))
            n.down_acc[:, lanes] += tm(n.dout_v[:, window], value.astype(BF))

        loop(F // hid_tile, step)

    for dz in range(1, nz):
        other_group(dz, 0, [near_blocks[dz - 1]])
        if dz == 1:
            rs_middle(1)
    key_load.wait()
    value_load.wait()
    n.dkv_recv[0, 0] = n.dkv[0, 0]
    n.dkv_recv[1, 0] = n.dkv[1, 0]
    n.dqs_recv[0] = n.dqs[0]
    n.drow[...] = jnp.zeros((ML, D), F32)

    def back_rows(slot, rows_from, k, buf):
        def step(t):
            lanes = pl.ds(pl.multiple_of(t * wide_tile, 128), wide_tile)
            grad = n.dqs_recv[k] if slot == 2 else n.dkv_recv[slot, k]
            if aligned:
                weight = n.w_v[buf, lanes, pl.ds(pl.multiple_of(head_of(k) * E, 128), E)]
                n.drow[rows_from:ML, lanes] += mt(grad, weight)
            else:
                weight = n.w_v[buf, pl.ds(pl.multiple_of(head_of(k) * E, 16), E), lanes]
                n.drow[rows_from:ML, lanes] += mm(grad, weight)

        loop(D // wide_tile, step)

    slots = sorted(range(H), key=lambda k: (k >= nc, k))
    for k in slots:
        if k:
            turned[k][0].wait_recv()
        back_rows(0, 0, k, 0)
    query_load = load(n.wq, n.w_v.at[0])
    for k in slots:
        if k:
            turned[k][1].wait_recv()
        back_rows(1, 0, k, 1)
    query_load.wait()
    for k in slots:
        if k:
            turned[k][2].wait_recv()
        back_rows(2, M, k, 0)
    for copy in (media_load, lat_load, dres_load):
        copy.wait()
    n.vec[...] = jnp.zeros((4, 8, D), F32)

    def norm_back_rows(raw, rows, grad_rows, which, extra, out):
        hat, inv = norm_rows(raw[rows].astype(F32))
        grad = n.drow[grad_rows]
        n.vec[which] += jnp.sum((grad * hat).reshape(-1, 8, D), axis=0)
        n.vec[which + 1] += jnp.sum(grad.reshape(-1, 8, D), axis=0)
        scaled = grad * n.vecs[which : which + 1]
        first = jnp.mean(scaled, axis=-1, keepdims=True)
        second = jnp.mean(scaled * hat, axis=-1, keepdims=True)
        result = inv * (scaled - first - hat * second)
        out[grad_rows] = result if extra is None else result + extra[rows]

    def media_step(i):
        rows = pl.ds(pl.multiple_of(i * 32, 32), 32)
        norm_back_rows(n.media_v, rows, rows, 0, None, n.drow)

    loop(M // 32, media_step)

    def lat_step(i):
        rows = pl.ds(pl.multiple_of(i * 32, 32), 32)
        norm_back_rows(n.lat_v, rows, pl.ds(pl.multiple_of(M + i * 32, 32), 32), 2, n.dres_v, n.drow)

    loop(L // 32, lat_step)
    outs = [load(n.drow.at[0:M], n.media_o), load(n.drow.at[M:ML], n.lat_o)]
    n.vec_own[...] = jnp.concatenate(
        [jnp.sum(n.vec[i], axis=0, keepdims=True) for i in range(4)] + [n.fvec[0:2], jnp.zeros((2, D), F32)], axis=0
    )
    vec_head = [copies.put(n.vec_own, n.vec_head.at[k - 1], (at.r, lax.rem(at.h + k, H))) for k in range(1, H)]
    rs_middle(2)
    late_blocks = {}
    for dx in range(1, nx):
        for dz in range(nz):
            late_blocks[dz, dx] = spread(dz, dx)
    span = D // nz
    for i, (dz, dx) in enumerate(late_blocks):
        other_group(dz, dx, [late_blocks[dz, dx]])
        if i == 0:
            rs_middle(0)
            for copy in vec_head:
                copy.wait_recv()
            total = n.vec_own[...]
            for k in range(1, H):
                total = total + n.vec_head[k - 1]
            for z in range(nz):
                n.vec_sum[z] = total[:, z * span : (z + 1) * span]
            vec_z = [
                copies.put(n.vec_sum.at[at.z_peer(d)], n.vec_z.at[d - 1], (at.z_peer(d) * nx + at.x, at.h)) for d in range(1, nz)
            ]
        if i == 1:
            for copy in vec_z:
                copy.wait_recv()
            total = n.vec_sum[at.z]
            for d in range(1, nz):
                total = total + n.vec_z[d - 1]
            n.vec_part[...] = total
            vec_x = [
                copies.put(n.vec_part, n.vec_x.at[d - 1], (at.z * nx + at.x_peer(d), at.h)) for d in range(1, nx)
            ]
    outs += [load(n.up_acc, n.up_o), load(n.down_acc, n.down_o)]
    for w in (3, 1, 2, 0):
        rs_end(w)
        outs.append(load(n.grad_v.at[w], n.grads_o.at[w]))
    for copy in vec_x:
        copy.wait_recv()
    total = n.vec_part[...]
    for d in range(1, nx):
        total = total + n.vec_x[d - 1]
    n.vec_done[...] = total
    outs.append(load(n.vec_done, n.vec_o))
    copies.finish()
    for copy in outs:
        copy.wait()


def backward(s, a, media, lat, vecs, wq, wk, wv, wout, wup, wdown, dattn_cols):
    ny, nc = factor_head(s.heads)
    nz, nx = factor_rows(s.rows)
    G, L, D, E, F, H = s.images, s.images * s.lat, s.width, s.cols, s.mine, s.heads
    M, GL = s.images * s.patch, s.images * s.lat * s.heads
    ML, B = M + L, s.width // s.rows
    outs = dict(
        media_o=((M, D), F32), lat_o=((L, D), F32), grads_o=((4, B, E), F32), up_o=((256, F), F32), down_o=((256, F), F32),
        vec_o=((8, D // nz), F32), fall_b=((s.rows, GL, D), BF),
    )
    scratch = dict(
        dattn_v=((GL, D), BF), mix_v=((H, GL, E), BF), wout_v=((E, D), BF), dcols_v=((GL, E), BF), dmixed=((GL, E), BF),
        keys_v=((H, M, E), BF), values_v=((H, M, E), BF), lkeys_v=((GL, E), BF), lvalues_v=((GL, E), BF), query_v=((GL, E), BF),
        norm_v=((H, ML, D), BF), ffn_v=((GL, D), BF), dout_v=((GL, D), BF), act_v=((GL, F), BF), dhid_v=((GL, F), BF),
        wup_v=((D, F), BF), wdown_v=((F, D), BF), w_v=((2, D, D), BF), media_v=((M, D), BF), lat_v=((L, D), BF), dres_v=((L, D), F32),
        dkv=((2, H, ML, E), BF), dqs=((H, L, E), BF), turn=((3, H, L, E), F32), dkv_recv=((2, H, ML, E), BF), dqs_recv=((H, L, E), BF),
        parts=((4, nx, nz, B, E), BF), x_recv=((4, max(nx - 1, 1), nz, B, E), BF), sums=((4, nz, B, E), BF),
        z_recv=((4, max(nz - 1, 1), B, E), BF), grad_v=((4, B, E), F32), up_acc=((256, F), F32), down_acc=((256, F), F32),
        drow=((ML, D), F32), vec=((4, 8, D), F32), vec_own=((8, D), F32), vec_head=((max(H - 1, 1), 8, D), F32),
        vec_sum=((nz, 8, D // nz), F32), vec_z=((max(nz - 1, 1), 8, D // nz), F32), vec_part=((8, D // nz), F32),
        vec_x=((max(nx - 1, 1), 8, D // nz), F32), vec_done=((8, D // nz), F32),
    )
    ins = dict(
        media=media, lat=lat, vecs=vecs, fvec=a["fvec_o"], dres=a["dres_o"], key_norm=a["key_norm_o"], keys=a["keys_o"],
        values=a["values_o"], lkeys=a["lkeys_o"], lvalues=a["lvalues_o"], query=a["query_o"], mixed=a["mixed_o"], dattn=a["dattn_o"],
        ffn=a["ffn_o"], dout=a["dout_o"], act=a["act_o"], dhid=a["dhid_o"], dall=a["dall"], fall=a["fall"], wq=wq, wk=wk, wv=wv,
        wout=wout, wup=wup, wdown=wdown,
    )
    if dattn_cols is not None:
        ins["dattn_cols"] = dattn_cols
    vmem = pl.BlockSpec(memory_space=pltpu.VMEM)
    s.names = list(ins) + list(outs) + list(scratch) + ["send", "recv", "local"]
    result = pl.pallas_call(
        functools.partial(backward_kernel, s),
        name="backward",
        out_shape=[jax.ShapeDtypeStruct(*o) for o in outs.values()],
        in_specs=[vmem if k in ("vecs", "fvec") else ANY for k in ins],
        out_specs=[ANY] * len(outs),
        scratch_shapes=[pltpu.VMEM(*v) for v in scratch.values()]
        + [pltpu.SemaphoreType.DMA((300,)), pltpu.SemaphoreType.DMA((300,)), pltpu.SemaphoreType.DMA((100,))],
        compiler_params=pltpu.CompilerParams(collective_id=2, has_side_effects=True, vmem_limit_bytes=62 << 20),
        cost_estimate=pl.CostEstimate(flops=30 * 10**9, bytes_accessed=8 * 10**7, transcendentals=10**6),
    )(*ins.values())
    return dict(zip(outs, result, strict=True))


def body(
    media, latents, counts, media_gain, media_shift, latent_gain, latent_shift, w_query, w_key, w_value, w_out,
    ffn_gain, ffn_shift, w_up, w_down, cotangent,
):
    rows, heads = lax.axis_size("rows"), lax.axis_size("head")
    at = Place(rows, heads)
    images, patch, width = media.shape
    lat = latents.shape[1]
    cols = width // heads
    s = types.SimpleNamespace(
        rows=rows, heads=heads, images=images, patch=patch, lat=lat, width=width, cols=cols, mine=w_up.shape[1] // heads
    )
    ids = at.r * images + jnp.arange(images, dtype=jnp.int32)
    table = jnp.arange(counts.shape[0], dtype=jnp.int32)
    limit = jnp.sum(jnp.where((ids // MAX_IMG)[:, None] == table[None, :], counts[None, :], 0), axis=1)
    live = ((ids % MAX_IMG) < limit).astype(F32)
    mask = jnp.repeat(live, lat)[:, None]
    vecs = jnp.stack([media_gain, media_shift, latent_gain, latent_shift, ffn_gain, ffn_shift, ffn_gain, ffn_shift])
    aligned = cols % 128 == 0

    def columns(array):
        return array if aligned else lax.dynamic_slice_in_dim(array, at.h * cols, cols, 1)

    flat_media, flat_lat, flat_cot = media.reshape(-1, width), latents.reshape(-1, width), cotangent.reshape(-1, width)
    a = forward(
        s, flat_media, flat_lat, flat_cot, mask, vecs, columns(w_query), columns(w_key), columns(w_value), w_out, w_up, w_down
    )
    turned = [w if aligned else w.T for w in (w_query, w_key, w_value)]
    b = backward(s, a, flat_media, flat_lat, vecs, *turned, w_out, w_up, w_down, None if aligned else columns(a["dattn_o"]))
    block = width // rows
    _, offset = window_of(at.r, block, width)
    up_grad = lax.dynamic_slice_in_dim(b["up_o"], offset, block, 0)
    down_grad = lax.dynamic_slice_in_dim(b["down_o"], offset, block, 0).T
    share = width // (rows * heads)
    vector = lax.dynamic_slice_in_dim(b["vec_o"], (at.x * heads + at.h) * share, share, 1)
    grads = b["grads_o"]
    return (
        a["out_o"].reshape(latents.shape), b["media_o"].reshape(media.shape), b["lat_o"].reshape(latents.shape),
        vector[0], vector[1], vector[2], vector[3], grads[0], grads[1], grads[2], grads[3], vector[4], vector[5], up_grad, down_grad,
    )


def solution(mesh):
    row = P("rows", "head", None)
    whole = P()
    vector = P(("rows", "head"))
    grid = P("rows", "head")
    return jax.shard_map(
        body,
        mesh=mesh,
        in_specs=(row, row) + (whole,) * 13 + (row,),
        out_specs=(row, row, row, vector, vector, vector, vector, grid, grid, grid, grid, vector, vector, grid, P("head", "rows")),
        check_vma=False,
    )
```

```python
import functools
import math
import types

import jax
import jax.numpy as jnp
from jax import lax
from jax.experimental import pallas as pl
from jax.experimental.pallas import tpu as pltpu
from jax.sharding import PartitionSpec as P

HEAD_DIM = 96
MAX_IMG = 8
EPSILON = 1e-05
BF = jnp.bfloat16
F32 = jnp.float32
MESH = pl.DeviceIdType.MESH
ANY = pl.BlockSpec(memory_space=pl.ANY)
VMEM = pl.BlockSpec(memory_space=pltpu.VMEM)
SMEM = pl.BlockSpec(memory_space=pltpu.SMEM)


def factor_rows(count):
    nz = 4 if count % 4 == 0 else 1
    return nz, count // nz


def factor_head(count):
    nc = 2 if count % 2 == 0 else 1
    return count // nc, nc


def mm(a, b):
    return lax.dot_general(a, b, (((1,), (0,)), ((), ())), preferred_element_type=F32)


def mt(a, b):
    return lax.dot_general(a, b, (((1,), (1,)), ((), ())), preferred_element_type=F32)


def tm(a, b):
    return lax.dot_general(a, b, (((0,), (0,)), ((), ())), preferred_element_type=F32)


class Place:
    def __init__(self, rows, heads):
        self.rows, self.heads = rows, heads
        self.nz, self.nx = factor_rows(rows)
        self.ny, self.nc = factor_head(heads)
        self.r = lax.axis_index("rows")
        self.h = lax.axis_index("head")
        self.z, self.x = self.r // self.nx, self.r % self.nx
        self.y, self.c = self.h // self.nc, self.h % self.nc

    def y_peer(self, d):
        return lax.rem(self.y + d, self.ny)

    def group(self, dz, dx):
        return lax.rem(self.z + dz, self.nz) * self.nx + lax.rem(self.x + dx, self.nx)

    def head_of(self, slot):
        d, e = divmod(slot, self.nc)
        return self.y_peer(d) * self.nc + (self.c if e == 0 else self.nc - 1 - self.c)

    def on_y(self, d):
        return self.r, self.y_peer(d) * self.nc + self.c

    def on_x(self, d):
        return self.group(0, d), self.h

    def on_z(self, d):
        return self.group(d, 0), self.h

    def partner(self):
        return self.r, self.y * self.nc + (self.nc - 1 - self.c)

    def greet(self):
        peers = [(self.r, lax.rem(self.h + d, self.heads)) for d in range(1, self.heads)]
        peers += [self.on_x(d) for d in range(1, self.nx)] + [self.on_z(d) for d in range(1, self.nz)]
        barrier = pltpu.get_barrier_semaphore()
        for peer in peers:
            pl.semaphore_signal(barrier, inc=1, device_id=peer, device_id_type=MESH)
        pl.semaphore_wait(barrier, len(peers))


class Copies:
    def __init__(self, at, send, recv, local):
        self.at, self.send, self.recv, self.local = at, send, recv, local
        self.used, self.used_local = 0, 0
        self.unsent, self.open = [], []

    def put(self, src, dst, peer):
        copy = pltpu.make_async_remote_copy(
            src_ref=src,
            dst_ref=dst,
            send_sem=self.send.at[self.used],
            recv_sem=self.recv.at[self.used],
            device_id=peer,
            device_id_type=MESH,
        )
        self.used += 1
        copy.start()
        self.unsent.append(copy)
        return copy

    def put_y(self, src, dst):
        return [self.put(src, dst, self.at.on_y(d)) for d in range(1, self.at.ny)]

    def put_x(self, src, dst):
        return [self.put(src, dst, self.at.on_x(d)) for d in range(1, self.at.nx)]

    def put_z(self, src, dst):
        return [self.put(src, dst, self.at.on_z(d)) for d in range(1, self.at.nz)]

    def put_core(self, src, dst):
        return [self.put(src, dst, self.at.partner())] if self.at.nc > 1 else []

    def sent(self, copies):
        for copy in copies:
            copy.wait_send()
        self.unsent = [c for c in self.unsent if all(c is not d for d in copies)]

    def move(self, src, dst):
        copy = pltpu.make_async_copy(src, dst, self.local.at[self.used_local])
        self.used_local += 1
        copy.start()
        self.open.append(copy)
        return copy

    def moved(self, *copies):
        for copy in copies:
            copy.wait()
        self.open = [c for c in self.open if all(c is not d for d in copies)]

    def finish(self):
        for copy in self.unsent:
            copy.wait_send()
        for copy in self.open:
            copy.wait()


def arrived(copies):
    for copy in copies:
        copy.wait_recv()


def norm_rows(block):
    mean = jnp.mean(block, axis=-1, keepdims=True)
    centered = block - mean
    scale = lax.rsqrt(jnp.mean(centered * centered, axis=-1, keepdims=True) + EPSILON)
    return centered * scale, scale


def gelu_pair(v):
    c = math.sqrt(2.0 / math.pi)
    square = v * v
    t = jnp.tanh(c * v * (1.0 + 0.044715 * square))
    half = 0.5 * (1.0 + t)
    slope = half + 0.5 * v * (1.0 - t * t) * (c * (1.0 + 3.0 * 0.044715 * square))
    return v * half, slope


def softmax(scores):
    powers = jnp.exp(scores - jnp.max(scores, axis=-1, keepdims=True))
    return powers * (1.0 / jnp.sum(powers, axis=-1, keepdims=True))


def head_mask(heads_here, rows, cols):
    shape = (heads_here * rows, cols)
    row = lax.broadcasted_iota(jnp.int32, shape, 0) // rows
    col = lax.broadcasted_iota(jnp.int32, shape, 1) // HEAD_DIM
    return (row == col).astype(F32)


def spread_heads(block, mask):
    return jnp.concatenate([block] * (mask.shape[0] // block.shape[0]), axis=0) * mask


def gather_heads(block, mask, rows):
    block = block * mask
    return sum(block[j * rows : (j + 1) * rows] for j in range(block.shape[0] // rows))


def sizes_of(s):
    ny, nc = factor_head(s.heads)
    nz, nx = factor_rows(s.rows)
    t = types.SimpleNamespace(ny=ny, nc=nc, nz=nz, nx=nx, G=s.images, D=s.width, E=s.cols, F=s.mine, H=s.heads)
    t.pr, t.ll = s.patch, s.lat
    t.M, t.L, t.LR = t.G * t.pr, t.G * t.ll, t.H * t.ll
    t.GL, t.ML, t.KC = t.G * t.LR, t.M + t.L, t.H * t.pr + t.LR
    t.B = t.D // s.rows
    t.heads_here = t.E // HEAD_DIM
    t.aligned = t.E % 128 == 0
    t.EP = -(-t.E // 128) * 128
    return t


def forward_kernel(s, names, *refs):
    n = types.SimpleNamespace(**dict(zip(names, refs, strict=True)))
    at = Place(s.rows, s.heads)
    t = sizes_of(s)
    ny, nc, nz, nx, G, H = t.ny, t.nc, t.nz, t.nx, t.G, t.H
    M, L, LR, GL, ML, D, E, F, ll, pr = t.M, t.L, t.LR, t.GL, t.ML, t.D, t.E, t.F, t.ll, t.pr
    io = Copies(at, n.send, n.recv, n.local)
    here = at.r

    vectors = ("media_gain", "media_shift", "latent_gain", "latent_shift", "ffn_gain", "ffn_shift")
    load_vecs = [io.move(getattr(n, k), n.vecs.at[i]) for i, k in enumerate(vectors)]
    load_lat = io.move(n.lat, n.raw_l.at[0])
    load_cot = io.move(n.cot, n.cot_v)
    load_media = io.move(n.media, n.raw_m.at[0])

    def columns(weight):
        return weight.at[:, pl.ds(pl.multiple_of(at.h * E, 128), E)] if t.aligned else weight

    load_qkv = [io.move(columns(w), v) for w, v in ((n.wk, n.wk_v), (n.wv, n.wv_v), (n.wq, n.wq_v))]
    at.greet()

    chunks = 2
    part = M // chunks

    def far_slot(d):
        return (ny - d) % ny * nc

    lat_far = [io.put(n.lat, n.raw_l.at[far_slot(d)], at.on_y(d)) for d in range(1, ny)]
    lat_near = io.put_core(n.lat, n.raw_l.at[1 % H])
    media_far, media_near = [], []
    for j in range(chunks):
        rows = slice(j * part, (j + 1) * part)
        media_far.append([io.put(n.media.at[rows], n.raw_m.at[far_slot(d), rows], at.on_y(d)) for d in range(1, ny)])
        media_near.append(io.put_core(n.media.at[rows], n.raw_m.at[1 % H, rows]))

    io.moved(load_cot)
    for i in range(G):
        image = here * G + i
        limit = n.counts[image // MAX_IMG]
        live = jnp.where(lax.rem(image, MAX_IMG) < limit, 1.0, 0.0).astype(F32)
        rows = slice(i * ll, (i + 1) * ll)
        n.wide_l[rows] = n.cot_v[rows].astype(F32) * live
    n.dslot[at.y, at.c] = n.wide_l[...].astype(BF)
    own_d = n.dslot.at[at.y, at.c]

    def quarter(r, y):
        return r, pl.ds(pl.multiple_of(y * L, 16), L)

    def across(y, block):
        where = n.dall.at[quarter(here, y)]
        return io.put_z(block, where), io.put_x(block, where)

    z_far, x_far = {}, {}
    z_far[0], x_far[0] = across(at.y, own_d)
    load_out = io.move(n.wout, n.wout_v)
    load_up = io.move(n.wup.at[:, pl.ds(pl.multiple_of(at.h * F, 128), F)], n.wup_v)
    load_down = io.move(n.wdown.at[pl.ds(pl.multiple_of(at.h * F, 16), F)], n.wdown_v)

    def forward_x(d):
        for dz, copy in enumerate(z_far[d], 1):
            copy.wait_recv()
            block = n.dall.at[quarter(at.group(nz - dz, 0), at.y_peer(d))]
            x_far[d] += io.put_x(block, block)

    norm_busy = {}
    turn_count = [0]

    def patches(k, first, last):
        buf = turn_count[0] % 2
        turn_count[0] += 1
        if buf in norm_busy:
            io.moved(norm_busy[buf])
        gain, shift = n.vecs[0:1], n.vecs[1:2]
        for i in range(first, last):
            rows = slice(i * 16, (i + 1) * 16)
            hat, _ = norm_rows(n.raw_m[k, rows].astype(F32))
            n.norm[buf, rows] = (hat * gain + shift).astype(BF)
        rows = slice(first * 16, last * 16)
        for weight, result in ((n.wk_v, n.keys), (n.wv_v, n.values)):
            wide = mm(n.norm[buf, rows], weight[...]).astype(BF)
            for i in range(first * 16 // pr, last * 16 // pr):
                base = i * pr - first * 16
                result[i, k * pr : (k + 1) * pr] = wide[base : base + pr]
        norm_busy[buf] = io.move(n.norm.at[buf, rows], n.key_norm_o.at[k * ML + first * 16 : k * ML + last * 16])

    io.moved(load_media, *load_qkv, *load_vecs)
    patches(0, 0, M // 16)
    if nc > 1:
        for copies in media_near:
            arrived(copies)
        patches(1, 0, M // 16)
    cot_far = io.put_y(own_d, own_d)
    cot_near = io.put_core(own_d, own_d)
    relay = []
    for d, copy in zip(range(1, ny), lat_far):
        copy.wait_recv()
        k = far_slot(d)
        relay += io.put_core(n.raw_l.at[k], n.raw_l.at[k + 1]) if nc > 1 else []
    io.moved(load_lat)
    arrived(lat_near)
    arrived(relay)
    for k in range(H):
        wide = n.raw_l[k].astype(F32)
        for i in range(G):
            n.resid[pl.ds(pl.multiple_of(i * LR + at.head_of(k) * ll, 8), ll)] = wide[i * ll : (i + 1) * ll]
    gain, shift = n.vecs[2:3], n.vecs[3:4]
    for i in range(H * L // 16):
        hat, _ = norm_rows(n.raw_l[i * 16 // L, i * 16 % L : i * 16 % L + 16].astype(F32))
        n.lnorm[i * 16 : (i + 1) * 16] = (hat * gain + shift).astype(BF)
    for k in range(H):
        io.move(n.lnorm.at[k * L : (k + 1) * L], n.key_norm_o.at[k * ML + M : (k + 1) * ML])
    for weight, result in ((n.wq_v, n.query), (n.wk_v, n.keys), (n.wv_v, n.values)):
        wide = mm(n.lnorm[...], weight[...])
        for k in range(H):
            for i in range(G):
                n.turn[pl.ds(pl.multiple_of(i * LR + at.head_of(k) * ll, 8), ll)] = wide[k * L + i * ll : k * L + (i + 1) * ll]
        for i in range(G):
            block = n.turn[i * LR : (i + 1) * LR].astype(BF)
            if result is n.query:
                result[i] = block
            else:
                result[i, H * pr : t.KC] = block
    media_relay = []
    for j in range(chunks):
        relays = []
        rows = slice(j * part, (j + 1) * part)
        for d, copy in zip(range(1, ny), media_far[j]):
            copy.wait_recv()
            k = far_slot(d)
            relays.append(io.put_core(n.raw_m.at[k, rows], n.raw_m.at[k + 1, rows]) if nc > 1 else [])
        for d in range(1, ny):
            patches(far_slot(d), j * part // 16, (j + 1) * part // 16)
        for d in range(1, ny):
            if nc > 1:
                arrived(relays[d - 1])
                patches(far_slot(d) + 1, j * part // 16, (j + 1) * part // 16)
    forward_x(0)
    mask = head_mask(t.heads_here, LR, E)
    mask_low = mask.astype(BF)
    scale = 1.0 / math.sqrt(HEAD_DIM)
    for i in range(G):
        scores = mt(spread_heads(n.query[i], mask_low), n.keys[i]) * scale
        probs = softmax(scores).astype(BF)
        mixed = gather_heads(mm(probs, n.values[i]), mask, LR)
        n.mix[at.h, i * LR : (i + 1) * LR] = mixed.astype(BF)
    mix_far = io.put_y(n.mix.at[at.h], n.mix.at[at.h])
    mix_near = io.put_core(n.mix.at[at.h], n.mix.at[at.h])
    for ref, out in ((n.keys, n.keys_o), (n.values, n.values_o), (n.query, n.query_o)):
        io.move(ref, out)
    io.moved(load_out, load_up, load_down)

    def add_mixed(head):
        n.resid[...] += mm(n.mix[head], n.wout_v[pl.ds(pl.multiple_of(head * E, 16), E)])

    add_mixed(at.h)
    arrived(cot_far)
    cot_relay = []
    for d in range(1, ny):
        block = n.dslot.at[at.y_peer(d), at.c]
        cot_relay += io.put_core(block, block)
        z_far[d], x_far[d] = across(at.y_peer(d), block)
    arrived(mix_near)
    if nc > 1:
        add_mixed(at.head_of(1))
    arrived(cot_near)
    arrived(cot_relay)
    for y in range(ny):
        for c in range(nc):
            wide = n.dslot[y, c].astype(F32)
            for i in range(G):
                n.part[i * LR + (y * nc + c) * ll : i * LR + (y * nc + c + 1) * ll] = wide[i * ll : (i + 1) * ll]
    n.dout[...] = n.part[...].astype(BF)
    io.move(n.dout, n.dout_o)
    mix_relay = []
    for d, copy in zip(range(1, ny), mix_far):
        copy.wait_recv()
        block = n.mix.at[at.head_of(far_slot(d))]
        mix_relay.append(io.put_core(block, block))
    for d in range(1, ny):
        add_mixed(at.head_of(far_slot(d)))
    for d in range(1, ny):
        if nc > 1:
            arrived(mix_relay[d - 1])
            add_mixed(at.head_of(far_slot(d) + 1))
    io.move(n.mix, n.mixed_o)
    gain, shift = n.vecs[4:5], n.vecs[5:6]
    for i in range(GL // 16):
        rows = slice(i * 16, (i + 1) * 16)
        hat, inv = norm_rows(n.resid[rows])
        n.hat[rows] = hat
        n.inv[rows] = jnp.broadcast_to(inv, (16, 128))
        n.ffn[rows] = (hat * gain + shift).astype(BF)
    io.move(n.ffn, n.ffn_o)

    def own_rows(ref):
        return jnp.concatenate([ref[pl.ds(pl.multiple_of(i * LR + at.h * ll, 8), ll)] for i in range(G)], axis=0)

    n.fq[...] = (own_rows(n.hat) * gain + shift).astype(BF)
    own_f = n.fall.at[at.z]
    ffn_far = io.put_z(n.fq, own_f)
    io.move(n.fq, own_f)
    value, slope = gelu_pair(mm(n.ffn[...], n.wup_v[...]))
    n.act[...] = value.astype(BF)
    n.dhid[...] = (mt(n.dout[...], n.wdown_v[...]) * slope).astype(BF)
    n.part[...] = mt(n.dhid[...], n.wup_v[...])
    half = GL // nc
    mine = pl.ds(pl.multiple_of(at.c * half, 16), half)
    theirs = pl.ds(pl.multiple_of((nc - 1 - at.c) * half, 16), half)
    swap = io.put_core(n.part.at[theirs], n.c_recv)
    io.move(n.act, n.act_o)
    io.move(n.dhid, n.dhid_o)
    out_part = mm(n.act[...], n.wdown_v[...])
    for i in range(G):
        for head in range(H):
            base = i * LR + head * ll
            n.outp[head % nc, head // nc, i * ll : (i + 1) * ll] = out_part[base : base + ll]
    out_swap = io.put_core(n.outp.at[nc - 1 - at.c], n.oc_recv)
    arrived(swap)
    total = n.part[mine]
    if nc > 1:
        total = total + n.c_recv[...]
    n.y_send[...] = total.astype(BF)
    sum_far = [io.put(n.y_send, n.y_recv.at[d - 1], at.on_y(d)) for d in range(1, ny)]
    arrived(out_swap)
    for y in range(ny):
        total = n.outp[at.c, y]
        if nc > 1:
            total = total + n.oc_recv[y]
        n.outp[at.c, y] = total
        n.oy_send[y] = total.astype(BF)
    for d in range(1, ny):
        forward_x(d)
    io.sent(swap)
    arrived(sum_far)
    total = n.y_send[...].astype(F32)
    for d in range(1, ny):
        total = total + n.y_recv[d - 1].astype(F32)
    n.share[...] = total
    share = io.put_core(n.share, n.s_recv)

    def residual_back(ref, base):
        for i in range(half // 16):
            rows = pl.ds(pl.multiple_of(base + i * 16, 16), 16)
            grad = ref[i * 16 : (i + 1) * 16]
            hat, inv = n.hat[rows], n.inv[rows, 0:1]
            n.part[rows] = grad
            scaled = grad * gain
            first = jnp.mean(scaled, axis=-1, keepdims=True)
            second = jnp.mean(scaled * hat, axis=-1, keepdims=True)
            d_res = n.dout[rows].astype(F32) + inv * (scaled - first - hat * second)
            n.resid[rows] = d_res
            n.dattn[rows] = d_res.astype(BF)

    n.own[0] = n.outp[at.c, at.y] + own_rows(n.resid)
    io.move(n.own.at[0], n.out_o)
    io.move(n.oy_send, n.out_send_o)
    residual_back(n.share, at.c * half)
    if nc > 1:
        arrived(share)
        residual_back(n.s_recv, (nc - 1 - at.c) * half)
    io.move(n.dattn, n.dattn_o)
    n.own[1] = own_rows(n.resid)
    io.move(n.own.at[1], n.dres_o)
    grad = own_rows(n.part)
    n.fvec[0:1] = jnp.sum(grad * own_rows(n.hat), axis=0, keepdims=True)
    n.fvec[1:2] = jnp.sum(grad, axis=0, keepdims=True)
    n.fvec[2:8] = jnp.zeros((6, D), F32)
    io.move(n.fvec, n.fvec_o)
    for d in range(ny):
        arrived(x_far[d])
    arrived(ffn_far)
    io.finish()


def call(kernel, s, name, ident, ins, outs, scratch, semaphores, places, limit, cost):
    names = list(ins) + list(outs) + list(scratch) + ["send", "recv", "local"]
    dma = [pltpu.SemaphoreType.DMA((count,)) for count in (semaphores, semaphores, 120)]
    result = pl.pallas_call(
        functools.partial(kernel, s, names),
        name=name,
        out_shape=[jax.ShapeDtypeStruct(*o) for o in outs.values()],
        in_specs=[places.get(k, ANY) for k in ins],
        out_specs=[ANY] * len(outs),
        scratch_shapes=[pltpu.VMEM(*v) for v in scratch.values()] + dma,
        compiler_params=pltpu.CompilerParams(collective_id=ident, has_side_effects=True, vmem_limit_bytes=limit << 20),
        cost_estimate=cost,
    )(*ins.values())
    return dict(zip(outs, result, strict=True))


def forward(s, ins):
    t = sizes_of(s)
    ny, nc, G, H, M, L, LR, GL, ML, D, E, F = t.ny, t.nc, t.G, t.H, t.M, t.L, t.LR, t.GL, t.ML, t.D, t.E, t.F
    half = GL // nc
    far = max(ny - 1, 1)
    outs = dict(
        out_o=((L, D), F32), dres_o=((L, D), F32), fvec_o=((8, D), F32), key_norm_o=((H * ML, D), BF),
        keys_o=((G, t.KC, E), BF), values_o=((G, t.KC, E), BF), query_o=((G, LR, E), BF), mixed_o=((H, GL, E), BF),
        dattn_o=((GL, D), BF), ffn_o=((GL, D), BF), dout_o=((GL, D), BF), act_o=((GL, F), BF), dhid_o=((GL, F), BF),
        dall=((s.rows, ny * L, D), BF), fall=((t.nz, L, D), BF), out_send_o=((ny, L, D), BF),
    )
    scratch = dict(
        vecs=((8, D), F32), cot_v=((L, D), BF), wide_l=((L, D), F32), raw_m=((H, M, D), BF), raw_l=((H, L, D), BF), dslot=((ny, nc, L, D), BF),
        norm=((2, M, D), BF), lnorm=((H * L, D), BF), turn=((GL, E), F32), keys=((G, t.KC, E), BF), values=((G, t.KC, E), BF),
        query=((G, LR, E), BF), mix=((H, GL, E), BF), resid=((GL, D), F32), hat=((GL, D), F32), inv=((GL, 128), F32),
        ffn=((GL, D), BF), dout=((GL, D), BF), act=((GL, F), BF), dhid=((GL, F), BF), part=((GL, D), F32),
        outp=((nc, ny, L, D), F32), c_recv=((half, D), F32), oc_recv=((ny, L, D), F32), y_send=((half, D), BF),
        y_recv=((far, half, D), BF), oy_send=((ny, L, D), BF), share=((half, D), F32),
        s_recv=((half, D), F32), fq=((L, D), BF), own=((2, L, D), F32), dattn=((GL, D), BF),
        fvec=((8, D), F32), wq_v=((D, E), BF), wk_v=((D, E), BF), wv_v=((D, E), BF), wout_v=((D, D), BF),
        wup_v=((D, F), BF), wdown_v=((F, D), BF),
    )
    places = {"counts": SMEM}
    cost = pl.CostEstimate(flops=8 * 10**9, bytes_accessed=4 * 10**7, transcendentals=10**6)
    return call(forward_kernel, s, "forward", 1, ins, outs, scratch, 200, places, 62, cost)


def window_of(position, block, width):
    base = jnp.minimum(position * block // 128 * 128, width - 256)
    return pl.multiple_of(base, 128), position * block - base


def backward_kernel(s, names, *refs):
    n = types.SimpleNamespace(**dict(zip(names, refs, strict=True)))
    at = Place(s.rows, s.heads)
    t = sizes_of(s)
    ny, nc, nz, nx, G, H = t.ny, t.nc, t.nz, t.nx, t.G, t.H
    M, L, LR, GL, ML, D, E, F, ll, pr, B = t.M, t.L, t.LR, t.GL, t.ML, t.D, t.E, t.F, t.ll, t.pr, t.B
    here = at.r
    io = Copies(at, n.send, n.recv, n.local)

    def quarter(r, y):
        return r, pl.ds(pl.multiple_of((at.c * ny + y) * L, 16), L)

    aligned = t.aligned
    first_loads = [io.move(n.dattn, n.dattn_v), io.move(n.mixed, n.mix_v)]
    first_loads.append(io.move(n.wout.at[pl.ds(pl.multiple_of(at.h * E, 16), E)], n.wout_v))
    if aligned:
        first_loads.append(io.move(n.dattn.at[:, pl.ds(pl.multiple_of(at.h * E, 128), E)], n.dcols_v))
    else:
        first_loads.append(io.move(n.dattn_cols, n.dcols_v))
    attend_loads = [io.move(getattr(n, k), getattr(n, k + "_v")) for k in ("keys", "values", "query")]
    norm_load = io.move(n.key_norm, n.norm_v)
    own_loads = [io.move(getattr(n, k), getattr(n, k + "_v")) for k in ("act", "dhid")]
    own_loads += [io.move(n.ffn, n.ffn_v.at[0]), io.move(n.dout, n.dout_v.at[0])]
    ffn_loads = [io.move(n.wup.at[:, pl.ds(pl.multiple_of(at.h * F, 128), F)], n.wup_v)]
    ffn_loads.append(io.move(n.wdown.at[pl.ds(pl.multiple_of(at.h * F, 16), F)], n.wdown_v))
    if aligned:
        row_loads = []
        for head in range(H):
            for j, weight in enumerate((n.wk, n.wv)):
                lanes = slice((2 * head + j) * E, (2 * head + j + 1) * E)
                row_loads.append(io.move(weight.at[:, head * E : (head + 1) * E], n.w_v.at[:, lanes]))
    else:
        row_loads = [io.move(n.wkv, n.w_v)]
    row_loads += [io.move(n.media_gain, n.vecs.at[0]), io.move(n.latent_gain, n.vecs.at[1]), io.move(n.out_own, n.out_own_v)]
    row_loads += [io.move(n.media, n.media_v), io.move(n.lat, n.lat_v), io.move(n.dres, n.dres_v)]
    at.greet()

    x_quarters = []
    for dz in range(nz):
        source = n.fall.at[lax.rem(at.z + dz, nz)]
        x_quarters.append(io.put_x(source, n.fall_b.at[quarter(at.group(dz, 0), at.y)]))
    y_quarters = {}
    for dz in range(1, nz):
        source = n.fall.at[lax.rem(at.z + dz, nz)]
        y_quarters[dz, 0] = io.put_y(source, n.fall_b.at[quarter(at.group(dz, 0), at.y)])

    def core_rows(c):
        return pl.ds(pl.multiple_of(c * ny * L, 16), ny * L)

    blocks = {}

    def spread(dz, dx):
        arrived(y_quarters[dz, dx])
        r = at.group(dz, dx)
        copies = io.put_core(n.dall.at[r], n.dall_b.at[r])
        for d in range(ny):
            block = quarter(r, at.y_peer(d))
            source = n.fall.at[lax.rem(at.z + dz, nz)] if (d == 0 and dx == 0) else n.fall_b.at[block]
            copies += io.put_core(source, n.fall_b.at[block])
        blocks[dz, dx] = copies

    io.moved(*first_loads)
    n.dmixed[...] = mt(n.dattn_v[...], n.wout_v[...]).astype(BF).reshape(G, LR, E)
    span = nx * B
    if E == span:
        tiles = [tm(n.mix_v[z], n.dcols_v[...]) for z in range(nz)]
    else:
        whole = jnp.concatenate([n.mix_v[head] for head in range(H)], axis=-1)
        tiles = [tm(whole[:, z * span : (z + 1) * span], n.dcols_v[...]) for z in range(nz)]
    for z in range(nz):
        for x in range(nx):
            n.p_out[z, x] = tiles[z][x * B : (x + 1) * B].astype(BF)
    out_z = [io.put(n.p_out.at[lax.rem(at.z + d, nz)], n.zr_out.at[d - 1], at.on_z(d)) for d in range(1, nz)]

    def out_middle():
        arrived(out_z)
        total = n.p_out[at.z].astype(F32)
        for d in range(1, nz):
            total = total + n.zr_out[d - 1].astype(F32)
        n.p_out[at.z] = total.astype(BF)
        return [io.put(n.p_out.at[at.z, lax.rem(at.x + d, nx)], n.xr_out.at[d - 1], at.on_x(d)) for d in range(1, nx)]

    def out_end(copies):
        arrived(copies)
        total = n.p_out[at.z, at.x].astype(F32)
        for d in range(1, nx):
            total = total + n.xr_out[d - 1].astype(F32)
        n.grad_v[0] = total
        io.move(n.grad_v.at[0], n.out_grad)

    parts = {"kv": (n.p_kv, n.xr_kv, n.zr_kv), "query": (n.p_query, n.xr_query, n.zr_query)}
    x_parts, z_parts = {}, {}
    z_order = list(range(1, nz)) + [0]

    def sum_start(w, rows, grads):
        part, x_recv = parts[w][:2]
        for dz in z_order:
            lanes = pl.ds(pl.multiple_of(lax.rem(at.z + dz, nz) * span, 128), span)
            tile = tm(rows(lanes), grads)
            for x in range(nx):
                part[dz, x] = tile[x * B : (x + 1) * B].astype(BF)
            x_parts[w, dz] = [
                io.put(part.at[dz, lax.rem(at.x + d, nx)], x_recv.at[dz, d - 1], at.on_x(d)) for d in range(1, nx)
            ]

    def sum_middle(w, dz):
        part, x_recv, z_recv = parts[w]
        arrived(x_parts[w, dz])
        total = part[dz, at.x].astype(F32)
        for d in range(1, nx):
            total = total + x_recv[dz, d - 1].astype(F32)
        part[dz, at.x] = total.astype(BF)
        if dz:
            z_parts[w, dz] = [io.put(part.at[dz, at.x], z_recv.at[dz - 1], at.on_z(dz))]

    def sum_end(w, outs):
        part, _, z_recv = parts[w]
        total = part[0, at.x].astype(F32)
        for dz in range(1, nz):
            arrived(z_parts[w, dz])
            total = total + z_recv[dz - 1].astype(F32)
        for j, (ref, out) in enumerate(outs):
            ref[...] = total[:, j * E : (j + 1) * E]
            io.move(ref, out)

    io.moved(*attend_loads)
    mask = head_mask(t.heads_here, LR, E)
    mask_low = mask.astype(BF)
    scale = 1.0 / math.sqrt(HEAD_DIM)
    for i in range(G):
        q = spread_heads(n.query_v[i], mask_low)
        d = spread_heads(n.dmixed[i], mask_low)
        k, v = n.keys_v[i], n.values_v[i]
        probs = softmax(mt(q, k) * scale)
        d_probs = mt(d, v)
        inner = jnp.sum(probs * d_probs, axis=-1, keepdims=True)
        d_scores = (probs * (d_probs - inner)).astype(BF)
        d_query = gather_heads(mm(d_scores, k), mask, LR) * scale
        d_pair = jnp.concatenate([tm(d_scores, q) * scale, tm(probs.astype(BF), d)], axis=-1)
        for slot in range(H):
            rows = slice(slot * ML + i * pr, slot * ML + (i + 1) * pr)
            n.dkv[rows] = d_pair[slot * pr : (slot + 1) * pr].astype(BF)
        for head in range(H):
            rows = slice(H * pr + head * ll, H * pr + (head + 1) * ll)
            n.turn_kv[head, i * ll : (i + 1) * ll] = d_pair[rows]
            n.turn_q[head, i * ll : (i + 1) * ll, 0:E] = d_query[head * ll : (head + 1) * ll]
    if t.EP > E:
        n.turn_q[:, :, E : t.EP] = jnp.zeros((H, L, t.EP - E), F32)
    for slot in range(H):
        head = at.head_of(slot)
        n.dkv[slot * ML + M : (slot + 1) * ML] = n.turn_kv[head].astype(BF)
        n.dq[slot * L : (slot + 1) * L] = n.turn_q[head].astype(BF)
    kv_lanes = pl.ds(pl.multiple_of(at.h * 2 * E, 128), 2 * E)
    q_lanes = pl.ds(pl.multiple_of(at.h * t.EP, 128), t.EP)
    turned = []
    for slot in range(1, H):
        peer = (at.r, at.head_of(slot))
        turned.append(io.put(n.dkv.at[slot * ML : (slot + 1) * ML], n.dkv_full.at[:, kv_lanes], peer))
        turned.append(io.put(n.dq.at[slot * L : (slot + 1) * L], n.dq_full.at[:, q_lanes], peer))
    out_far = [io.put(n.out_send.at[at.y_peer(d)], n.out_recv.at[d - 1], at.on_y(d)) for d in range(1, ny)]
    io.moved(norm_load)
    sum_start("kv", lambda lanes: n.norm_v[:, lanes], n.dkv[...])
    sum_start(
        "query",
        lambda lanes: jnp.concatenate([n.norm_v[slot * ML + M : (slot + 1) * ML, lanes] for slot in range(H)], axis=0),
        n.dq[:, 0:E],
    )
    base, offset = window_of(here, B, D)
    window = pl.ds(base, 256)
    io.moved(*own_loads)
    n.up_acc[...] = tm(n.ffn_v[0, :, window], n.dhid_v[...])
    n.down_acc[...] = tm(n.dout_v[0, :, window], n.act_v[...])
    order = [(dz, 0) for dz in range(1, nz)] + [(dz, nx - dx) for dx in range(1, nx) for dz in range(nz)]
    fetched = {}

    def fetch(index):
        dz, dx = order[index]
        buf = (index + 1) % 2
        r = at.group(dz, dx)
        arrived(blocks[dz, dx])
        copies = []
        for c in range(nc):
            rows = core_rows(at.c if c == 0 else nc - 1 - at.c)
            source = n.dall if c == 0 else n.dall_b
            copies.append(io.move(source.at[r], n.dout_v.at[buf, rows]))
        if dx > 0:
            copies.append(io.move(n.fall_b.at[r], n.ffn_v.at[buf]))
        else:
            for slot in range(H):
                head = at.head_of(slot)
                rows = pl.ds(pl.multiple_of((head % nc * ny + head // nc) * L, 16), L)
                source = n.fall.at[lax.rem(at.z + dz, nz)] if slot == 0 else n.fall_b.at[r, rows]
                copies.append(io.move(source, n.ffn_v.at[buf, rows]))
        fetched[index] = copies

    def other_group(index):
        io.moved(*fetched[index])
        buf = (index + 1) % 2
        rows, grads = n.ffn_v[buf], n.dout_v[buf]
        value, slope = gelu_pair(mm(rows, n.wup_v[...]))
        d_hidden = (mt(grads, n.wdown_v[...]) * slope).astype(BF)
        n.up_acc[...] += tm(n.ffn_v[buf, :, window], d_hidden)
        n.down_acc[...] += tm(n.dout_v[buf, :, window], value.astype(BF))

    near = nz - 1
    for dz in range(1, nz):
        spread(dz, 0)
    fetch(0)
    io.moved(*ffn_loads)
    for index in range(near):
        if index + 1 < near:
            fetch(index + 1)
        other_group(index)
        if index == 0:
            for dx in range(1, nx):
                for dz in range(nz):
                    x_quarters[dz][dx - 1].wait_recv()
                    block = quarter(at.group(dz, nx - dx), at.y)
                    y_quarters[dz, nx - dx] = io.put_y(n.fall_b.at[block], n.fall_b.at[block])
    sum_middle("kv", z_order[0])
    out_x = out_middle()
    if nz > 2:
        sum_middle("kv", z_order[1])
    n.dkv_full[:, kv_lanes] = n.dkv[0:ML]
    n.dq_full[:, q_lanes] = n.dq[0:L]
    io.moved(*row_loads)
    arrived(turned)
    n.drow[...] = mt(n.dkv_full[...], n.w_v[...])
    q_load = io.move(n.wq, n.w_v.at[:, 0 : n.wq.shape[1]])

    def norm_back_rows(raw, first, count, base, gain, extra):
        sum_hat, sum_one = jnp.zeros((8, D), F32), jnp.zeros((8, D), F32)
        for i in range(first // 16, (first + count) // 16):
            rows = slice(i * 16, (i + 1) * 16)
            grad_rows = slice(base + i * 16, base + (i + 1) * 16)
            hat, inv = norm_rows(raw[rows].astype(F32))
            grad = n.drow[grad_rows]
            product = grad * hat
            sum_hat += product[:8] + product[8:]
            sum_one += grad[:8] + grad[8:]
            scaled = grad * gain
            mean = jnp.mean(scaled, axis=-1, keepdims=True)
            second = jnp.mean(scaled * hat, axis=-1, keepdims=True)
            result = inv * (scaled - mean - hat * second)
            n.drow[grad_rows] = result if extra is None else result + extra[rows]
        return [jnp.sum(v, axis=0, keepdims=True) for v in (sum_hat, sum_one)]

    n.vec_own[0:1], n.vec_own[1:2] = norm_back_rows(n.media_v, 0, M, 0, n.vecs[0:1], None)
    io.move(n.drow.at[0:M], n.media_o)
    io.moved(q_load)
    n.drow[M:ML] += mt(n.dq_full[...], n.w_v[:, 0 : n.wq.shape[1]])
    n.vec_own[2:3], n.vec_own[3:4] = norm_back_rows(n.lat_v, 0, L, M, n.vecs[1:2], n.dres_v)
    io.move(n.drow.at[M:ML], n.lat_o)
    n.vec_own[4:6] = n.fvec[0:2]
    n.vec_own[6:8] = jnp.zeros((2, D), F32)
    vec_head = [io.put(n.vec_own, n.vec_head.at[k - 1], (at.r, lax.rem(at.h + k, H))) for k in range(1, H)]
    for dz in z_order[min(2, nz - 1) :]:
        sum_middle("kv", dz)
    arrived(out_far)
    total = n.out_own_v[...]
    for d in range(1, ny):
        total = total + n.out_recv[d - 1].astype(F32)
    n.out_own_v[...] = total
    io.move(n.out_own_v, n.out_o)
    def vectors_middle():
        arrived(vec_head)
        total = n.vec_own[...]
        for k in range(1, H):
            total = total + n.vec_head[k - 1]
        for z in range(nz):
            n.vec_sum[z] = total[:, z * span : (z + 1) * span]
        vec_z = [io.put(n.vec_sum.at[lax.rem(at.z + d, nz)], n.vec_z.at[d - 1], at.on_z(d)) for d in range(1, nz)]
        return vec_z

    count = len(order)
    for index in range(near, count):
        spread(*order[index])
    query_order = list(z_order)
    for index in range(near, count):
        if index == near:
            fetch(index)
        if index + 1 < count:
            fetch(index + 1)
        other_group(index)
        if index == min(near + 2, count - 1):
            vec_z = vectors_middle()
        if index >= near + 1 and query_order:
            sum_middle("query", query_order.pop(0))
    for dz in query_order:
        sum_middle("query", dz)
    arrived(vec_z)
    total = n.vec_sum[at.z]
    for d in range(1, nz):
        total = total + n.vec_z[d - 1]
    n.vec_part[...] = total
    vec_x = [io.put(n.vec_part, n.vec_x.at[d - 1], at.on_x(d)) for d in range(1, nx)]
    own_rows = pl.ds(pl.multiple_of(offset, 8), B)
    io.move(n.up_acc.at[own_rows], n.up_grad)
    n.down_v[...] = n.down_acc[own_rows].T
    io.move(n.down_v, n.down_grad)
    out_end(out_x)
    sum_end("kv", [(n.grad_v.at[1], n.key_grad), (n.grad_v.at[2], n.value_grad)])
    arrived(vec_x)
    total = n.vec_part[...]
    for d in range(1, nx):
        total = total + n.vec_x[d - 1]
    n.vec_done[...] = total
    io.move(n.vec_done, n.vec_o)
    sum_end("query", [(n.grad_v.at[3], n.query_grad)])
    io.finish()


def backward(s, ins):
    t = sizes_of(s)
    ny, nc, nz, nx, G, H = t.ny, t.nc, t.nz, t.nx, t.G, t.H
    M, L, LR, GL, ML, D, E, F, B = t.M, t.L, t.LR, t.GL, t.ML, t.D, t.E, t.F, t.B
    fx, fz, fh = max(nx - 1, 1), max(nz - 1, 1), max(H - 1, 1)
    span = D // nz
    outs = dict(
        media_o=((M, D), F32), lat_o=((L, D), F32), query_grad=((B, E), F32), key_grad=((B, E), F32), value_grad=((B, E), F32),
        out_grad=((B, E), F32), up_grad=((B, F), F32), down_grad=((F, B), F32), vec_o=((8, span), F32), out_o=((L, D), F32),
        fall_b=((s.rows, GL, D), BF), dall_b=((s.rows, ny * L, D), BF),
    )
    scratch = dict(
        dattn_v=((GL, D), BF), mix_v=((H, GL, E), BF), wout_v=((E, D), BF), dcols_v=((GL, E), BF), dmixed=((G, LR, E), BF),
        keys_v=((G, t.KC, E), BF), values_v=((G, t.KC, E), BF), query_v=((G, LR, E), BF), norm_v=((H * ML, D), BF),
        ffn_v=((2, GL, D), BF), dout_v=((2, GL, D), BF), act_v=((GL, F), BF), dhid_v=((GL, F), BF), wup_v=((D, F), BF),
        wdown_v=((F, D), BF), w_v=((D, max(2 * D, H * t.EP)), BF), media_v=((M, D), BF), lat_v=((L, D), BF), dres_v=((L, D), F32),
        dkv=((H * ML, 2 * E), BF), dq=((H * L, t.EP), BF), turn_kv=((H, L, 2 * E), F32), turn_q=((H, L, t.EP), F32),
        dkv_full=((ML, 2 * D), BF), dq_full=((L, H * t.EP), BF), grad_v=((4, B, E), F32), up_acc=((256, F), F32),
        down_acc=((256, F), F32), drow=((ML, D), F32), vec_own=((8, D), F32), vec_head=((fh, 8, D), F32),
        vec_sum=((nz, 8, span), F32), vec_z=((fz, 8, span), F32), vec_part=((8, span), F32), vec_x=((fx, 8, span), F32),
        vec_done=((8, span), F32), vecs=((8, D), F32), out_own_v=((L, D), F32), out_recv=((max(ny - 1, 1), L, D), BF),
        down_v=((F, B), F32), p_out=((nz, nx, B, E), BF), zr_out=((fz, nx, B, E), BF), xr_out=((fx, B, E), BF),
    )
    for w, lanes in (("kv", 2 * E), ("query", E)):
        scratch["p_" + w] = ((nz, nx, B, lanes), BF)
        scratch["xr_" + w] = ((nz, fx, B, lanes), BF)
        scratch["zr_" + w] = ((fz, B, lanes), BF)
    places = {"fvec": VMEM}
    cost = pl.CostEstimate(flops=30 * 10**9, bytes_accessed=8 * 10**7, transcendentals=10**6)
    return call(backward_kernel, s, "backward", 2, ins, outs, scratch, 300, places, 62, cost)


def body(
    media, latents, counts, media_gain, media_shift, latent_gain, latent_shift, w_query, w_key, w_value, w_out,
    ffn_gain, ffn_shift, w_up, w_down, cotangent,
):
    rows, heads = lax.axis_size("rows"), lax.axis_size("head")
    at = Place(rows, heads)
    images, patch, width = media.shape
    lat = latents.shape[1]
    cols = width // heads
    s = types.SimpleNamespace(
        rows=rows, heads=heads, images=images, patch=patch, lat=lat, width=width, cols=cols, mine=w_up.shape[1] // heads
    )
    t = sizes_of(s)

    def columns(array):
        return array if t.aligned else lax.dynamic_slice_in_dim(array, at.h * cols, cols, 1)

    gains = dict(
        media_gain=media_gain, media_shift=media_shift, latent_gain=latent_gain, latent_shift=latent_shift,
        ffn_gain=ffn_gain, ffn_shift=ffn_shift,
    )
    rows_in = dict(media=media.reshape(-1, width), lat=latents.reshape(-1, width))
    a = forward(
        s,
        dict(
            rows_in, cot=cotangent.reshape(-1, width), counts=counts, **gains, wq=columns(w_query), wk=columns(w_key),
            wv=columns(w_value), wout=w_out, wup=w_up, wdown=w_down,
        ),
    )
    ins = dict(
        rows_in, media_gain=gains["media_gain"], latent_gain=gains["latent_gain"], fvec=a["fvec_o"], dres=a["dres_o"],
        key_norm=a["key_norm_o"], keys=a["keys_o"], values=a["values_o"], query=a["query_o"], mixed=a["mixed_o"],
        dattn=a["dattn_o"], ffn=a["ffn_o"], dout=a["dout_o"], act=a["act_o"], dhid=a["dhid_o"], dall=a["dall"], fall=a["fall"],
        wout=w_out, wup=w_up, wdown=w_down, out_own=a["out_o"], out_send=a["out_send_o"],
    )
    if t.aligned:
        ins.update(wk=w_key, wv=w_value, wq=w_query)
    else:
        pair = jnp.stack([w_key.reshape(width, heads, cols), w_value.reshape(width, heads, cols)], axis=2)
        padded = jnp.pad(w_query.reshape(width, heads, cols), ((0, 0), (0, 0), (0, t.EP - cols)))
        ins.update(wkv=pair.reshape(width, 2 * width), wq=padded.reshape(width, -1), dattn_cols=columns(a["dattn_o"]))
    b = backward(s, ins)
    share = width // (rows * heads)
    vector = lax.dynamic_slice_in_dim(b["vec_o"], (at.x * heads + at.h) * share, share, 1)
    return (
        b["out_o"].reshape(latents.shape), b["media_o"].reshape(media.shape), b["lat_o"].reshape(latents.shape),
        vector[0], vector[1], vector[2], vector[3], b["query_grad"], b["key_grad"], b["value_grad"], b["out_grad"],
        vector[4], vector[5], b["up_grad"], b["down_grad"],
    )


def solution(mesh):
    row = P("rows", "head", None)
    whole = P()
    vector = P(("rows", "head"))
    grid = P("rows", "head")
    return jax.shard_map(
        body,
        mesh=mesh,
        in_specs=(row, row) + (whole,) * 13 + (row,),
        out_specs=(row, row, row, vector, vector, vector, vector, grid, grid, grid, grid, vector, vector, grid, P("head", "rows")),
        check_vma=False,
    )
```

```python
import functools
import math
import types

import jax
import jax.numpy as jnp
from jax import lax
from jax.experimental import pallas as pl
from jax.experimental.pallas import tpu as pltpu
from jax.sharding import PartitionSpec as P

HEAD_DIM = 96
MAX_IMG = 8
EPSILON = 1e-05
BF = jnp.bfloat16
F32 = jnp.float32
MESH = pl.DeviceIdType.MESH
ANY = pl.BlockSpec(memory_space=pl.ANY)
VMEM = pl.BlockSpec(memory_space=pltpu.VMEM)
SMEM = pl.BlockSpec(memory_space=pltpu.SMEM)


def factor_rows(count):
    nz = 4 if count % 4 == 0 else 1
    return nz, count // nz


def factor_head(count):
    nc = 2 if count % 2 == 0 else 1
    return count // nc, nc


def mm(a, b):
    return lax.dot_general(a, b, (((1,), (0,)), ((), ())), preferred_element_type=F32)


def mt(a, b):
    return lax.dot_general(a, b, (((1,), (1,)), ((), ())), preferred_element_type=F32)


def tm(a, b):
    return lax.dot_general(a, b, (((0,), (0,)), ((), ())), preferred_element_type=F32)


class Place:
    def __init__(self, rows, heads):
        self.rows, self.heads = rows, heads
        self.nz, self.nx = factor_rows(rows)
        self.ny, self.nc = factor_head(heads)
        self.r = lax.axis_index("rows")
        self.h = lax.axis_index("head")
        self.z, self.x = self.r // self.nx, self.r % self.nx
        self.y, self.c = self.h // self.nc, self.h % self.nc

    def y_peer(self, d):
        return lax.rem(self.y + d, self.ny)

    def group(self, dz, dx):
        return lax.rem(self.z + dz, self.nz) * self.nx + lax.rem(self.x + dx, self.nx)

    def head_of(self, slot):
        d, e = divmod(slot, self.nc)
        return self.y_peer(d) * self.nc + (self.c if e == 0 else self.nc - 1 - self.c)

    def on_y(self, d):
        return self.r, self.y_peer(d) * self.nc + self.c

    def on_x(self, d):
        return self.group(0, d), self.h

    def on_z(self, d):
        return self.group(d, 0), self.h

    def partner(self):
        return self.r, self.y * self.nc + (self.nc - 1 - self.c)

    def greet(self):
        peers = [(self.r, lax.rem(self.h + d, self.heads)) for d in range(1, self.heads)]
        peers += [self.on_x(d) for d in range(1, self.nx)] + [self.on_z(d) for d in range(1, self.nz)]
        barrier = pltpu.get_barrier_semaphore()
        for peer in peers:
            pl.semaphore_signal(barrier, inc=1, device_id=peer, device_id_type=MESH)
        pl.semaphore_wait(barrier, len(peers))


class Copies:
    def __init__(self, at, send, recv, local):
        self.at, self.send, self.recv, self.local = at, send, recv, local
        self.used, self.used_local = 0, 0
        self.unsent, self.open = [], []

    def plan(self, src, dst, peer):
        copy = pltpu.make_async_remote_copy(
            src_ref=src,
            dst_ref=dst,
            send_sem=self.send.at[self.used],
            recv_sem=self.recv.at[self.used],
            device_id=peer,
            device_id_type=MESH,
        )
        self.used += 1
        self.unsent.append(copy)
        return copy

    def put(self, src, dst, peer):
        copy = self.plan(src, dst, peer)
        copy.start()
        return copy

    def put_y(self, src, dst):
        return [self.put(src, dst, self.at.on_y(d)) for d in range(1, self.at.ny)]

    def put_x(self, src, dst):
        return [self.put(src, dst, self.at.on_x(d)) for d in range(1, self.at.nx)]

    def put_z(self, src, dst):
        return [self.put(src, dst, self.at.on_z(d)) for d in range(1, self.at.nz)]

    def put_core(self, src, dst):
        return [self.put(src, dst, self.at.partner())] if self.at.nc > 1 else []

    def sent(self, copies):
        for copy in copies:
            copy.wait_send()
        self.unsent = [c for c in self.unsent if all(c is not d for d in copies)]

    def plan_move(self, src, dst):
        copy = pltpu.make_async_copy(src, dst, self.local.at[self.used_local])
        self.used_local += 1
        self.open.append(copy)
        return copy

    def move(self, src, dst):
        copy = self.plan_move(src, dst)
        copy.start()
        return copy

    def moved(self, *copies):
        for copy in copies:
            copy.wait()
        self.open = [c for c in self.open if all(c is not d for d in copies)]

    def finish(self):
        for copy in self.unsent:
            copy.wait_send()
        for copy in self.open:
            copy.wait()


def begin(copies):
    for copy in copies:
        copy.start()


def arrived(copies):
    for copy in copies:
        copy.wait_recv()


def norm_rows(block):
    mean = jnp.mean(block, axis=-1, keepdims=True)
    centered = block - mean
    scale = lax.rsqrt(jnp.mean(centered * centered, axis=-1, keepdims=True) + EPSILON)
    return centered * scale, scale


def sweep(first, last, step, carry=0):
    together = next(k for k in (4, 2, 1) if (last - first) // 16 % k == 0)

    def turn(i, value):
        for j in range(together):
            start = first + i * (16 * together) + j * 16
            value = step(pl.ds(pl.multiple_of(start, 16), 16), value)
        return value

    return lax.fori_loop(0, (last - first) // (16 * together), turn, carry)


def gelu_pair(v):
    c = math.sqrt(2.0 / math.pi)
    square = v * v
    t = jnp.tanh(c * v * (1.0 + 0.044715 * square))
    half = 0.5 * (1.0 + t)
    slope = half + 0.5 * v * (1.0 - t * t) * (c * (1.0 + 3.0 * 0.044715 * square))
    return v * half, slope


def softmax(scores):
    powers = jnp.exp(scores - jnp.max(scores, axis=-1, keepdims=True))
    return powers * (1.0 / jnp.sum(powers, axis=-1, keepdims=True))


def head_mask(heads_here, rows, cols):
    shape = (heads_here * rows, cols)
    row = lax.broadcasted_iota(jnp.int32, shape, 0) // rows
    col = lax.broadcasted_iota(jnp.int32, shape, 1) // HEAD_DIM
    return (row == col).astype(F32)


def spread_heads(block, mask):
    return jnp.concatenate([block] * (mask.shape[0] // block.shape[0]), axis=0) * mask


def gather_heads(block, mask, rows):
    block = block * mask
    return sum(block[j * rows : (j + 1) * rows] for j in range(block.shape[0] // rows))


def sizes_of(s):
    ny, nc = factor_head(s.heads)
    nz, nx = factor_rows(s.rows)
    t = types.SimpleNamespace(ny=ny, nc=nc, nz=nz, nx=nx, G=s.images, D=s.width, E=s.cols, F=s.mine, H=s.heads)
    t.pr, t.ll = s.patch, s.lat
    t.M, t.L, t.LR = t.G * t.pr, t.G * t.ll, t.H * t.ll
    t.GL, t.ML, t.KC = t.G * t.LR, t.M + t.L, t.H * t.pr + t.LR
    t.B = t.D // s.rows
    t.heads_here = t.E // HEAD_DIM
    t.aligned = t.E % 128 == 0
    t.EP = -(-t.E // 128) * 128
    return t


def forward_kernel(s, names, *refs):
    n = types.SimpleNamespace(**dict(zip(names, refs, strict=True)))
    at = Place(s.rows, s.heads)
    t = sizes_of(s)
    ny, nc, nz, nx, G, H = t.ny, t.nc, t.nz, t.nx, t.G, t.H
    M, L, LR, GL, ML, D, E, F, ll, pr = t.M, t.L, t.LR, t.GL, t.ML, t.D, t.E, t.F, t.ll, t.pr
    io = Copies(at, n.send, n.recv, n.local)
    here = at.r

    vectors = ("media_gain", "media_shift", "latent_gain", "latent_shift", "ffn_gain", "ffn_shift")
    load_vecs = [io.move(getattr(n, k), n.vecs.at[i]) for i, k in enumerate(vectors)]
    load_lat = io.move(n.lat, n.raw_l.at[0:L])
    load_cot = io.move(n.cot, n.cot_v)
    load_media = io.move(n.media, n.raw_m.at[0])

    def columns(weight):
        return weight.at[:, pl.ds(pl.multiple_of(at.h * E, 128), E)] if t.aligned else weight

    load_qkv = [io.move(columns(w), v) for w, v in ((n.wk, n.wk_v), (n.wv, n.wv_v), (n.wq, n.wq_v))]
    at.greet()

    chunks = 2
    part = M // chunks

    def far_slot(d):
        return (ny - d) % ny * nc

    def lat_rows(k):
        return n.raw_l.at[k * L : (k + 1) * L]

    lat_far = [io.put(n.lat, lat_rows(far_slot(d)), at.on_y(d)) for d in range(1, ny)]
    lat_near = io.put_core(n.lat, lat_rows(1 % H))
    media_far, media_near = [], []
    for j in range(chunks):
        rows = slice(j * part, (j + 1) * part)
        media_far.append([io.put(n.media.at[rows], n.raw_m.at[far_slot(d), rows], at.on_y(d)) for d in range(1, ny)])
        media_near.append(io.put_core(n.media.at[rows], n.raw_m.at[1 % H, rows]))

    io.moved(load_cot)
    for i in range(G):
        image = here * G + i
        limit = n.counts[image // MAX_IMG]
        live = jnp.where(lax.rem(image, MAX_IMG) < limit, 1.0, 0.0).astype(F32)
        rows = slice(i * ll, (i + 1) * ll)
        n.wide_l[rows] = n.cot_v[rows].astype(F32) * live
    n.dslot[at.y, at.c] = n.wide_l[...].astype(BF)
    own_d = n.dslot.at[at.y, at.c]

    def quarter(r, y):
        return r, pl.ds(pl.multiple_of(y * L, 16), L)

    def across(y, block):
        where = n.dall.at[quarter(here, y)]
        return io.put_z(block, where), io.put_x(block, where)

    z_far, x_far = {}, {}
    z_far[0], x_far[0] = across(at.y, own_d)
    load_out = io.move(n.wout, n.wout_v)
    load_up = io.move(n.wup.at[:, pl.ds(pl.multiple_of(at.h * F, 128), F)], n.wup_v)
    load_down = io.move(n.wdown.at[pl.ds(pl.multiple_of(at.h * F, 16), F)], n.wdown_v)

    def forward_x(d):
        for dz, copy in enumerate(z_far[d], 1):
            copy.wait_recv()
            block = n.dall.at[quarter(at.group(nz - dz, 0), at.y_peer(d))]
            x_far[d] += io.put_x(block, block)

    norm_busy = {}
    turn_count = [0]

    def patches(k, first, last):
        buf = turn_count[0] % 2
        turn_count[0] += 1
        if buf in norm_busy:
            io.moved(norm_busy[buf])

        def step(rows, carry):
            hat, _ = norm_rows(n.raw_m[k, rows].astype(F32))
            n.norm[buf, rows] = (hat * n.vecs[0:1] + n.vecs[1:2]).astype(BF)
            return carry

        sweep(first * 16, last * 16, step)
        rows = slice(first * 16, last * 16)
        for weight, result in ((n.wk_v, n.keys), (n.wv_v, n.values)):
            wide = mm(n.norm[buf, rows], weight[...]).astype(BF)
            for i in range(first * 16 // pr, last * 16 // pr):
                base = i * pr - first * 16
                result[i, k * pr : (k + 1) * pr] = wide[base : base + pr]
        norm_busy[buf] = io.move(n.norm.at[buf, rows], n.key_norm_o.at[k * ML + first * 16 : k * ML + last * 16])

    io.moved(load_media, *load_qkv, *load_vecs)
    patches(0, 0, M // 16)
    if nc > 1:
        for copies in media_near:
            arrived(copies)
        patches(1, 0, M // 16)
    cot_far = io.put_y(own_d, own_d)
    cot_near = io.put_core(own_d, own_d)
    relay = []
    for d, copy in zip(range(1, ny), lat_far):
        copy.wait_recv()
        k = far_slot(d)
        relay += io.put_core(lat_rows(k), lat_rows(k + 1)) if nc > 1 else []
    io.moved(load_lat)
    arrived(lat_near)
    arrived(relay)
    for k in range(H):
        wide = n.raw_l[k * L : (k + 1) * L].astype(F32)
        for i in range(G):
            n.resid[pl.ds(pl.multiple_of(i * LR + at.head_of(k) * ll, 8), ll)] = wide[i * ll : (i + 1) * ll]

    def latent_step(rows, carry):
        hat, _ = norm_rows(n.raw_l[rows].astype(F32))
        n.lnorm[rows] = (hat * n.vecs[2:3] + n.vecs[3:4]).astype(BF)
        return carry

    sweep(0, H * L, latent_step)
    for k in range(H):
        io.move(n.lnorm.at[k * L : (k + 1) * L], n.key_norm_o.at[k * ML + M : (k + 1) * ML])
    for weight, result in ((n.wq_v, n.query), (n.wk_v, n.keys), (n.wv_v, n.values)):
        wide = mm(n.lnorm[...], weight[...])
        for k in range(H):
            for i in range(G):
                n.turn[pl.ds(pl.multiple_of(i * LR + at.head_of(k) * ll, 8), ll)] = wide[k * L + i * ll : k * L + (i + 1) * ll]
        for i in range(G):
            block = n.turn[i * LR : (i + 1) * LR].astype(BF)
            if result is n.query:
                result[i] = block
            else:
                result[i, H * pr : t.KC] = block
    media_relay = []
    for j in range(chunks):
        relays = []
        rows = slice(j * part, (j + 1) * part)
        for d, copy in zip(range(1, ny), media_far[j]):
            copy.wait_recv()
            k = far_slot(d)
            relays.append(io.put_core(n.raw_m.at[k, rows], n.raw_m.at[k + 1, rows]) if nc > 1 else [])
        for d in range(1, ny):
            patches(far_slot(d), j * part // 16, (j + 1) * part // 16)
        for d in range(1, ny):
            if nc > 1:
                arrived(relays[d - 1])
                patches(far_slot(d) + 1, j * part // 16, (j + 1) * part // 16)
    forward_x(0)
    mask = head_mask(t.heads_here, LR, E)
    mask_low = mask.astype(BF)
    scale = 1.0 / math.sqrt(HEAD_DIM)
    for i in range(G):
        scores = mt(spread_heads(n.query[i], mask_low), n.keys[i]) * scale
        probs = softmax(scores).astype(BF)
        mixed = gather_heads(mm(probs, n.values[i]), mask, LR)
        n.mix[at.h, i * LR : (i + 1) * LR] = mixed.astype(BF)
    mix_far = io.put_y(n.mix.at[at.h], n.mix.at[at.h])
    mix_near = io.put_core(n.mix.at[at.h], n.mix.at[at.h])
    for ref, out in ((n.keys, n.keys_o), (n.values, n.values_o), (n.query, n.query_o)):
        io.move(ref, out)
    io.moved(load_out, load_up, load_down)

    def add_mixed(head):
        n.resid[...] += mm(n.mix[head], n.wout_v[pl.ds(pl.multiple_of(head * E, 16), E)])

    add_mixed(at.h)
    arrived(cot_far)
    cot_relay = []
    for d in range(1, ny):
        block = n.dslot.at[at.y_peer(d), at.c]
        cot_relay += io.put_core(block, block)
        z_far[d], x_far[d] = across(at.y_peer(d), block)
    arrived(mix_near)
    if nc > 1:
        add_mixed(at.head_of(1))
    arrived(cot_near)
    arrived(cot_relay)
    for y in range(ny):
        for c in range(nc):
            wide = n.dslot[y, c].astype(F32)
            for i in range(G):
                n.part[i * LR + (y * nc + c) * ll : i * LR + (y * nc + c + 1) * ll] = wide[i * ll : (i + 1) * ll]
    n.dout[...] = n.part[...].astype(BF)
    io.move(n.dout, n.dout_o)
    mix_relay = []
    for d, copy in zip(range(1, ny), mix_far):
        copy.wait_recv()
        block = n.mix.at[at.head_of(far_slot(d))]
        mix_relay.append(io.put_core(block, block))
    for d in range(1, ny):
        add_mixed(at.head_of(far_slot(d)))
    for d in range(1, ny):
        if nc > 1:
            arrived(mix_relay[d - 1])
            add_mixed(at.head_of(far_slot(d) + 1))
    io.move(n.mix, n.mixed_o)
    gain, shift = n.vecs[4:5], n.vecs[5:6]

    def ffn_step(rows, carry):
        hat, inv = norm_rows(n.resid[rows])
        n.hat[rows] = hat
        n.inv[rows] = jnp.broadcast_to(inv, (16, 128))
        n.ffn[rows] = (hat * n.vecs[4:5] + n.vecs[5:6]).astype(BF)
        return carry

    sweep(0, GL, ffn_step)
    io.move(n.ffn, n.ffn_o)

    def own_rows(ref):
        return jnp.concatenate([ref[pl.ds(pl.multiple_of(i * LR + at.h * ll, 8), ll)] for i in range(G)], axis=0)

    n.fq[...] = (own_rows(n.hat) * gain + shift).astype(BF)
    own_f = n.fall.at[at.z]
    ffn_far = io.put_z(n.fq, own_f)
    io.move(n.fq, own_f)
    value, slope = gelu_pair(mm(n.ffn[...], n.wup_v[...]))
    n.act[...] = value.astype(BF)
    n.dhid[...] = (mt(n.dout[...], n.wdown_v[...]) * slope).astype(BF)
    n.part[...] = mt(n.dhid[...], n.wup_v[...])
    half = GL // nc
    mine = pl.ds(pl.multiple_of(at.c * half, 16), half)
    theirs = pl.ds(pl.multiple_of((nc - 1 - at.c) * half, 16), half)
    swap = io.put_core(n.part.at[theirs], n.c_recv)
    io.move(n.act, n.act_o)
    io.move(n.dhid, n.dhid_o)
    out_part = mm(n.act[...], n.wdown_v[...])
    for i in range(G):
        for head in range(H):
            base = i * LR + head * ll
            n.outp[head % nc, head // nc, i * ll : (i + 1) * ll] = out_part[base : base + ll]
    out_swap = io.put_core(n.outp.at[nc - 1 - at.c], n.oc_recv)
    arrived(swap)
    total = n.part[mine]
    if nc > 1:
        total = total + n.c_recv[...]
    n.y_send[...] = total.astype(BF)
    sum_far = [io.put(n.y_send, n.y_recv.at[d - 1], at.on_y(d)) for d in range(1, ny)]
    arrived(out_swap)
    for y in range(ny):
        total = n.outp[at.c, y]
        if nc > 1:
            total = total + n.oc_recv[y]
        n.outp[at.c, y] = total
        n.oy_send[y] = total.astype(BF)
    for d in range(1, ny):
        forward_x(d)
    io.sent(swap)
    arrived(sum_far)
    total = n.y_send[...].astype(F32)
    for d in range(1, ny):
        total = total + n.y_recv[d - 1].astype(F32)
    n.share[...] = total
    share = io.put_core(n.share, n.s_recv)

    def residual_back(ref, base):
        def step(from_rows, carry):
            rows = pl.ds(pl.multiple_of(base + from_rows.start, 16), 16)
            grad = ref[from_rows]
            hat, inv = n.hat[rows], n.inv[rows, 0:1]
            n.part[rows] = grad
            scaled = grad * n.vecs[4:5]
            first = jnp.mean(scaled, axis=-1, keepdims=True)
            second = jnp.mean(scaled * hat, axis=-1, keepdims=True)
            d_res = n.dout[rows].astype(F32) + inv * (scaled - first - hat * second)
            n.resid[rows] = d_res
            n.dattn[rows] = d_res.astype(BF)
            return carry

        sweep(0, half, step)

    n.own[0] = n.outp[at.c, at.y] + own_rows(n.resid)
    io.move(n.own.at[0], n.out_o)
    io.move(n.oy_send, n.out_send_o)
    residual_back(n.share, at.c * half)
    if nc > 1:
        arrived(share)
        residual_back(n.s_recv, (nc - 1 - at.c) * half)
    io.move(n.dattn, n.dattn_o)
    n.own[1] = own_rows(n.resid)
    io.move(n.own.at[1], n.dres_o)
    grad = own_rows(n.part)
    n.fvec[0:1] = jnp.sum(grad * own_rows(n.hat), axis=0, keepdims=True)
    n.fvec[1:2] = jnp.sum(grad, axis=0, keepdims=True)
    n.fvec[2:8] = jnp.zeros((6, D), F32)
    io.move(n.fvec, n.fvec_o)
    for d in range(ny):
        arrived(x_far[d])
    arrived(ffn_far)
    io.finish()


def call(kernel, s, name, ident, ins, outs, scratch, semaphores, places, limit, cost):
    names = list(ins) + list(outs) + list(scratch) + ["send", "recv", "local"]
    dma = [pltpu.SemaphoreType.DMA((count,)) for count in (semaphores, semaphores, 120)]
    result = pl.pallas_call(
        functools.partial(kernel, s, names),
        name=name,
        out_shape=[jax.ShapeDtypeStruct(*o) for o in outs.values()],
        in_specs=[places.get(k, ANY) for k in ins],
        out_specs=[ANY] * len(outs),
        scratch_shapes=[pltpu.VMEM(*v) for v in scratch.values()] + dma,
        compiler_params=pltpu.CompilerParams(collective_id=ident, has_side_effects=True, vmem_limit_bytes=limit << 20),
        cost_estimate=cost,
    )(*ins.values())
    return dict(zip(outs, result, strict=True))


def forward(s, ins):
    t = sizes_of(s)
    ny, nc, G, H, M, L, LR, GL, ML, D, E, F = t.ny, t.nc, t.G, t.H, t.M, t.L, t.LR, t.GL, t.ML, t.D, t.E, t.F
    half = GL // nc
    far = max(ny - 1, 1)
    outs = dict(
        out_o=((L, D), F32), dres_o=((L, D), F32), fvec_o=((8, D), F32), key_norm_o=((H * ML, D), BF),
        keys_o=((G, t.KC, E), BF), values_o=((G, t.KC, E), BF), query_o=((G, LR, E), BF), mixed_o=((H, GL, E), BF),
        dattn_o=((GL, D), BF), ffn_o=((GL, D), BF), dout_o=((GL, D), BF), act_o=((GL, F), BF), dhid_o=((GL, F), BF),
        dall=((s.rows, ny * L, D), BF), fall=((t.nz, L, D), BF), out_send_o=((ny, L, D), BF),
    )
    scratch = dict(
        vecs=((8, D), F32), cot_v=((L, D), BF), wide_l=((L, D), F32), raw_m=((H, M, D), BF), raw_l=((H * L, D), BF), dslot=((ny, nc, L, D), BF),
        norm=((2, M, D), BF), lnorm=((H * L, D), BF), turn=((GL, E), F32), keys=((G, t.KC, E), BF), values=((G, t.KC, E), BF),
        query=((G, LR, E), BF), mix=((H, GL, E), BF), resid=((GL, D), F32), hat=((GL, D), F32), inv=((GL, 128), F32),
        ffn=((GL, D), BF), dout=((GL, D), BF), act=((GL, F), BF), dhid=((GL, F), BF), part=((GL, D), F32),
        outp=((nc, ny, L, D), F32), c_recv=((half, D), F32), oc_recv=((ny, L, D), F32), y_send=((half, D), BF),
        y_recv=((far, half, D), BF), oy_send=((ny, L, D), BF), share=((half, D), F32),
        s_recv=((half, D), F32), fq=((L, D), BF), own=((2, L, D), F32), dattn=((GL, D), BF),
        fvec=((8, D), F32), wq_v=((D, E), BF), wk_v=((D, E), BF), wv_v=((D, E), BF), wout_v=((D, D), BF),
        wup_v=((D, F), BF), wdown_v=((F, D), BF),
    )
    places = {"counts": SMEM}
    cost = pl.CostEstimate(flops=8 * 10**9, bytes_accessed=4 * 10**7, transcendentals=10**6)
    return call(forward_kernel, s, "forward", 1, ins, outs, scratch, 200, places, 62, cost)


def window_of(position, block, width):
    base = jnp.minimum(position * block // 128 * 128, width - 256)
    return pl.multiple_of(base, 128), position * block - base


def backward_kernel(s, names, *refs):
    n = types.SimpleNamespace(**dict(zip(names, refs, strict=True)))
    at = Place(s.rows, s.heads)
    t = sizes_of(s)
    ny, nc, nz, nx, G, H = t.ny, t.nc, t.nz, t.nx, t.G, t.H
    M, L, LR, GL, ML, D, E, F, ll, pr, B = t.M, t.L, t.LR, t.GL, t.ML, t.D, t.E, t.F, t.ll, t.pr, t.B
    here = at.r
    io = Copies(at, n.send, n.recv, n.local)

    def quarter(r, y):
        return r, pl.ds(pl.multiple_of((at.c * ny + y) * L, 16), L)

    aligned = t.aligned
    first_loads = [io.move(n.dattn, n.ffn_v.at[1]), io.move(n.mixed, n.mix_v)]
    first_loads.append(io.move(n.wout.at[pl.ds(pl.multiple_of(at.h * E, 16), E)], n.wout_v))
    if aligned:
        first_loads.append(io.move(n.dattn.at[:, pl.ds(pl.multiple_of(at.h * E, 128), E)], n.dcols_v))
    else:
        first_loads.append(io.move(n.dattn_cols, n.dcols_v))
    attend_loads = [io.move(getattr(n, k), getattr(n, k + "_v")) for k in ("keys", "values", "query")]
    norm_load = io.move(n.key_norm, n.norm_v)
    own_loads = [io.move(n.act, n.dout_v.at[1, :, 0:F]), io.move(n.ffn, n.ffn_v.at[0]), io.move(n.dout, n.dout_v.at[0])]
    ffn_loads = [io.move(n.wup.at[:, pl.ds(pl.multiple_of(at.h * F, 128), F)], n.wup_v)]
    ffn_loads.append(io.move(n.wdown.at[pl.ds(pl.multiple_of(at.h * F, 16), F)], n.wdown_v))
    if aligned:
        row_loads = []
        for head in range(H):
            for j, weight in enumerate((n.wk, n.wv)):
                lanes = slice((2 * head + j) * E, (2 * head + j + 1) * E)
                row_loads.append(io.move(weight.at[:, head * E : (head + 1) * E], n.w_v.at[:, lanes]))
    else:
        row_loads = [io.move(n.wkv, n.w_v)]
    row_loads += [io.move(n.media_gain, n.vecs.at[0]), io.move(n.latent_gain, n.vecs.at[1]), io.move(n.out_own, n.out_own_v)]
    row_loads += [io.move(n.media, n.media_v), io.move(n.lat, n.lat_v), io.move(n.dres, n.dres_v)]
    at.greet()

    x_quarters = []
    for dz in range(nz):
        source = n.fall.at[lax.rem(at.z + dz, nz)]
        x_quarters.append(io.put_x(source, n.fall_b.at[quarter(at.group(dz, 0), at.y)]))
    y_quarters = {}
    for dz in range(1, nz):
        source = n.fall.at[lax.rem(at.z + dz, nz)]
        y_quarters[dz, 0] = io.put_y(source, n.fall_b.at[quarter(at.group(dz, 0), at.y)])

    def core_rows(c):
        return pl.ds(pl.multiple_of(c * ny * L, 16), ny * L)

    for dx in range(1, nx):
        for dz in range(nz):
            block = n.fall_b.at[quarter(at.group(dz, nx - dx), at.y)]
            y_quarters[dz, nx - dx] = [io.plan(block, block, at.on_y(d)) for d in range(1, ny)]
    order = [(dz, 0) for dz in range(1, nz)] + [(dz, nx - dx) for dx in range(1, nx) for dz in range(nz)]
    near, count = nz - 1, len(order)
    to_core, fetched = [], []
    for index, (dz, dx) in enumerate(order):
        r = at.group(dz, dx)
        buf = (index + 1) % 2
        copies = [io.plan(n.dall.at[r], n.dall_b.at[r], at.partner())] if nc > 1 else []
        for d in range(ny):
            block = n.fall_b.at[quarter(r, at.y_peer(d))]
            source = n.fall.at[lax.rem(at.z + dz, nz)] if (d == 0 and dx == 0) else block
            copies += [io.plan(source, block, at.partner())] if nc > 1 else []
        to_core.append(copies)
        copies = []
        for c in range(nc):
            rows = core_rows(at.c if c == 0 else nc - 1 - at.c)
            source = n.dall if c == 0 else n.dall_b
            copies.append(io.plan_move(source.at[r], n.dout_v.at[buf, rows]))
        if dx > 0:
            copies.append(io.plan_move(n.fall_b.at[r], n.ffn_v.at[buf]))
        else:
            for slot in range(H):
                head = at.head_of(slot)
                rows = pl.ds(pl.multiple_of((head % nc * ny + head // nc) * L, 16), L)
                source = n.fall.at[lax.rem(at.z + dz, nz)] if slot == 0 else n.fall_b.at[r, rows]
                copies.append(io.plan_move(source, n.ffn_v.at[buf, rows]))
        fetched.append(copies)

    def spread(index):
        arrived(y_quarters[order[index]])
        begin(to_core[index])

    def fetch(index):
        if index < count:
            arrived(to_core[index])
            begin(fetched[index])

    io.moved(*first_loads)
    n.dmixed[...] = mt(n.ffn_v[1], n.wout_v[...]).astype(BF).reshape(G, LR, E)
    own_loads.append(io.move(n.dhid, n.ffn_v.at[1, :, 0:F]))
    span = nx * B
    if E == span:
        tiles = [tm(n.mix_v[z], n.dcols_v[...]) for z in range(nz)]
    else:
        whole = jnp.concatenate([n.mix_v[head] for head in range(H)], axis=-1)
        tiles = [tm(whole[:, z * span : (z + 1) * span], n.dcols_v[...]) for z in range(nz)]
    for z in range(nz):
        for x in range(nx):
            n.p_out[z, x] = tiles[z][x * B : (x + 1) * B].astype(BF)
    out_x = [io.plan(n.p_out.at[at.z, lax.rem(at.x + d, nx)], n.xr_out.at[d - 1], at.on_x(d)) for d in range(1, nx)]
    out_z = [io.put(n.p_out.at[lax.rem(at.z + d, nz)], n.zr_out.at[d - 1], at.on_z(d)) for d in range(1, nz)]

    def out_middle():
        arrived(out_z)
        total = n.p_out[at.z].astype(F32)
        for d in range(1, nz):
            total = total + n.zr_out[d - 1].astype(F32)
        n.p_out[at.z] = total.astype(BF)
        begin(out_x)

    def out_end():
        arrived(out_x)
        total = n.p_out[at.z, at.x].astype(F32)
        for d in range(1, nx):
            total = total + n.xr_out[d - 1].astype(F32)
        n.grad_v[0] = total
        io.move(n.grad_v.at[0], n.out_grad)

    parts = {"kv": (n.p_kv, n.xr_kv, n.zr_kv), "query": (n.p_query, n.xr_query, n.zr_query)}
    x_parts, z_parts = {}, {}
    z_order = list(range(1, nz)) + [0]

    def sum_start(w, rows, grads):
        part, x_recv = parts[w][:2]
        for dz in z_order:
            lanes = pl.ds(pl.multiple_of(lax.rem(at.z + dz, nz) * span, 128), span)
            tile = tm(rows(lanes), grads)
            for x in range(nx):
                part[dz, x] = tile[x * B : (x + 1) * B].astype(BF)
            z_parts[w, dz] = [io.plan(part.at[dz, at.x], parts[w][2].at[dz - 1], at.on_z(dz))] if dz else []
            x_parts[w, dz] = [
                io.put(part.at[dz, lax.rem(at.x + d, nx)], x_recv.at[dz, d - 1], at.on_x(d)) for d in range(1, nx)
            ]

    def sum_middle(w, dz):
        part, x_recv, _ = parts[w]
        arrived(x_parts[w, dz])
        total = part[dz, at.x].astype(F32)
        for d in range(1, nx):
            total = total + x_recv[dz, d - 1].astype(F32)
        part[dz, at.x] = total.astype(BF)
        begin(z_parts[w, dz])

    def sum_end(w, outs):
        part, _, z_recv = parts[w]
        total = part[0, at.x].astype(F32)
        for dz in range(1, nz):
            arrived(z_parts[w, dz])
            total = total + z_recv[dz - 1].astype(F32)
        for j, (ref, out) in enumerate(outs):
            ref[...] = total[:, j * E : (j + 1) * E]
            io.move(ref, out)

    io.moved(*attend_loads)
    mask = head_mask(t.heads_here, LR, E)
    mask_low = mask.astype(BF)
    scale = 1.0 / math.sqrt(HEAD_DIM)
    for i in range(G):
        q = spread_heads(n.query_v[i], mask_low)
        d = spread_heads(n.dmixed[i], mask_low)
        k, v = n.keys_v[i], n.values_v[i]
        probs = softmax(mt(q, k) * scale)
        d_probs = mt(d, v)
        inner = jnp.sum(probs * d_probs, axis=-1, keepdims=True)
        d_scores = (probs * (d_probs - inner)).astype(BF)
        d_query = gather_heads(mm(d_scores, k), mask, LR) * scale
        d_pair = jnp.concatenate([tm(d_scores, q) * scale, tm(probs.astype(BF), d)], axis=-1)
        for slot in range(H):
            rows = slice(slot * ML + i * pr, slot * ML + (i + 1) * pr)
            n.dkv[rows] = d_pair[slot * pr : (slot + 1) * pr].astype(BF)
        for head in range(H):
            rows = slice(H * pr + head * ll, H * pr + (head + 1) * ll)
            n.turn_kv[head, i * ll : (i + 1) * ll] = d_pair[rows]
            n.turn_q[head, i * ll : (i + 1) * ll, 0:E] = d_query[head * ll : (head + 1) * ll]
    if t.EP > E:
        n.turn_q[:, :, E : t.EP] = jnp.zeros((H, L, t.EP - E), F32)
    for slot in range(H):
        head = at.head_of(slot)
        n.dkv[slot * ML + M : (slot + 1) * ML] = n.turn_kv[head].astype(BF)
        n.dq[slot * L : (slot + 1) * L] = n.turn_q[head].astype(BF)
    kv_lanes = pl.ds(pl.multiple_of(at.h * 2 * E, 128), 2 * E)
    q_lanes = pl.ds(pl.multiple_of(at.h * t.EP, 128), t.EP)
    turned = []
    for slot in range(1, H):
        peer = (at.r, at.head_of(slot))
        turned.append(io.put(n.dkv.at[slot * ML : (slot + 1) * ML], n.dkv_full.at[:, kv_lanes], peer))
        turned.append(io.put(n.dq.at[slot * L : (slot + 1) * L], n.dq_full.at[:, q_lanes], peer))
    out_far = [io.put(n.out_send.at[at.y_peer(d)], n.out_recv.at[d - 1], at.on_y(d)) for d in range(1, ny)]
    io.moved(norm_load)
    sum_start("kv", lambda lanes: n.norm_v[:, lanes], n.dkv[...])
    sum_start(
        "query",
        lambda lanes: jnp.concatenate([n.norm_v[slot * ML + M : (slot + 1) * ML, lanes] for slot in range(H)], axis=0),
        n.dq[:, 0:E],
    )
    base, offset = window_of(here, B, D)
    window = pl.ds(base, 256)
    io.moved(*own_loads)
    n.up_acc[...] = tm(n.ffn_v[0, :, window], n.ffn_v[1, :, 0:F])
    n.down_acc[...] = tm(n.dout_v[0, :, window], n.dout_v[1, :, 0:F])
    q_load = io.plan_move(n.wq, n.w_v.at[:, 0 : n.wq.shape[1]])
    media_out, lat_out = io.plan_move(n.drow.at[0:M], n.media_o), io.plan_move(n.drow.at[M:ML], n.lat_o)
    own_out = io.plan_move(n.out_own_v, n.out_o)
    vec_head = [io.plan(n.vec_own, n.vec_head.at[k - 1], (at.r, lax.rem(at.h + k, H))) for k in range(1, H)]
    vec_z = [io.plan(n.vec_sum.at[lax.rem(at.z + d, nz)], n.vec_z.at[d - 1], at.on_z(d)) for d in range(1, nz)]

    def norm_back_rows(raw, size, base, gain_row, extra):
        def step(rows, sums):
            grad_rows = pl.ds(pl.multiple_of(base + rows.start, 16), 16)
            hat, inv = norm_rows(raw[rows].astype(F32))
            grad = n.drow[grad_rows]
            product = grad * hat
            scaled = grad * n.vecs[gain_row : gain_row + 1]
            mean = jnp.mean(scaled, axis=-1, keepdims=True)
            second = jnp.mean(scaled * hat, axis=-1, keepdims=True)
            result = inv * (scaled - mean - hat * second)
            n.drow[grad_rows] = result if extra is None else result + extra[rows]
            return sums[0] + product[:8] + product[8:], sums[1] + grad[:8] + grad[8:]

        sums = sweep(0, size, step, (jnp.zeros((8, D), F32), jnp.zeros((8, D), F32)))
        return [jnp.sum(v, axis=0, keepdims=True) for v in sums]

    def own_gradients():
        n.dkv_full[:, kv_lanes] = n.dkv[0:ML]
        n.dq_full[:, q_lanes] = n.dq[0:L]
        io.moved(*row_loads)
        arrived(turned)
        n.drow[...] = mt(n.dkv_full[...], n.w_v[...])
        begin([q_load])
        n.vec_own[0:1], n.vec_own[1:2] = norm_back_rows(n.media_v, M, 0, 0, None)
        begin([media_out])
        io.moved(q_load)
        n.drow[M:ML] += mt(n.dq_full[...], n.w_v[:, 0 : n.wq.shape[1]])
        n.vec_own[2:3], n.vec_own[3:4] = norm_back_rows(n.lat_v, L, M, 1, n.dres_v)
        begin([lat_out])
        n.vec_own[4:6] = n.fvec[0:2]
        n.vec_own[6:8] = jnp.zeros((2, D), F32)
        begin(vec_head)

    def vectors_middle():
        arrived(vec_head)
        total = n.vec_own[...]
        for k in range(1, H):
            total = total + n.vec_head[k - 1]
        for z in range(nz):
            n.vec_sum[z] = total[:, z * span : (z + 1) * span]
        begin(vec_z)

    def own_output():
        arrived(out_far)
        total = n.out_own_v[...]
        for d in range(1, ny):
            total = total + n.out_recv[d - 1].astype(F32)
        n.out_own_v[...] = total
        begin([own_out])

    before = {index: [lambda index=index: io.moved(*fetched[index]), lambda index=index: fetch(index + 1)] for index in range(count)}
    after = {index: [] for index in range(count)}
    del before[near - 1][1:]

    def late_quarters():
        for dz, dx in order[near:]:
            arrived([x_quarters[dz][nx - dx - 1]])
            begin(y_quarters[dz, dx])

    after[0] += [late_quarters]
    after[near - 1] += [lambda: sum_middle("kv", z_order[0]), out_middle]
    after[near - 1] += [lambda dz=dz: sum_middle("kv", dz) for dz in z_order[1:2]]
    after[near - 1] += [own_gradients]
    after[near - 1] += [lambda dz=dz: sum_middle("kv", dz) for dz in z_order[2:]]
    after[near - 1] += [own_output]
    after[near - 1] += [lambda index=index: spread(index) for index in range(near, count)]
    after[near - 1] += [lambda: fetch(near)]
    late = list(range(near + 1, count)) or [count - 1]
    after[late[0]] += [lambda: sum_middle("query", z_order[0])]
    after[late[min(1, len(late) - 1)]] += [vectors_middle]
    for dz in z_order[1:]:
        after[late[min(dz, len(late) - 1)] if dz else late[-1]] += [lambda dz=dz: sum_middle("query", dz)]
    for index in range(near):
        spread(index)
    fetch(0)
    io.moved(*ffn_loads)

    def at_index(index, actions):
        for k in range(count):
            if actions[k]:

                @pl.when(index == k)
                def _():
                    for action in actions[k]:
                        action()

    def group_step(index, carry):
        at_index(index, before)
        buf = lax.rem(index + 1, 2)
        value, slope = gelu_pair(mm(n.ffn_v[buf], n.wup_v[...]))
        d_hidden = (mt(n.dout_v[buf], n.wdown_v[...]) * slope).astype(BF)
        n.up_acc[...] += tm(n.ffn_v[buf, :, window], d_hidden)
        n.down_acc[...] += tm(n.dout_v[buf, :, window], value.astype(BF))
        at_index(index, after)
        return carry

    lax.fori_loop(0, count, group_step, 0)
    arrived(vec_z)
    total = n.vec_sum[at.z]
    for d in range(1, nz):
        total = total + n.vec_z[d - 1]
    n.vec_part[...] = total
    vec_x = [io.put(n.vec_part, n.vec_x.at[d - 1], at.on_x(d)) for d in range(1, nx)]
    own_rows = pl.ds(pl.multiple_of(offset, 8), B)
    io.move(n.up_acc.at[own_rows], n.up_grad)
    io.move(n.down_acc.at[own_rows], n.down_grad)
    out_end()
    sum_end("kv", [(n.grad_v.at[1], n.key_grad), (n.grad_v.at[2], n.value_grad)])
    arrived(vec_x)
    total = n.vec_part[...]
    for d in range(1, nx):
        total = total + n.vec_x[d - 1]
    n.vec_done[...] = total
    io.move(n.vec_done, n.vec_o)
    sum_end("query", [(n.grad_v.at[3], n.query_grad)])
    io.finish()


def backward(s, ins):
    t = sizes_of(s)
    ny, nc, nz, nx, G, H = t.ny, t.nc, t.nz, t.nx, t.G, t.H
    M, L, LR, GL, ML, D, E, F, B = t.M, t.L, t.LR, t.GL, t.ML, t.D, t.E, t.F, t.B
    fx, fz, fh = max(nx - 1, 1), max(nz - 1, 1), max(H - 1, 1)
    span = D // nz
    outs = dict(
        media_o=((M, D), F32), lat_o=((L, D), F32), query_grad=((B, E), F32), key_grad=((B, E), F32), value_grad=((B, E), F32),
        out_grad=((B, E), F32), up_grad=((B, F), F32), down_grad=((B, F), F32), vec_o=((8, span), F32), out_o=((L, D), F32),
        fall_b=((s.rows, GL, D), BF), dall_b=((s.rows, ny * L, D), BF),
    )
    scratch = dict(
        mix_v=((H, GL, E), BF), wout_v=((E, D), BF), dcols_v=((GL, E), BF), dmixed=((G, LR, E), BF),
        keys_v=((G, t.KC, E), BF), values_v=((G, t.KC, E), BF), query_v=((G, LR, E), BF), norm_v=((H * ML, D), BF),
        ffn_v=((2, GL, D), BF), dout_v=((2, GL, D), BF), wup_v=((D, F), BF),
        wdown_v=((F, D), BF), w_v=((D, max(2 * D, H * t.EP)), BF), media_v=((M, D), BF), lat_v=((L, D), BF), dres_v=((L, D), F32),
        dkv=((H * ML, 2 * E), BF), dq=((H * L, t.EP), BF), turn_kv=((H, L, 2 * E), F32), turn_q=((H, L, t.EP), F32),
        dkv_full=((ML, 2 * D), BF), dq_full=((L, H * t.EP), BF), grad_v=((4, B, E), F32), up_acc=((256, F), F32),
        down_acc=((256, F), F32), drow=((ML, D), F32), vec_own=((8, D), F32), vec_head=((fh, 8, D), F32),
        vec_sum=((nz, 8, span), F32), vec_z=((fz, 8, span), F32), vec_part=((8, span), F32), vec_x=((fx, 8, span), F32),
        vec_done=((8, span), F32), vecs=((8, D), F32), out_own_v=((L, D), F32), out_recv=((max(ny - 1, 1), L, D), BF),
        p_out=((nz, nx, B, E), BF), zr_out=((fz, nx, B, E), BF), xr_out=((fx, B, E), BF),
    )
    for w, lanes in (("kv", 2 * E), ("query", E)):
        scratch["p_" + w] = ((nz, nx, B, lanes), BF)
        scratch["xr_" + w] = ((nz, fx, B, lanes), BF)
        scratch["zr_" + w] = ((fz, B, lanes), BF)
    places = {"fvec": VMEM}
    cost = pl.CostEstimate(flops=30 * 10**9, bytes_accessed=8 * 10**7, transcendentals=10**6)
    return call(backward_kernel, s, "backward", 2, ins, outs, scratch, 300, places, 63, cost)


def finish_kernel(count, *refs):
    ins, outs, held = refs[:count], refs[count : 2 * count], refs[2 * count : 3 * count]
    read, write = refs[3 * count :]
    loads = [pltpu.make_async_copy(a, b, read.at[i]) for i, (a, b) in enumerate(zip(ins, held))]
    stores = [pltpu.make_async_copy(a, b, write.at[i]) for i, (a, b) in enumerate(zip(held, outs))]
    for copy in loads:
        copy.start()
    for load, store in zip(loads, stores):
        load.wait()
        store.start()
    for copy in stores:
        copy.wait()


def finish(arrays):
    count = len(arrays)
    return pl.pallas_call(
        functools.partial(finish_kernel, count),
        name="finish",
        out_shape=[jax.ShapeDtypeStruct(a.shape, a.dtype) for a in arrays],
        in_specs=[ANY] * count,
        out_specs=[ANY] * count,
        scratch_shapes=[pltpu.VMEM(a.shape, a.dtype) for a in arrays] + [pltpu.SemaphoreType.DMA((count,))] * 2,
        compiler_params=pltpu.CompilerParams(vmem_limit_bytes=62 << 20),
    )(*arrays)


def body(
    media, latents, counts, media_gain, media_shift, latent_gain, latent_shift, w_query, w_key, w_value, w_out,
    ffn_gain, ffn_shift, w_up, w_down, cotangent,
):
    rows, heads = lax.axis_size("rows"), lax.axis_size("head")
    at = Place(rows, heads)
    images, patch, width = media.shape
    lat = latents.shape[1]
    cols = width // heads
    s = types.SimpleNamespace(
        rows=rows, heads=heads, images=images, patch=patch, lat=lat, width=width, cols=cols, mine=w_up.shape[1] // heads
    )
    t = sizes_of(s)

    def columns(array):
        return array if t.aligned else lax.dynamic_slice_in_dim(array, at.h * cols, cols, 1)

    gains = dict(
        media_gain=media_gain, media_shift=media_shift, latent_gain=latent_gain, latent_shift=latent_shift,
        ffn_gain=ffn_gain, ffn_shift=ffn_shift,
    )
    rows_in = dict(media=media.reshape(-1, width), lat=latents.reshape(-1, width))
    a = forward(
        s,
        dict(
            rows_in, cot=cotangent.reshape(-1, width), counts=counts, **gains, wq=columns(w_query), wk=columns(w_key),
            wv=columns(w_value), wout=w_out, wup=w_up, wdown=w_down,
        ),
    )
    ins = dict(
        rows_in, media_gain=gains["media_gain"], latent_gain=gains["latent_gain"], fvec=a["fvec_o"], dres=a["dres_o"],
        key_norm=a["key_norm_o"], keys=a["keys_o"], values=a["values_o"], query=a["query_o"], mixed=a["mixed_o"],
        dattn=a["dattn_o"], ffn=a["ffn_o"], dout=a["dout_o"], act=a["act_o"], dhid=a["dhid_o"], dall=a["dall"], fall=a["fall"],
        wout=w_out, wup=w_up, wdown=w_down, out_own=a["out_o"], out_send=a["out_send_o"],
    )
    if t.aligned:
        ins.update(wk=w_key, wv=w_value, wq=w_query)
    else:
        pair = jnp.stack([w_key.reshape(width, heads, cols), w_value.reshape(width, heads, cols)], axis=2)
        padded = jnp.pad(w_query.reshape(width, heads, cols), ((0, 0), (0, 0), (0, t.EP - cols)))
        ins.update(wkv=pair.reshape(width, 2 * width), wq=padded.reshape(width, -1), dattn_cols=columns(a["dattn_o"]))
    b = backward(s, ins)
    share = width // (rows * heads)
    vector = lax.dynamic_slice_in_dim(b["vec_o"], (at.x * heads + at.h) * share, share, 1)
    names = ("out_o", "media_o", "lat_o", "query_grad", "key_grad", "value_grad", "out_grad", "up_grad", "down_grad")
    out, media_grad, latents_grad, query_grad, key_grad, value_grad, out_grad, up_grad, down_grad = finish([b[k] for k in names])
    return (
        out.reshape(latents.shape), media_grad.reshape(media.shape), latents_grad.reshape(latents.shape), vector[0], vector[1],
        vector[2], vector[3], query_grad, key_grad, value_grad, out_grad, vector[4], vector[5], up_grad, down_grad.T,
    )


def solution(mesh):
    row = P("rows", "head", None)
    whole = P()
    vector = P(("rows", "head"))
    grid = P("rows", "head")
    return jax.shard_map(
        body,
        mesh=mesh,
        in_specs=(row, row) + (whole,) * 13 + (row,),
        out_specs=(row, row, row, vector, vector, vector, vector, grid, grid, grid, grid, vector, vector, grid, P("head", "rows")),
        check_vma=False,
    )
```

```python
import functools
import math
import types

import jax
import jax.numpy as jnp
from jax import lax
from jax.experimental import pallas as pl
from jax.experimental.pallas import tpu as pltpu
from jax.sharding import PartitionSpec as P

HEAD_DIM = 96
MAX_IMG = 8
EPSILON = 1e-05
BF = jnp.bfloat16
F32 = jnp.float32
MESH = pl.DeviceIdType.MESH
ANY = pl.BlockSpec(memory_space=pl.ANY)
VMEM = pl.BlockSpec(memory_space=pltpu.VMEM)
SMEM = pl.BlockSpec(memory_space=pltpu.SMEM)


def factor_rows(count):
    nz = 4 if count % 4 == 0 else 1
    return nz, count // nz


def factor_head(count):
    nc = 2 if count % 2 == 0 else 1
    return count // nc, nc


def mm(a, b):
    return lax.dot_general(a, b, (((1,), (0,)), ((), ())), preferred_element_type=F32)


def mt(a, b):
    return lax.dot_general(a, b, (((1,), (1,)), ((), ())), preferred_element_type=F32)


def tm(a, b):
    return lax.dot_general(a, b, (((0,), (0,)), ((), ())), preferred_element_type=F32)


class Place:
    def __init__(self, rows, heads):
        self.rows, self.heads = rows, heads
        self.nz, self.nx = factor_rows(rows)
        self.ny, self.nc = factor_head(heads)
        self.r = lax.axis_index("rows")
        self.h = lax.axis_index("head")
        self.z, self.x = lax.div(self.r, self.nx), lax.rem(self.r, self.nx)
        self.y, self.c = lax.div(self.h, self.nc), lax.rem(self.h, self.nc)
        self.zs, self.xs, self.ys = [
            [self.turn(at, d, size) for d in range(size)]
            for at, size in ((self.z, self.nz), (self.x, self.nx), (self.y, self.ny))
        ]
        self.other = self.nc - 1 - self.c
        self.groups = [[z * self.nx + x for x in self.xs] for z in self.zs]
        self.slots = [y * self.nc + c for y in self.ys for c in (self.c, self.other)[: self.nc]]
        self.partner = (self.r, self.y * self.nc + self.other)

    @staticmethod
    def turn(at, d, size):
        if d == 0:
            return at
        there = at + d
        return jnp.where(there >= size, there - size, there)

    def group(self, dz, dx):
        return self.groups[dz % self.nz][dx % self.nx]

    def on_y(self, d):
        return self.r, self.slots[d * self.nc]

    def on_x(self, d):
        return self.group(0, d), self.h

    def on_z(self, d):
        return self.group(d, 0), self.h

    def greet(self):
        peers = [(self.r, head) for head in self.slots[1:]]
        peers += [self.on_x(d) for d in range(1, self.nx)] + [self.on_z(d) for d in range(1, self.nz)]
        barrier = pltpu.get_barrier_semaphore()
        for peer in peers:
            pl.semaphore_signal(barrier, inc=1, device_id=peer, device_id_type=MESH)
        pl.semaphore_wait(barrier, len(peers))


class Copies:
    def __init__(self, at, send, recv, local):
        self.at, self.send, self.recv, self.local = at, send, recv, local
        self.used, self.used_local = 0, 0
        self.unsent, self.open = [], []

    def plan(self, src, dst, peer):
        copy = pltpu.make_async_remote_copy(
            src_ref=src,
            dst_ref=dst,
            send_sem=self.send.at[self.used],
            recv_sem=self.recv.at[self.used],
            device_id=peer,
            device_id_type=MESH,
        )
        self.used += 1
        self.unsent.append(copy)
        return copy

    def put(self, src, dst, peer):
        copy = self.plan(src, dst, peer)
        copy.start()
        return copy

    def put_y(self, src, dst):
        return [self.put(src, dst, self.at.on_y(d)) for d in range(1, self.at.ny)]

    def put_x(self, src, dst):
        return [self.put(src, dst, self.at.on_x(d)) for d in range(1, self.at.nx)]

    def put_z(self, src, dst):
        return [self.put(src, dst, self.at.on_z(d)) for d in range(1, self.at.nz)]

    def put_core(self, src, dst):
        return [self.put(src, dst, self.at.partner)] if self.at.nc > 1 else []

    def sent(self, copies):
        for copy in copies:
            copy.wait_send()
        self.unsent = [c for c in self.unsent if all(c is not d for d in copies)]

    def plan_move(self, src, dst):
        copy = pltpu.make_async_copy(src, dst, self.local.at[self.used_local])
        self.used_local += 1
        self.open.append(copy)
        return copy

    def move(self, src, dst):
        copy = self.plan_move(src, dst)
        copy.start()
        return copy

    def moved(self, *copies):
        for copy in copies:
            copy.wait()
        self.open = [c for c in self.open if all(c is not d for d in copies)]

    def finish(self):
        for copy in self.unsent:
            copy.wait_send()
        for copy in self.open:
            copy.wait()


def begin(copies):
    for copy in copies:
        copy.start()


def arrived(copies):
    for copy in copies:
        copy.wait_recv()


def norm_rows(block):
    mean = jnp.mean(block, axis=-1, keepdims=True)
    centered = block - mean
    scale = lax.rsqrt(jnp.mean(centered * centered, axis=-1, keepdims=True) + EPSILON)
    return centered * scale, scale


def sweep(first, last, step, carry=0):
    together = next(k for k in (4, 2, 1) if (last - first) // 16 % k == 0)

    def turn(i, value):
        for j in range(together):
            start = first + i * (16 * together) + j * 16
            value = step(pl.ds(pl.multiple_of(start, 16), 16), value)
        return value

    return lax.fori_loop(0, (last - first) // (16 * together), turn, carry)


def gelu_pair(v):
    c = math.sqrt(2.0 / math.pi)
    square = v * v
    t = jnp.tanh(c * v * (1.0 + 0.044715 * square))
    half = 0.5 * (1.0 + t)
    slope = half + 0.5 * v * (1.0 - t * t) * (c * (1.0 + 3.0 * 0.044715 * square))
    return v * half, slope


def softmax(scores):
    powers = jnp.exp(scores - jnp.max(scores, axis=-1, keepdims=True))
    return powers * (1.0 / jnp.sum(powers, axis=-1, keepdims=True))


def head_mask(heads_here, rows, cols):
    col = lax.broadcasted_iota(jnp.int32, (rows, cols), 1)
    return jnp.concatenate(
        [((col >= j * HEAD_DIM) & (col < (j + 1) * HEAD_DIM)).astype(F32) for j in range(heads_here)], axis=0
    )


def spread_heads(block, mask):
    return jnp.concatenate([block] * (mask.shape[0] // block.shape[0]), axis=0) * mask


def gather_heads(block, mask, rows):
    block = block * mask
    return sum(block[j * rows : (j + 1) * rows] for j in range(block.shape[0] // rows))


def sizes_of(s):
    ny, nc = factor_head(s.heads)
    nz, nx = factor_rows(s.rows)
    t = types.SimpleNamespace(ny=ny, nc=nc, nz=nz, nx=nx, G=s.images, D=s.width, E=s.cols, F=s.mine, H=s.heads)
    t.pr, t.ll = s.patch, s.lat
    t.M, t.L, t.LR = t.G * t.pr, t.G * t.ll, t.H * t.ll
    t.GL, t.ML, t.KC = t.G * t.LR, t.M + t.L, t.H * t.pr + t.LR
    t.B = t.D // s.rows
    t.heads_here = t.E // HEAD_DIM
    t.aligned = t.E % 128 == 0
    t.EP = -(-t.E // 128) * 128
    return t


def forward_kernel(s, names, *refs):
    n = types.SimpleNamespace(**dict(zip(names, refs, strict=True)))
    at = Place(s.rows, s.heads)
    t = sizes_of(s)
    ny, nc, nz, nx, G, H = t.ny, t.nc, t.nz, t.nx, t.G, t.H
    M, L, LR, GL, ML, D, E, F, ll, pr = t.M, t.L, t.LR, t.GL, t.ML, t.D, t.E, t.F, t.ll, t.pr
    io = Copies(at, n.send, n.recv, n.local)
    here = at.r

    vectors = ("media_gain", "media_shift", "latent_gain", "latent_shift", "ffn_gain", "ffn_shift")
    load_vecs = [io.move(getattr(n, k), n.vecs.at[i]) for i, k in enumerate(vectors)]
    load_lat = io.move(n.lat, n.raw_l.at[0:L])
    load_cot = io.move(n.cot, n.cot_v)
    load_media = io.move(n.media, n.raw_m.at[0])

    def columns(weight):
        return weight.at[:, pl.ds(pl.multiple_of(at.h * E, 128), E)] if t.aligned else weight

    load_qkv = [io.move(columns(w), v) for w, v in ((n.wk, n.wk_v), (n.wv, n.wv_v), (n.wq, n.wq_v))]
    at.greet()

    chunks = 2
    part = M // chunks

    def far_slot(d):
        return (ny - d) % ny * nc

    def lat_rows(k):
        return n.raw_l.at[k * L : (k + 1) * L]

    lat_far = [io.put(n.lat, lat_rows(far_slot(d)), at.on_y(d)) for d in range(1, ny)]
    lat_near = io.put_core(n.lat, lat_rows(1 % H))
    media_far, media_near = [], []
    for j in range(chunks):
        rows = slice(j * part, (j + 1) * part)
        media_far.append([io.put(n.media.at[rows], n.raw_m.at[far_slot(d), rows], at.on_y(d)) for d in range(1, ny)])
        media_near.append(io.put_core(n.media.at[rows], n.raw_m.at[1 % H, rows]))

    io.moved(load_cot)
    for i in range(G):
        image = here * G + i
        limit = n.counts[lax.div(image, MAX_IMG)]
        live = jnp.where(lax.rem(image, MAX_IMG) < limit, 1.0, 0.0).astype(F32)
        rows = slice(i * ll, (i + 1) * ll)
        n.wide_l[rows] = n.cot_v[rows].astype(F32) * live
    n.dslot[at.y, at.c] = n.wide_l[...].astype(BF)
    own_d = n.dslot.at[at.y, at.c]

    def quarter(r, y):
        return r, pl.ds(pl.multiple_of(y * L, 16), L)

    def across(y, block):
        where = n.dall.at[quarter(here, y)]
        return io.put_z(block, where), io.put_x(block, where)

    z_far, x_far = {}, {}
    z_far[0], x_far[0] = across(at.y, own_d)
    load_out = io.move(n.wout, n.wout_v)
    load_up = io.move(n.wup.at[:, pl.ds(pl.multiple_of(at.h * F, 128), F)], n.wup_v)
    load_down = io.move(n.wdown.at[pl.ds(pl.multiple_of(at.h * F, 16), F)], n.wdown_v)

    def forward_x(d):
        for dz, copy in enumerate(z_far[d], 1):
            copy.wait_recv()
            block = n.dall.at[quarter(at.group(nz - dz, 0), at.ys[d])]
            x_far[d] += io.put_x(block, block)

    norm_busy = {}
    turn_count = [0]

    def patches(k, first, last):
        buf = turn_count[0] % 2
        turn_count[0] += 1
        if buf in norm_busy:
            io.moved(norm_busy[buf])

        def step(rows, carry):
            hat, _ = norm_rows(n.raw_m[k, rows].astype(F32))
            n.norm[buf, rows] = (hat * n.vecs[0:1] + n.vecs[1:2]).astype(BF)
            return carry

        sweep(first * 16, last * 16, step)
        rows = slice(first * 16, last * 16)
        for weight, result in ((n.wk_v, n.keys), (n.wv_v, n.values)):
            wide = mm(n.norm[buf, rows], weight[...]).astype(BF)
            for i in range(first * 16 // pr, last * 16 // pr):
                base = i * pr - first * 16
                result[i, k * pr : (k + 1) * pr] = wide[base : base + pr]
        norm_busy[buf] = io.move(n.norm.at[buf, rows], n.key_norm_o.at[k * ML + first * 16 : k * ML + last * 16])

    io.moved(load_media, *load_qkv, *load_vecs)
    patches(0, 0, M // 16)
    if nc > 1:
        for copies in media_near:
            arrived(copies)
        patches(1, 0, M // 16)
    cot_far = io.put_y(own_d, own_d)
    cot_near = io.put_core(own_d, own_d)
    relay = []
    for d, copy in zip(range(1, ny), lat_far):
        copy.wait_recv()
        k = far_slot(d)
        relay += io.put_core(lat_rows(k), lat_rows(k + 1)) if nc > 1 else []
    io.moved(load_lat)
    arrived(lat_near)
    arrived(relay)
    for k in range(H):
        wide = n.raw_l[k * L : (k + 1) * L].astype(F32)
        for i in range(G):
            n.resid[pl.ds(pl.multiple_of(i * LR + at.slots[k] * ll, 8), ll)] = wide[i * ll : (i + 1) * ll]

    def latent_step(rows, carry):
        hat, _ = norm_rows(n.raw_l[rows].astype(F32))
        n.lnorm[rows] = (hat * n.vecs[2:3] + n.vecs[3:4]).astype(BF)
        return carry

    sweep(0, H * L, latent_step)
    for k in range(H):
        io.move(n.lnorm.at[k * L : (k + 1) * L], n.key_norm_o.at[k * ML + M : (k + 1) * ML])
    for weight, result in ((n.wq_v, n.query), (n.wk_v, n.keys), (n.wv_v, n.values)):
        wide = mm(n.lnorm[...], weight[...])
        for k in range(H):
            for i in range(G):
                n.turn[pl.ds(pl.multiple_of(i * LR + at.slots[k] * ll, 8), ll)] = wide[k * L + i * ll : k * L + (i + 1) * ll]
        for i in range(G):
            block = n.turn[i * LR : (i + 1) * LR].astype(BF)
            if result is n.query:
                result[i] = block
            else:
                result[i, H * pr : t.KC] = block
    media_relay = []
    for j in range(chunks):
        relays = []
        rows = slice(j * part, (j + 1) * part)
        for d, copy in zip(range(1, ny), media_far[j]):
            copy.wait_recv()
            k = far_slot(d)
            relays.append(io.put_core(n.raw_m.at[k, rows], n.raw_m.at[k + 1, rows]) if nc > 1 else [])
        for d in range(1, ny):
            patches(far_slot(d), j * part // 16, (j + 1) * part // 16)
        for d in range(1, ny):
            if nc > 1:
                arrived(relays[d - 1])
                patches(far_slot(d) + 1, j * part // 16, (j + 1) * part // 16)
    arrived(cot_far)
    cot_relay = []
    for d in range(1, ny):
        block = n.dslot.at[at.ys[d], at.c]
        cot_relay += io.put_core(block, block)
        z_far[d], x_far[d] = across(at.ys[d], block)
    forward_x(0)
    mask = head_mask(t.heads_here, LR, E)
    mask_low = mask.astype(BF)
    scale = 1.0 / math.sqrt(HEAD_DIM)
    for i in range(G):
        scores = mt(spread_heads(n.query[i], mask_low), n.keys[i]) * scale
        probs = softmax(scores).astype(BF)
        mixed = gather_heads(mm(probs, n.values[i]), mask, LR)
        n.mix[at.h, i * LR : (i + 1) * LR] = mixed.astype(BF)
    mix_far = io.put_y(n.mix.at[at.h], n.mix.at[at.h])
    mix_near = io.put_core(n.mix.at[at.h], n.mix.at[at.h])
    for ref, out in ((n.keys, n.keys_o), (n.values, n.values_o), (n.query, n.query_o)):
        io.move(ref, out)
    io.moved(load_out, load_up, load_down)

    def add_mixed(head):
        n.resid[...] += mm(n.mix[head], n.wout_v[pl.ds(pl.multiple_of(head * E, 16), E)])

    add_mixed(at.h)
    arrived(mix_near)
    if nc > 1:
        add_mixed(at.slots[1])
    arrived(cot_near)
    arrived(cot_relay)
    for y in range(ny):
        for c in range(nc):
            wide = n.dslot[y, c].astype(F32)
            for i in range(G):
                n.part[i * LR + (y * nc + c) * ll : i * LR + (y * nc + c + 1) * ll] = wide[i * ll : (i + 1) * ll]
    n.dout[...] = n.part[...].astype(BF)
    io.move(n.dout, n.dout_o)
    mix_relay = []
    for d, copy in zip(range(1, ny), mix_far):
        copy.wait_recv()
        block = n.mix.at[at.slots[far_slot(d)]]
        mix_relay.append(io.put_core(block, block))
    for d in range(1, ny):
        add_mixed(at.slots[far_slot(d)])
    for d in range(1, ny):
        if nc > 1:
            arrived(mix_relay[d - 1])
            add_mixed(at.slots[far_slot(d) + 1])
    io.move(n.mix, n.mixed_o)
    gain, shift = n.vecs[4:5], n.vecs[5:6]

    def ffn_step(rows, carry):
        hat, inv = norm_rows(n.resid[rows])
        n.hat[rows] = hat
        n.inv[rows] = jnp.broadcast_to(inv, (16, 128))
        n.ffn[rows] = (hat * n.vecs[4:5] + n.vecs[5:6]).astype(BF)
        return carry

    sweep(0, GL, ffn_step)
    io.move(n.ffn, n.ffn_o)

    def own_rows(ref):
        return jnp.concatenate([ref[pl.ds(pl.multiple_of(i * LR + at.h * ll, 8), ll)] for i in range(G)], axis=0)

    n.fq[...] = (own_rows(n.hat) * gain + shift).astype(BF)
    own_f = n.fall.at[at.z]
    ffn_far = io.put_z(n.fq, own_f)
    io.move(n.fq, own_f)
    value, slope = gelu_pair(mm(n.ffn[...], n.wup_v[...]))
    n.act[...] = value.astype(BF)
    n.dhid[...] = (mt(n.dout[...], n.wdown_v[...]) * slope).astype(BF)
    n.part[...] = mt(n.dhid[...], n.wup_v[...])
    half = GL // nc
    theirs = pl.ds(pl.multiple_of((nc - 1 - at.c) * half, 16), half)
    swap = io.put_core(n.part.at[theirs], n.c_recv)
    io.move(n.act, n.act_o)
    io.move(n.dhid, n.dhid_o)
    out_part = mm(n.act[...], n.wdown_v[...])
    for i in range(G):
        for head in range(H):
            base = i * LR + head * ll
            n.outp[head % nc, head // nc, i * ll : (i + 1) * ll] = out_part[base : base + ll]
    out_swap = io.put_core(n.outp.at[nc - 1 - at.c], n.oc_recv)
    arrived(swap)
    pieces = 2
    piece = half // pieces
    sum_far = []
    for j in range(pieces):
        rows = slice(j * piece, (j + 1) * piece)
        total = n.part[pl.ds(pl.multiple_of(at.c * half + j * piece, 16), piece)]
        if nc > 1:
            total = total + n.c_recv[rows]
        n.y_send[rows] = total.astype(BF)
        sum_far.append([io.put(n.y_send.at[rows], n.y_recv.at[d - 1, rows], at.on_y(d)) for d in range(1, ny)])
    arrived(out_swap)
    for y in range(ny):
        total = n.outp[at.c, y]
        if nc > 1:
            total = total + n.oc_recv[y]
        n.outp[at.c, y] = total
        n.oy_send[y] = total.astype(BF)
    for d in range(1, ny):
        forward_x(d)
    io.sent(swap)

    def residual_back(ref, base, first, last):
        def step(from_rows, carry):
            rows = pl.ds(pl.multiple_of(base + from_rows.start, 16), 16)
            grad = ref[from_rows]
            hat, inv = n.hat[rows], n.inv[rows, 0:1]
            n.part[rows] = grad
            scaled = grad * n.vecs[4:5]
            first = jnp.mean(scaled, axis=-1, keepdims=True)
            second = jnp.mean(scaled * hat, axis=-1, keepdims=True)
            d_res = n.dout[rows].astype(F32) + inv * (scaled - first - hat * second)
            n.resid[rows] = d_res
            n.dattn[rows] = d_res.astype(BF)
            return carry

        sweep(first, last, step)

    n.own[0] = n.outp[at.c, at.y] + own_rows(n.resid)
    io.move(n.own.at[0], n.out_o)
    io.move(n.oy_send, n.out_send_o)
    share = []
    for j in range(pieces):
        rows = slice(j * piece, (j + 1) * piece)
        arrived(sum_far[j])
        total = n.y_send[rows].astype(F32)
        for d in range(1, ny):
            total = total + n.y_recv[d - 1, rows].astype(F32)
        n.share[rows] = total
        share.append(io.put_core(n.share.at[rows], n.s_recv.at[rows]))
        residual_back(n.share, at.c * half, j * piece, (j + 1) * piece)
    if nc > 1:
        for j in range(pieces):
            arrived(share[j])
            residual_back(n.s_recv, (nc - 1 - at.c) * half, j * piece, (j + 1) * piece)
    io.move(n.dattn, n.dattn_o)
    n.own[1] = own_rows(n.resid)
    io.move(n.own.at[1], n.dres_o)
    grad = own_rows(n.part)
    n.fvec[0:1] = jnp.sum(grad * own_rows(n.hat), axis=0, keepdims=True)
    n.fvec[1:2] = jnp.sum(grad, axis=0, keepdims=True)
    n.fvec[2:8] = jnp.zeros((6, D), F32)
    io.move(n.fvec, n.fvec_o)
    for d in range(ny):
        arrived(x_far[d])
    arrived(ffn_far)
    io.finish()


def call(kernel, s, name, ident, ins, outs, scratch, semaphores, places, limit, cost):
    names = list(ins) + list(outs) + list(scratch) + ["send", "recv", "local"]
    dma = [pltpu.SemaphoreType.DMA((count,)) for count in (semaphores, semaphores, 120)]
    result = pl.pallas_call(
        functools.partial(kernel, s, names),
        name=name,
        out_shape=[jax.ShapeDtypeStruct(*o) for o in outs.values()],
        in_specs=[places.get(k, ANY) for k in ins],
        out_specs=[ANY] * len(outs),
        scratch_shapes=[pltpu.VMEM(*v) for v in scratch.values()] + dma,
        compiler_params=pltpu.CompilerParams(collective_id=ident, has_side_effects=True, vmem_limit_bytes=limit << 20),
        cost_estimate=cost,
    )(*ins.values())
    return dict(zip(outs, result, strict=True))


def forward(s, ins):
    t = sizes_of(s)
    ny, nc, G, H, M, L, LR, GL, ML, D, E, F = t.ny, t.nc, t.G, t.H, t.M, t.L, t.LR, t.GL, t.ML, t.D, t.E, t.F
    half = GL // nc
    far = max(ny - 1, 1)
    outs = dict(
        out_o=((L, D), F32), dres_o=((L, D), F32), fvec_o=((8, D), F32), key_norm_o=((H * ML, D), BF),
        keys_o=((G, t.KC, E), BF), values_o=((G, t.KC, E), BF), query_o=((G, LR, E), BF), mixed_o=((H, GL, E), BF),
        dattn_o=((GL, D), BF), ffn_o=((GL, D), BF), dout_o=((GL, D), BF), act_o=((GL, F), BF), dhid_o=((GL, F), BF),
        dall=((s.rows, ny * L, D), BF), fall=((t.nz, L, D), BF), out_send_o=((ny, L, D), BF),
    )
    scratch = dict(
        vecs=((8, D), F32), cot_v=((L, D), BF), wide_l=((L, D), F32), raw_m=((H, M, D), BF), raw_l=((H * L, D), BF), dslot=((ny, nc, L, D), BF),
        norm=((2, M, D), BF), lnorm=((H * L, D), BF), turn=((GL, E), F32), keys=((G, t.KC, E), BF), values=((G, t.KC, E), BF),
        query=((G, LR, E), BF), mix=((H, GL, E), BF), resid=((GL, D), F32), hat=((GL, D), F32), inv=((GL, 128), F32),
        ffn=((GL, D), BF), dout=((GL, D), BF), act=((GL, F), BF), dhid=((GL, F), BF), part=((GL, D), F32),
        outp=((nc, ny, L, D), F32), c_recv=((half, D), F32), oc_recv=((ny, L, D), F32), y_send=((half, D), BF),
        y_recv=((far, half, D), BF), oy_send=((ny, L, D), BF), share=((half, D), F32),
        s_recv=((half, D), F32), fq=((L, D), BF), own=((2, L, D), F32), dattn=((GL, D), BF),
        fvec=((8, D), F32), wq_v=((D, E), BF), wk_v=((D, E), BF), wv_v=((D, E), BF), wout_v=((D, D), BF),
        wup_v=((D, F), BF), wdown_v=((F, D), BF),
    )
    places = {"counts": SMEM}
    cost = pl.CostEstimate(flops=8 * 10**9, bytes_accessed=4 * 10**7, transcendentals=10**6)
    return call(forward_kernel, s, "forward", 1, ins, outs, scratch, 200, places, 62, cost)


def window_of(position, block, width):
    base = jnp.minimum(position * block // 128 * 128, width - 256)
    return pl.multiple_of(base, 128), position * block - base


def backward_kernel(s, names, *refs):
    n = types.SimpleNamespace(**dict(zip(names, refs, strict=True)))
    at = Place(s.rows, s.heads)
    t = sizes_of(s)
    ny, nc, nz, nx, G, H = t.ny, t.nc, t.nz, t.nx, t.G, t.H
    M, L, LR, GL, ML, D, E, F, ll, pr, B = t.M, t.L, t.LR, t.GL, t.ML, t.D, t.E, t.F, t.ll, t.pr, t.B
    here = at.r
    io = Copies(at, n.send, n.recv, n.local)

    def quarter(r, y):
        return r, pl.ds(pl.multiple_of((at.c * ny + y) * L, 16), L)

    aligned = t.aligned
    first_loads = [io.move(n.dattn, n.ffn_v.at[1]), io.move(n.mixed, n.mix_v)]
    first_loads.append(io.move(n.wout.at[pl.ds(pl.multiple_of(at.h * E, 16), E)], n.wout_v))
    if aligned:
        first_loads.append(io.move(n.dattn.at[:, pl.ds(pl.multiple_of(at.h * E, 128), E)], n.dcols_v))
    else:
        first_loads.append(io.move(n.dattn_cols, n.dcols_v))
    attend_loads = [io.move(getattr(n, k), getattr(n, k + "_v")) for k in ("keys", "values", "query")]
    norm_load = io.move(n.key_norm, n.norm_v)
    own_loads = [io.move(n.act, n.dout_v.at[1, :, 0:F]), io.move(n.ffn, n.ffn_v.at[0]), io.move(n.dout, n.dout_v.at[0])]
    ffn_loads = [io.move(n.wup.at[:, pl.ds(pl.multiple_of(at.h * F, 128), F)], n.wup_v)]
    ffn_loads.append(io.move(n.wdown.at[pl.ds(pl.multiple_of(at.h * F, 16), F)], n.wdown_v))
    if aligned:
        row_loads = []
        for head in range(H):
            for j, weight in enumerate((n.wk, n.wv)):
                lanes = slice((2 * head + j) * E, (2 * head + j + 1) * E)
                row_loads.append(io.move(weight.at[:, head * E : (head + 1) * E], n.w_v.at[:, lanes]))
    else:
        row_loads = [io.move(n.wkv, n.w_v)]
    row_loads += [io.move(n.media_gain, n.vecs.at[0]), io.move(n.latent_gain, n.vecs.at[1]), io.move(n.out_own, n.out_own_v)]
    row_loads += [io.move(n.media, n.media_v), io.move(n.lat, n.lat_v), io.move(n.dres, n.dres_v)]
    at.greet()

    x_quarters = []
    for dz in range(nz):
        source = n.fall.at[at.zs[dz]]
        x_quarters.append(io.put_x(source, n.fall_b.at[quarter(at.group(dz, 0), at.y)]))
    y_quarters = {}
    for dz in range(1, nz):
        source = n.fall.at[at.zs[dz]]
        y_quarters[dz, 0] = io.put_y(source, n.fall_b.at[quarter(at.group(dz, 0), at.y)])

    def core_rows(c):
        return pl.ds(pl.multiple_of(c * ny * L, 16), ny * L)

    for dx in range(1, nx):
        for dz in range(nz):
            block = n.fall_b.at[quarter(at.group(dz, nx - dx), at.y)]
            y_quarters[dz, nx - dx] = [io.plan(block, block, at.on_y(d)) for d in range(1, ny)]
    order = [(dz, 0) for dz in range(1, nz)] + [(dz, nx - dx) for dx in range(1, nx) for dz in range(nz)]
    near, count = nz - 1, len(order)
    to_core, fetched = [], []
    for index, (dz, dx) in enumerate(order):
        r = at.group(dz, dx)
        buf = (index + 1) % 2
        copies = [io.plan(n.dall.at[r], n.dall_b.at[r], at.partner)] if nc > 1 else []
        for d in range(ny):
            block = n.fall_b.at[quarter(r, at.ys[d])]
            source = n.fall.at[at.zs[dz]] if (d == 0 and dx == 0) else block
            copies += [io.plan(source, block, at.partner)] if nc > 1 else []
        to_core.append(copies)
        copies = []
        for c in range(nc):
            rows = core_rows(at.c if c == 0 else nc - 1 - at.c)
            source = n.dall if c == 0 else n.dall_b
            copies.append(io.plan_move(source.at[r], n.dout_v.at[buf, rows]))
        if dx > 0:
            copies.append(io.plan_move(n.fall_b.at[r], n.ffn_v.at[buf]))
        else:
            for slot in range(H):
                core = at.c if slot % nc == 0 else at.other
                rows = pl.ds(pl.multiple_of((core * ny + at.ys[slot // nc]) * L, 16), L)
                source = n.fall.at[at.zs[dz]] if slot == 0 else n.fall_b.at[r, rows]
                copies.append(io.plan_move(source, n.ffn_v.at[buf, rows]))
        fetched.append(copies)

    def spread(index):
        arrived(y_quarters[order[index]])
        begin(to_core[index])

    def fetch(index):
        if index < count:
            arrived(to_core[index])
            begin(fetched[index])

    io.moved(*first_loads)
    n.dmixed[...] = mt(n.ffn_v[1], n.wout_v[...]).astype(BF).reshape(G, LR, E)
    own_loads.append(io.move(n.dhid, n.ffn_v.at[1, :, 0:F]))
    span = nx * B
    if E == span:
        tiles = [tm(n.mix_v[z], n.dcols_v[...]) for z in range(nz)]
    else:
        whole = jnp.concatenate([n.mix_v[head] for head in range(H)], axis=-1)
        tiles = [tm(whole[:, z * span : (z + 1) * span], n.dcols_v[...]) for z in range(nz)]
    for z in range(nz):
        for x in range(nx):
            n.p_out[z, x] = tiles[z][x * B : (x + 1) * B].astype(BF)
    out_x = [io.plan(n.p_out.at[at.z, at.xs[d]], n.xr_out.at[d - 1], at.on_x(d)) for d in range(1, nx)]
    out_z = [io.put(n.p_out.at[at.zs[d]], n.zr_out.at[d - 1], at.on_z(d)) for d in range(1, nz)]

    def out_middle():
        arrived(out_z)
        total = n.p_out[at.z].astype(F32)
        for d in range(1, nz):
            total = total + n.zr_out[d - 1].astype(F32)
        n.p_out[at.z] = total.astype(BF)
        begin(out_x)

    def out_end():
        arrived(out_x)
        total = n.p_out[at.z, at.x].astype(F32)
        for d in range(1, nx):
            total = total + n.xr_out[d - 1].astype(F32)
        n.grad_v[0] = total
        io.move(n.grad_v.at[0], n.out_grad)

    parts = {"kv": (n.p_kv, n.xr_kv, n.zr_kv), "query": (n.p_query, n.xr_query, n.zr_query)}
    x_parts, z_parts = {}, {}
    z_order = list(range(1, nz)) + [0]

    def sum_start(w, rows, grads):
        part, x_recv = parts[w][:2]
        for dz in z_order:
            lanes = pl.ds(pl.multiple_of(at.zs[dz] * span, 128), span)
            tile = tm(rows(lanes), grads)
            for x in range(nx):
                part[dz, x] = tile[x * B : (x + 1) * B].astype(BF)
            z_parts[w, dz] = [io.plan(part.at[dz, at.x], parts[w][2].at[dz - 1], at.on_z(dz))] if dz else []
            x_parts[w, dz] = [
                io.put(part.at[dz, at.xs[d]], x_recv.at[dz, d - 1], at.on_x(d)) for d in range(1, nx)
            ]

    def sum_middle(w, dz):
        part, x_recv, _ = parts[w]
        arrived(x_parts[w, dz])
        total = part[dz, at.x].astype(F32)
        for d in range(1, nx):
            total = total + x_recv[dz, d - 1].astype(F32)
        part[dz, at.x] = total.astype(BF)
        begin(z_parts[w, dz])

    def sum_end(w, outs):
        part, _, z_recv = parts[w]
        total = part[0, at.x].astype(F32)
        for dz in range(1, nz):
            arrived(z_parts[w, dz])
            total = total + z_recv[dz - 1].astype(F32)
        for j, (ref, out) in enumerate(outs):
            ref[...] = total[:, j * E : (j + 1) * E]
            io.move(ref, out)

    io.moved(*attend_loads)
    mask = head_mask(t.heads_here, LR, E)
    mask_low = mask.astype(BF)
    scale = 1.0 / math.sqrt(HEAD_DIM)
    for i in range(G):
        q = spread_heads(n.query_v[i], mask_low)
        d = spread_heads(n.dmixed[i], mask_low)
        k, v = n.keys_v[i], n.values_v[i]
        probs = softmax(mt(q, k) * scale)
        d_probs = mt(d, v)
        inner = jnp.sum(probs * d_probs, axis=-1, keepdims=True)
        d_scores = (probs * (d_probs - inner)).astype(BF)
        d_query = gather_heads(mm(d_scores, k), mask, LR) * scale
        d_pair = jnp.concatenate([tm(d_scores, q) * scale, tm(probs.astype(BF), d)], axis=-1)
        for slot in range(H):
            rows = slice(slot * ML + i * pr, slot * ML + (i + 1) * pr)
            n.dkv[rows] = d_pair[slot * pr : (slot + 1) * pr].astype(BF)
        for head in range(H):
            rows = slice(H * pr + head * ll, H * pr + (head + 1) * ll)
            n.turn_kv[head, i * ll : (i + 1) * ll] = d_pair[rows]
            n.turn_q[head, i * ll : (i + 1) * ll, 0:E] = d_query[head * ll : (head + 1) * ll]
    if t.EP > E:
        n.turn_q[:, :, E : t.EP] = jnp.zeros((H, L, t.EP - E), F32)
    for slot in range(H):
        head = at.slots[slot]
        n.dkv[slot * ML + M : (slot + 1) * ML] = n.turn_kv[head].astype(BF)
        n.dq[slot * L : (slot + 1) * L] = n.turn_q[head].astype(BF)
    kv_lanes = pl.ds(pl.multiple_of(at.h * 2 * E, 128), 2 * E)
    q_lanes = pl.ds(pl.multiple_of(at.h * t.EP, 128), t.EP)
    turned = []
    for slot in range(1, H):
        peer = (at.r, at.slots[slot])
        turned.append(io.put(n.dkv.at[slot * ML : (slot + 1) * ML], n.dkv_full.at[:, kv_lanes], peer))
        turned.append(io.put(n.dq.at[slot * L : (slot + 1) * L], n.dq_full.at[:, q_lanes], peer))
    out_far = [io.plan(n.out_send.at[at.ys[d]], n.out_recv.at[d - 1], at.on_y(d)) for d in range(1, ny)]
    io.moved(norm_load)
    sum_start("kv", lambda lanes: n.norm_v[:, lanes], n.dkv[...])
    sum_start(
        "query",
        lambda lanes: jnp.concatenate([n.norm_v[slot * ML + M : (slot + 1) * ML, lanes] for slot in range(H)], axis=0),
        n.dq[:, 0:E],
    )
    base, offset = window_of(here, B, D)
    window = pl.ds(base, 256)
    io.moved(*own_loads)
    n.up_acc[...] = tm(n.ffn_v[0, :, window], n.ffn_v[1, :, 0:F])
    n.down_acc[...] = tm(n.dout_v[0, :, window], n.dout_v[1, :, 0:F])
    q_load = io.plan_move(n.wq, n.w_v.at[:, 0 : n.wq.shape[1]])
    media_out, lat_out = io.plan_move(n.drow.at[0:M], n.media_o), io.plan_move(n.drow.at[M:ML], n.lat_o)
    own_out = io.plan_move(n.out_own_v, n.out_o)
    vec_z = [io.plan(n.vec_sum.at[at.zs[d]], n.vec_z.at[d - 1], at.on_z(d)) for d in range(1, nz)]

    def back_slot(k):
        return (ny - k // nc) % ny * nc + k % nc

    vec_head = [io.plan(n.vec_own, n.vec_head.at[back_slot(k) - 1], (at.r, at.slots[k])) for k in range(1, H)]

    def norm_back_rows(raw, size, base, gain_row, extra):
        def step(rows, sums):
            grad_rows = pl.ds(pl.multiple_of(base + rows.start, 16), 16)
            hat, inv = norm_rows(raw[rows].astype(F32))
            grad = n.drow[grad_rows]
            product = grad * hat
            scaled = grad * n.vecs[gain_row : gain_row + 1]
            mean = jnp.mean(scaled, axis=-1, keepdims=True)
            second = jnp.mean(scaled * hat, axis=-1, keepdims=True)
            result = inv * (scaled - mean - hat * second)
            n.drow[grad_rows] = result if extra is None else result + extra[rows]
            return sums[0] + product[:8] + product[8:], sums[1] + grad[:8] + grad[8:]

        sums = sweep(0, size, step, (jnp.zeros((8, D), F32), jnp.zeros((8, D), F32)))
        return [jnp.sum(v, axis=0, keepdims=True) for v in sums]

    def own_gradients():
        n.dkv_full[:, kv_lanes] = n.dkv[0:ML]
        n.dq_full[:, q_lanes] = n.dq[0:L]
        io.moved(*row_loads)
        arrived(turned)
        n.drow[...] = mt(n.dkv_full[...], n.w_v[...])
        begin([q_load])
        n.vec_own[0:1], n.vec_own[1:2] = norm_back_rows(n.media_v, M, 0, 0, None)
        begin([media_out])
        io.moved(q_load)
        n.drow[M:ML] += mt(n.dq_full[...], n.w_v[:, 0 : n.wq.shape[1]])
        n.vec_own[2:3], n.vec_own[3:4] = norm_back_rows(n.lat_v, L, M, 1, n.dres_v)
        begin([lat_out])
        n.vec_own[4:6] = n.fvec[0:2]
        n.vec_own[6:8] = jnp.zeros((2, D), F32)
        begin(vec_head)
        begin(out_far)

    def vectors_middle():
        arrived(vec_head)
        total = n.vec_own[...]
        for k in range(1, H):
            total = total + n.vec_head[k - 1]
        for z in range(nz):
            n.vec_sum[z] = total[:, z * span : (z + 1) * span]
        begin(vec_z)

    def own_output():
        arrived(out_far)
        total = n.out_own_v[...]
        for d in range(1, ny):
            total = total + n.out_recv[d - 1].astype(F32)
        n.out_own_v[...] = total
        begin([own_out])

    before, middle, after = [{index: [] for index in range(count)} for _ in range(3)]

    def late_quarters():
        for dz, dx in order[near:]:
            arrived([x_quarters[dz][nx - dx - 1]])
            begin(y_quarters[dz, dx])

    for index in range(count):
        before[index] += [lambda index=index: io.moved(*fetched[index])]
        if index + 1 < count and index != near - 1:
            before[index] += [lambda index=index: spread(index + 1)]
            middle[index] += [lambda index=index: fetch(index + 1)]
    middle[0] += [late_quarters]
    after[near - 1] += [lambda: sum_middle("kv", z_order[0]), out_middle]
    after[near - 1] += [lambda dz=dz: sum_middle("kv", dz) for dz in z_order[1:2]]
    after[near - 1] += [own_gradients]
    after[near - 1] += [lambda dz=dz: sum_middle("kv", dz) for dz in z_order[2:]]
    after[near - 1] += [lambda: spread(near), lambda: fetch(near)]
    late = list(range(near, count))
    after[late[min(1, len(late) - 1)]] += [vectors_middle]
    for position, dz in enumerate(z_order):
        after[late[min(position + 1, len(late) - 1)]] += [lambda dz=dz: sum_middle("query", dz)]
    after[late[-1]] += [own_output]
    spread(0)
    fetch(0)
    io.moved(*ffn_loads)

    def at_index(index, actions):
        for k in range(count):
            if actions[k]:

                @pl.when(index == k)
                def _():
                    for action in actions[k]:
                        action()

    def group_step(index, carry):
        at_index(index, before)
        buf = lax.rem(index + 1, 2)
        value, slope = gelu_pair(mm(n.ffn_v[buf], n.wup_v[...]))
        n.down_acc[...] += tm(n.dout_v[buf, :, window], value.astype(BF))
        n.slope[...] = slope
        at_index(index, middle)
        d_hidden = (mt(n.dout_v[buf], n.wdown_v[...]) * n.slope[...]).astype(BF)
        n.up_acc[...] += tm(n.ffn_v[buf, :, window], d_hidden)
        at_index(index, after)
        return carry

    lax.fori_loop(0, count, group_step, 0)
    arrived(vec_z)
    total = n.vec_sum[at.z]
    for d in range(1, nz):
        total = total + n.vec_z[d - 1]
    n.vec_part[...] = total
    vec_x = [io.put(n.vec_part, n.vec_x.at[d - 1], at.on_x(d)) for d in range(1, nx)]
    own_rows = pl.ds(pl.multiple_of(offset, 8), B)
    io.move(n.up_acc.at[own_rows], n.up_grad)
    io.move(n.down_acc.at[own_rows], n.down_grad)
    out_end()
    sum_end("kv", [(n.grad_v.at[1], n.key_grad), (n.grad_v.at[2], n.value_grad)])
    arrived(vec_x)
    total = n.vec_part[...]
    for d in range(1, nx):
        total = total + n.vec_x[d - 1]
    n.vec_done[...] = total
    io.move(n.vec_done, n.vec_o)
    sum_end("query", [(n.grad_v.at[3], n.query_grad)])
    io.finish()


def backward(s, ins):
    t = sizes_of(s)
    ny, nc, nz, nx, G, H = t.ny, t.nc, t.nz, t.nx, t.G, t.H
    M, L, LR, GL, ML, D, E, F, B = t.M, t.L, t.LR, t.GL, t.ML, t.D, t.E, t.F, t.B
    fx, fz, fh = max(nx - 1, 1), max(nz - 1, 1), max(H - 1, 1)
    span = D // nz
    outs = dict(
        media_o=((M, D), F32), lat_o=((L, D), F32), query_grad=((B, E), F32), key_grad=((B, E), F32), value_grad=((B, E), F32),
        out_grad=((B, E), F32), up_grad=((B, F), F32), down_grad=((B, F), F32), vec_o=((8, span), F32), out_o=((L, D), F32),
        fall_b=((s.rows, GL, D), BF), dall_b=((s.rows, ny * L, D), BF),
    )
    scratch = dict(
        mix_v=((H, GL, E), BF), wout_v=((E, D), BF), dcols_v=((GL, E), BF), dmixed=((G, LR, E), BF),
        keys_v=((G, t.KC, E), BF), values_v=((G, t.KC, E), BF), query_v=((G, LR, E), BF), norm_v=((H * ML, D), BF),
        ffn_v=((2, GL, D), BF), dout_v=((2, GL, D), BF), wup_v=((D, F), BF),
        wdown_v=((F, D), BF), w_v=((D, max(2 * D, H * t.EP)), BF), media_v=((M, D), BF), lat_v=((L, D), BF), dres_v=((L, D), F32),
        dkv=((H * ML, 2 * E), BF), dq=((H * L, t.EP), BF), turn_kv=((H, L, 2 * E), F32), turn_q=((H, L, t.EP), F32),
        dkv_full=((ML, 2 * D), BF), dq_full=((L, H * t.EP), BF), grad_v=((4, B, E), F32), up_acc=((256, F), F32),
        down_acc=((256, F), F32), drow=((ML, D), F32), slope=((GL, F), F32), vec_own=((8, D), F32), vec_head=((fh, 8, D), F32),
        vec_sum=((nz, 8, span), F32), vec_z=((fz, 8, span), F32), vec_part=((8, span), F32), vec_x=((fx, 8, span), F32),
        vec_done=((8, span), F32), vecs=((8, D), F32), out_own_v=((L, D), F32), out_recv=((max(ny - 1, 1), L, D), BF),
        p_out=((nz, nx, B, E), BF), zr_out=((fz, nx, B, E), BF), xr_out=((fx, B, E), BF),
    )
    for w, lanes in (("kv", 2 * E), ("query", E)):
        scratch["p_" + w] = ((nz, nx, B, lanes), BF)
        scratch["xr_" + w] = ((nz, fx, B, lanes), BF)
        scratch["zr_" + w] = ((fz, B, lanes), BF)
    places = {"fvec": VMEM}
    cost = pl.CostEstimate(flops=30 * 10**9, bytes_accessed=8 * 10**7, transcendentals=10**6)
    return call(backward_kernel, s, "backward", 2, ins, outs, scratch, 300, places, 63, cost)


def finish_kernel(count, *refs):
    ins, outs, held = refs[:count], refs[count : 2 * count], refs[2 * count : 3 * count]
    read, write = refs[3 * count :]
    loads = [pltpu.make_async_copy(a, b, read.at[i]) for i, (a, b) in enumerate(zip(ins, held))]
    stores = [pltpu.make_async_copy(a, b, write.at[i]) for i, (a, b) in enumerate(zip(held, outs))]
    for copy in loads:
        copy.start()
    for load, store in zip(loads, stores):
        load.wait()
        store.start()
    for copy in stores:
        copy.wait()


def finish(arrays):
    count = len(arrays)
    return pl.pallas_call(
        functools.partial(finish_kernel, count),
        name="finish",
        out_shape=[jax.ShapeDtypeStruct(a.shape, a.dtype) for a in arrays],
        in_specs=[ANY] * count,
        out_specs=[ANY] * count,
        scratch_shapes=[pltpu.VMEM(a.shape, a.dtype) for a in arrays] + [pltpu.SemaphoreType.DMA((count,))] * 2,
        compiler_params=pltpu.CompilerParams(vmem_limit_bytes=62 << 20),
    )(*arrays)


def body(
    media, latents, counts, media_gain, media_shift, latent_gain, latent_shift, w_query, w_key, w_value, w_out,
    ffn_gain, ffn_shift, w_up, w_down, cotangent,
):
    rows, heads = lax.axis_size("rows"), lax.axis_size("head")
    at = Place(rows, heads)
    images, patch, width = media.shape
    lat = latents.shape[1]
    cols = width // heads
    s = types.SimpleNamespace(
        rows=rows, heads=heads, images=images, patch=patch, lat=lat, width=width, cols=cols, mine=w_up.shape[1] // heads
    )
    t = sizes_of(s)

    def columns(array):
        return array if t.aligned else lax.dynamic_slice_in_dim(array, at.h * cols, cols, 1)

    gains = dict(
        media_gain=media_gain, media_shift=media_shift, latent_gain=latent_gain, latent_shift=latent_shift,
        ffn_gain=ffn_gain, ffn_shift=ffn_shift,
    )
    rows_in = dict(media=media.reshape(-1, width), lat=latents.reshape(-1, width))
    a = forward(
        s,
        dict(
            rows_in, cot=cotangent.reshape(-1, width), counts=counts, **gains, wq=columns(w_query), wk=columns(w_key),
            wv=columns(w_value), wout=w_out, wup=w_up, wdown=w_down,
        ),
    )
    ins = dict(
        rows_in, media_gain=gains["media_gain"], latent_gain=gains["latent_gain"], fvec=a["fvec_o"], dres=a["dres_o"],
        key_norm=a["key_norm_o"], keys=a["keys_o"], values=a["values_o"], query=a["query_o"], mixed=a["mixed_o"],
        dattn=a["dattn_o"], ffn=a["ffn_o"], dout=a["dout_o"], act=a["act_o"], dhid=a["dhid_o"], dall=a["dall"], fall=a["fall"],
        wout=w_out, wup=w_up, wdown=w_down, out_own=a["out_o"], out_send=a["out_send_o"],
    )
    if t.aligned:
        ins.update(wk=w_key, wv=w_value, wq=w_query)
    else:
        pair = jnp.stack([w_key.reshape(width, heads, cols), w_value.reshape(width, heads, cols)], axis=2)
        padded = jnp.pad(w_query.reshape(width, heads, cols), ((0, 0), (0, 0), (0, t.EP - cols)))
        ins.update(wkv=pair.reshape(width, 2 * width), wq=padded.reshape(width, -1), dattn_cols=columns(a["dattn_o"]))
    b = backward(s, ins)
    share = width // (rows * heads)
    vector = lax.dynamic_slice_in_dim(b["vec_o"], (at.x * heads + at.h) * share, share, 1)
    names = ("out_o", "media_o", "lat_o", "query_grad", "key_grad", "value_grad", "out_grad", "up_grad", "down_grad")
    out, media_grad, latents_grad, query_grad, key_grad, value_grad, out_grad, up_grad, down_grad = finish([b[k] for k in names])
    return (
        out.reshape(latents.shape), media_grad.reshape(media.shape), latents_grad.reshape(latents.shape), vector[0], vector[1],
        vector[2], vector[3], query_grad, key_grad, value_grad, out_grad, vector[4], vector[5], up_grad, down_grad.T,
    )


def solution(mesh):
    row = P("rows", "head", None)
    whole = P()
    vector = P(("rows", "head"))
    grid = P("rows", "head")
    return jax.shard_map(
        body,
        mesh=mesh,
        in_specs=(row, row) + (whole,) * 13 + (row,),
        out_specs=(row, row, row, vector, vector, vector, vector, grid, grid, grid, grid, vector, vector, grid, P("head", "rows")),
        check_vma=False,
    )
```

```python
import functools
import math
import types

import jax
import jax.numpy as jnp
from jax import lax
from jax.experimental import pallas as pl
from jax.experimental.pallas import tpu as pltpu
from jax.sharding import PartitionSpec as P

HEAD_DIM = 96
MAX_IMG = 8
EPSILON = 1e-05
BF = jnp.bfloat16
F32 = jnp.float32
MESH = pl.DeviceIdType.MESH
ANY = pl.BlockSpec(memory_space=pl.ANY)
VMEM = pl.BlockSpec(memory_space=pltpu.VMEM)
SMEM = pl.BlockSpec(memory_space=pltpu.SMEM)


def factor_rows(count):
    nz = 4 if count % 4 == 0 else 1
    return nz, count // nz


def factor_head(count):
    nc = 2 if count % 2 == 0 else 1
    return count // nc, nc


def mm(a, b):
    return lax.dot_general(a, b, (((1,), (0,)), ((), ())), preferred_element_type=F32)


def mt(a, b):
    return lax.dot_general(a, b, (((1,), (1,)), ((), ())), preferred_element_type=F32)


def tm(a, b):
    return lax.dot_general(a, b, (((0,), (0,)), ((), ())), preferred_element_type=F32)


class Place:
    def __init__(self, rows, heads):
        self.rows, self.heads = rows, heads
        self.nz, self.nx = factor_rows(rows)
        self.ny, self.nc = factor_head(heads)
        self.r = lax.axis_index("rows")
        self.h = lax.axis_index("head")
        self.z, self.x = lax.div(self.r, self.nx), lax.rem(self.r, self.nx)
        self.y, self.c = lax.div(self.h, self.nc), lax.rem(self.h, self.nc)
        self.zs, self.xs, self.ys = [
            [self.turn(at, d, size) for d in range(size)]
            for at, size in ((self.z, self.nz), (self.x, self.nx), (self.y, self.ny))
        ]
        self.other = self.nc - 1 - self.c
        self.groups = [[z * self.nx + x for x in self.xs] for z in self.zs]
        self.slots = [y * self.nc + c for y in self.ys for c in (self.c, self.other)[: self.nc]]
        self.partner = (self.r, self.y * self.nc + self.other)

    @staticmethod
    def turn(at, d, size):
        if d == 0:
            return at
        there = at + d
        return jnp.where(there >= size, there - size, there)

    def group(self, dz, dx):
        return self.groups[dz % self.nz][dx % self.nx]

    def on_y(self, d):
        return self.r, self.slots[d * self.nc]

    def on_x(self, d):
        return self.group(0, d), self.h

    def on_z(self, d):
        return self.group(d, 0), self.h

    def greet(self):
        peers = [(self.r, head) for head in self.slots[1:]]
        peers += [self.on_x(d) for d in range(1, self.nx)] + [self.on_z(d) for d in range(1, self.nz)]
        barrier = pltpu.get_barrier_semaphore()
        for peer in peers:
            pl.semaphore_signal(barrier, inc=1, device_id=peer, device_id_type=MESH)
        pl.semaphore_wait(barrier, len(peers))


class Copies:
    def __init__(self, at, send, recv, local):
        self.at, self.send, self.recv, self.local = at, send, recv, local
        self.used, self.used_local = 0, 0
        self.unsent, self.open = [], []

    def plan(self, src, dst, peer):
        copy = pltpu.make_async_remote_copy(
            src_ref=src,
            dst_ref=dst,
            send_sem=self.send.at[self.used],
            recv_sem=self.recv.at[self.used],
            device_id=peer,
            device_id_type=MESH,
        )
        self.used += 1
        self.unsent.append(copy)
        return copy

    def put(self, src, dst, peer):
        copy = self.plan(src, dst, peer)
        copy.start()
        return copy

    def put_y(self, src, dst):
        return [self.put(src, dst, self.at.on_y(d)) for d in range(1, self.at.ny)]

    def put_x(self, src, dst):
        return [self.put(src, dst, self.at.on_x(d)) for d in range(1, self.at.nx)]

    def put_z(self, src, dst):
        return [self.put(src, dst, self.at.on_z(d)) for d in range(1, self.at.nz)]

    def put_core(self, src, dst):
        return [self.put(src, dst, self.at.partner)] if self.at.nc > 1 else []

    def sent(self, copies):
        for copy in copies:
            copy.wait_send()
        self.unsent = [c for c in self.unsent if all(c is not d for d in copies)]

    def plan_move(self, src, dst):
        copy = pltpu.make_async_copy(src, dst, self.local.at[self.used_local])
        self.used_local += 1
        self.open.append(copy)
        return copy

    def move(self, src, dst):
        copy = self.plan_move(src, dst)
        copy.start()
        return copy

    def moved(self, *copies):
        for copy in copies:
            copy.wait()
        self.open = [c for c in self.open if all(c is not d for d in copies)]

    def finish(self):
        for copy in self.unsent:
            copy.wait_send()
        for copy in self.open:
            copy.wait()


def begin(copies):
    for copy in copies:
        copy.start()


def arrived(copies):
    for copy in copies:
        copy.wait_recv()


def norm_rows(block):
    mean = jnp.mean(block, axis=-1, keepdims=True)
    centered = block - mean
    scale = lax.rsqrt(jnp.mean(centered * centered, axis=-1, keepdims=True) + EPSILON)
    return centered * scale, scale


def sweep(first, last, step, carry=0):
    together = next(k for k in (4, 2, 1) if (last - first) // 16 % k == 0)

    def turn(i, value):
        for j in range(together):
            start = first + i * (16 * together) + j * 16
            value = step(pl.ds(pl.multiple_of(start, 16), 16), value)
        return value

    return lax.fori_loop(0, (last - first) // (16 * together), turn, carry)


def gelu_pair(v):
    c = math.sqrt(2.0 / math.pi)
    square = v * v
    t = jnp.tanh(c * v * (1.0 + 0.044715 * square))
    half = 0.5 * (1.0 + t)
    slope = half + 0.5 * v * (1.0 - t * t) * (c * (1.0 + 3.0 * 0.044715 * square))
    return v * half, slope


def softmax(scores):
    powers = jnp.exp(scores - jnp.max(scores, axis=-1, keepdims=True))
    return powers * (1.0 / jnp.sum(powers, axis=-1, keepdims=True))


def head_mask(heads_here, rows, cols):
    col = lax.broadcasted_iota(jnp.int32, (rows, cols), 1)
    return jnp.concatenate(
        [((col >= j * HEAD_DIM) & (col < (j + 1) * HEAD_DIM)).astype(F32) for j in range(heads_here)], axis=0
    )


def spread_heads(block, mask):
    return jnp.concatenate([block] * (mask.shape[0] // block.shape[0]), axis=0) * mask


def gather_heads(block, mask, rows):
    block = block * mask
    return sum(block[j * rows : (j + 1) * rows] for j in range(block.shape[0] // rows))


def sizes_of(s):
    ny, nc = factor_head(s.heads)
    nz, nx = factor_rows(s.rows)
    t = types.SimpleNamespace(ny=ny, nc=nc, nz=nz, nx=nx, G=s.images, D=s.width, E=s.cols, F=s.mine, H=s.heads)
    t.pr, t.ll = s.patch, s.lat
    t.M, t.L, t.LR = t.G * t.pr, t.G * t.ll, t.H * t.ll
    t.GL, t.ML, t.KC = t.G * t.LR, t.M + t.L, t.H * t.pr + t.LR
    t.B = t.D // s.rows
    t.heads_here = t.E // HEAD_DIM
    t.aligned = t.E % 128 == 0
    t.EP = -(-t.E // 128) * 128
    t.by_rows = t.aligned and ny == 2 and nc == 2
    t.W = ny * t.E if t.by_rows else t.E
    t.wide_heads = t.W // HEAD_DIM
    return t


def forward_kernel(s, names, *refs):
    n = types.SimpleNamespace(**dict(zip(names, refs, strict=True)))
    at = Place(s.rows, s.heads)
    t = sizes_of(s)
    ny, nc, nz, nx, G, H = t.ny, t.nc, t.nz, t.nx, t.G, t.H
    M, L, LR, GL, ML, D, E, F, ll, pr = t.M, t.L, t.LR, t.GL, t.ML, t.D, t.E, t.F, t.ll, t.pr
    io = Copies(at, n.send, n.recv, n.local)
    here = at.r

    vectors = ("media_gain", "media_shift", "latent_gain", "latent_shift", "ffn_gain", "ffn_shift")
    load_vecs = [io.move(getattr(n, k), n.vecs.at[i]) for i, k in enumerate(vectors)]
    load_lat = io.move(n.lat, n.raw_l.at[0:L])
    load_cot = io.move(n.cot, n.cot_v)
    load_media = io.move(n.media, n.raw_m.at[0])

    def columns(weight):
        return weight.at[:, pl.ds(pl.multiple_of(at.h * E, 128), E)] if t.aligned else weight

    load_qkv = [io.move(columns(w), v.at[:, 0:E]) for w, v in ((n.wk, n.wk_v), (n.wv, n.wv_v), (n.wq, n.wq_v))]
    if t.by_rows:
        for w, v in ((n.wk, n.wk_v), (n.wv, n.wv_v), (n.wq, n.wq_v)):
            lanes = pl.ds(pl.multiple_of(at.slots[nc] * E, 128), E)
            load_qkv.append(io.move(w.at[:, lanes], v.at[:, E : 2 * E]))
    at.greet()

    bounds = [0, pr, M] if t.by_rows and G > 1 else [0, M // 2, M]
    chunks = len(bounds) - 1

    def far_slot(d):
        return (ny - d) % ny * nc

    def lat_rows(k):
        return n.raw_l.at[k * L : (k + 1) * L]

    lat_far = [io.put(n.lat, lat_rows(far_slot(d)), at.on_y(d)) for d in range(1, ny)]
    lat_near = io.put_core(n.lat, lat_rows(1 % H))
    media_far, media_near = [], []

    def send_patches(j):
        rows = slice(bounds[j], bounds[j + 1])
        media_far.append([io.put(n.media.at[rows], n.raw_m.at[far_slot(d), rows], at.on_y(d)) for d in range(1, ny)])

    for j in range(chunks):
        rows = slice(bounds[j], bounds[j + 1])
        media_near.append(io.put_core(n.media.at[rows], n.raw_m.at[1 % H, rows]))
    if not t.by_rows:
        for j in range(chunks):
            send_patches(j)

    io.moved(load_cot)
    for i in range(G):
        image = here * G + i
        limit = n.counts[lax.div(image, MAX_IMG)]
        live = jnp.where(lax.rem(image, MAX_IMG) < limit, 1.0, 0.0).astype(F32)
        rows = slice(i * ll, (i + 1) * ll)
        n.wide_l[rows] = n.cot_v[rows].astype(F32) * live
    n.dslot[at.y, at.c] = n.wide_l[...].astype(BF)
    own_d = n.dslot.at[at.y, at.c]

    def quarter(r, y):
        return r, pl.ds(pl.multiple_of(y * L, 16), L)

    def across(y, block):
        where = n.dall.at[quarter(here, y)]
        return io.put_z(block, where), io.put_x(block, where)

    z_far, x_far = {}, {}
    if t.by_rows:
        cot_far = io.put_y(own_d, own_d)
        cot_near = io.put_core(own_d, own_d)
        send_patches(0)
    z_far[0], x_far[0] = across(at.y, own_d)
    load_out = io.move(n.wout, n.wout_v)
    load_up = io.move(n.wup.at[:, pl.ds(pl.multiple_of(at.h * F, 128), F)], n.wup_v)
    load_down = io.move(n.wdown.at[pl.ds(pl.multiple_of(at.h * F, 16), F)], n.wdown_v)

    def forward_x(d, first=1, last=nz):
        for dz in range(first, last):
            z_far[d][dz - 1].wait_recv()
            block = n.dall.at[quarter(at.group(nz - dz, 0), at.ys[d])]
            x_far[d] += io.put_x(block, block)

    norm_busy = {}
    turn_count = [0]

    def patches(k, first, last):
        buf = turn_count[0] % 2
        turn_count[0] += 1
        if buf in norm_busy:
            io.moved(norm_busy[buf])

        def step(rows, carry):
            hat, _ = norm_rows(n.raw_m[k, rows].astype(F32))
            n.norm[buf, rows] = (hat * n.vecs[0:1] + n.vecs[1:2]).astype(BF)
            return carry

        sweep(first * 16, last * 16, step)
        rows = slice(first * 16, last * 16)
        near = t.by_rows and k < nc
        lanes = t.W if near else E
        for weight, result, chip in ((n.wk_v, n.keys, n.keys_w), (n.wv_v, n.values, n.values_w)):
            wide = mm(n.norm[buf, rows], weight[:, 0:lanes]).astype(BF)
            for i in range(first * 16 // pr, last * 16 // pr):
                base = i * pr - first * 16
                result[i, k * pr : (k + 1) * pr] = wide[base : base + pr, 0:E]
                if near:
                    chip[i, k * pr : (k + 1) * pr] = wide[base : base + pr]
        norm_busy[buf] = io.move(n.norm.at[buf, rows], n.key_norm_o.at[k * ML + first * 16 : k * ML + last * 16])

    io.moved(load_media, *load_qkv, *load_vecs)
    patches(0, 0, M // 16)
    if nc > 1:
        for copies in media_near:
            arrived(copies)
        patches(1, 0, M // 16)
    if not t.by_rows:
        cot_far = io.put_y(own_d, own_d)
        cot_near = io.put_core(own_d, own_d)
    relay = []
    for d, copy in zip(range(1, ny), lat_far):
        copy.wait_recv()
        k = far_slot(d)
        relay += io.put_core(lat_rows(k), lat_rows(k + 1)) if nc > 1 else []
    io.moved(load_lat)
    arrived(lat_near)
    arrived(relay)
    for k in range(H):
        wide = n.raw_l[k * L : (k + 1) * L].astype(F32)
        for i in range(G):
            n.resid[pl.ds(pl.multiple_of(i * LR + at.slots[k] * ll, 8), ll)] = wide[i * ll : (i + 1) * ll]

    def latent_step(rows, carry):
        hat, _ = norm_rows(n.raw_l[rows].astype(F32))
        n.lnorm[rows] = (hat * n.vecs[2:3] + n.vecs[3:4]).astype(BF)
        return carry

    sweep(0, H * L, latent_step)
    for k in range(H):
        io.move(n.lnorm.at[k * L : (k + 1) * L], n.key_norm_o.at[k * ML + M : (k + 1) * ML])
    for weight, result, chip in ((n.wq_v, n.query, n.query_w), (n.wk_v, n.keys, n.keys_w), (n.wv_v, n.values, n.values_w)):
        wide = mm(n.lnorm[...], weight[...])
        for k in range(H):
            for i in range(G):
                n.turn[pl.ds(pl.multiple_of(i * LR + at.slots[k] * ll, 8), ll)] = wide[k * L + i * ll : k * L + (i + 1) * ll]
        for i in range(G):
            block = n.turn[i * LR : (i + 1) * LR].astype(BF)
            if result is n.query:
                result[i] = block[:, 0:E]
                if t.by_rows:
                    chip[i] = block
            else:
                result[i, H * pr : t.KC] = block[:, 0:E]
                if t.by_rows:
                    pair = [wide[k * L + i * ll : k * L + (i + 1) * ll] for k in range(nc)]
                    chip[i, nc * pr : nc * (pr + ll)] = jnp.concatenate(pair, axis=0).astype(BF)

    def far_patches(j):
        relays = []
        rows = slice(bounds[j], bounds[j + 1])
        for d, copy in zip(range(1, ny), media_far[j]):
            copy.wait_recv()
            k = far_slot(d)
            relays.append(io.put_core(n.raw_m.at[k, rows], n.raw_m.at[k + 1, rows]) if nc > 1 else [])
        for d in range(1, ny):
            patches(far_slot(d), bounds[j] // 16, bounds[j + 1] // 16)
        for d in range(1, ny):
            if nc > 1:
                arrived(relays[d - 1])
                patches(far_slot(d) + 1, bounds[j] // 16, bounds[j + 1] // 16)

    cot_relay = []

    def far_cotangents():
        arrived(cot_far)
        for d in range(1, ny):
            block = n.dslot.at[at.ys[d], at.c]
            cot_relay.extend(io.put_core(block, block))

    def cross_cotangents():
        for d in range(1, ny):
            z_far[d], x_far[d] = across(at.ys[d], n.dslot.at[at.ys[d], at.c])

    def group_cotangents():
        arrived(cot_near)
        arrived(cot_relay)
        for y in range(ny):
            for c in range(nc):
                wide = n.dslot[y, c].astype(F32)
                for i in range(G):
                    n.part[i * LR + (y * nc + c) * ll : i * LR + (y * nc + c + 1) * ll] = wide[i * ll : (i + 1) * ll]
        n.dout[...] = n.part[...].astype(BF)
        io.move(n.dout, n.dout_o)

    def add_mixed(head):
        n.resid[...] += mm(n.mix[head], n.wout_v[pl.ds(pl.multiple_of(head * E, 16), E)])

    scale = 1.0 / math.sqrt(HEAD_DIM)
    mask = head_mask(t.wide_heads, LR, t.W)
    mask_low = mask.astype(BF)
    if t.by_rows:
        far_cotangents()
        lane = lax.broadcasted_iota(jnp.int32, (LR, 128), 1)
        for i in range(G):
            scores = mt(spread_heads(n.query_w[i], mask_low), n.keys_w[i]) * scale
            top = jnp.max(scores, axis=-1, keepdims=True)
            powers = jnp.exp(scores - top)
            total = jnp.sum(powers, axis=-1, keepdims=True)
            mixed = gather_heads(mm(powers.astype(BF), n.values_w[i]) * (1.0 / total), mask, LR)
            rows = slice(i * LR, (i + 1) * LR)
            n.o_send[rows] = mixed.astype(BF)
            log_total = top + jnp.log(total)
            stats = jnp.zeros((LR, 128), F32)
            for j in range(t.wide_heads):
                one = log_total[j * LR : (j + 1) * LR]
                high = one.astype(BF).astype(F32)
                stats = jnp.where(lane == j, high, stats)
                stats = jnp.where(lane == j + t.wide_heads, one - high, stats)
            n.l_send[rows] = stats.astype(BF)
        o_far = io.put_y(n.o_send, n.o_recv) + io.put_y(n.l_send, n.l_recv)
        send_patches(1)
        row = lax.broadcasted_iota(jnp.int32, (128, t.W), 0)
        col = lax.broadcasted_iota(jnp.int32, (128, t.W), 1)
        widen = jnp.zeros((128, t.W), F32)
        for j in range(t.wide_heads):
            inside = (col >= j * HEAD_DIM) & (col < (j + 1) * HEAD_DIM)
            widen = jnp.where(inside & ((row == j) | (row == j + t.wide_heads)), 1.0, widen)
        widen = widen.astype(BF)

        def other_chip(block):
            return jnp.concatenate([block[:, E : 2 * E], block[:, 0:E]], axis=-1)

        far_patches(0)
        group_cotangents()
        io.moved(load_out, load_up, load_down)
        forward_x(0)
        cross_cotangents()
        arrived(o_far)
        for i in range(G):
            rows = slice(i * LR, (i + 1) * LR)
            near_log, far_log = mm(n.l_send[rows], widen), other_chip(mm(n.l_recv[rows], widen))
            top = jnp.maximum(near_log, far_log)
            near_part, far_part = jnp.exp(near_log - top), jnp.exp(far_log - top)
            mixed = n.o_send[rows].astype(F32) * near_part + other_chip(n.o_recv[rows].astype(F32)) * far_part
            mixed = mixed * (1.0 / (near_part + far_part))
            for d in range(ny):
                n.mix[at.slots[d * nc], rows] = mixed[:, d * E : (d + 1) * E].astype(BF)
        mix_near = [io.put_core(n.mix.at[at.slots[d * nc]], n.mix.at[at.slots[d * nc]]) for d in range(ny)]
        for d in range(ny):
            add_mixed(at.slots[d * nc])
        for d in range(ny):
            arrived(mix_near[d])
            add_mixed(at.slots[d * nc + 1])
    else:
        for j in range(chunks):
            far_patches(j)
        far_cotangents()
        cross_cotangents()
        forward_x(0)
        for i in range(G):
            scores = mt(spread_heads(n.query[i], mask_low), n.keys[i]) * scale
            probs = softmax(scores).astype(BF)
            mixed = gather_heads(mm(probs, n.values[i]), mask, LR)
            n.mix[at.h, i * LR : (i + 1) * LR] = mixed.astype(BF)
        mix_far = io.put_y(n.mix.at[at.h], n.mix.at[at.h])
        mix_near = io.put_core(n.mix.at[at.h], n.mix.at[at.h])
        io.moved(load_out, load_up, load_down)
        add_mixed(at.h)
        arrived(mix_near)
        if nc > 1:
            add_mixed(at.slots[1])
        group_cotangents()
        mix_relay = []
        for d, copy in zip(range(1, ny), mix_far):
            copy.wait_recv()
            block = n.mix.at[at.slots[far_slot(d)]]
            mix_relay.append(io.put_core(block, block))
        for d in range(1, ny):
            add_mixed(at.slots[far_slot(d)])
        for d in range(1, ny):
            if nc > 1:
                arrived(mix_relay[d - 1])
                add_mixed(at.slots[far_slot(d) + 1])
    io.move(n.mix, n.mixed_o)
    gain, shift = n.vecs[4:5], n.vecs[5:6]

    def ffn_step(rows, carry):
        hat, inv = norm_rows(n.resid[rows])
        n.hat[rows] = hat
        n.inv[rows] = jnp.broadcast_to(inv, (16, 128))
        n.ffn[rows] = (hat * n.vecs[4:5] + n.vecs[5:6]).astype(BF)
        return carry

    sweep(0, GL, ffn_step)
    io.move(n.ffn, n.ffn_o)

    def own_rows(ref):
        return jnp.concatenate([ref[pl.ds(pl.multiple_of(i * LR + at.h * ll, 8), ll)] for i in range(G)], axis=0)

    n.fq[...] = (own_rows(n.hat) * gain + shift).astype(BF)
    own_f = n.fall.at[at.z]
    ffn_far = io.put_z(n.fq, own_f)
    io.move(n.fq, own_f)
    value, slope = gelu_pair(mm(n.ffn[...], n.wup_v[...]))
    n.act[...] = value.astype(BF)
    n.dhid[...] = (mt(n.dout[...], n.wdown_v[...]) * slope).astype(BF)
    n.part[...] = mt(n.dhid[...], n.wup_v[...])
    half = GL // nc
    theirs = pl.ds(pl.multiple_of((nc - 1 - at.c) * half, 16), half)
    swap = io.put_core(n.part.at[theirs], n.c_recv)
    io.move(n.act, n.act_o)
    io.move(n.dhid, n.dhid_o)
    out_part = mm(n.act[...], n.wdown_v[...])
    for i in range(G):
        for head in range(H):
            base = i * LR + head * ll
            n.outp[head % nc, head // nc, i * ll : (i + 1) * ll] = out_part[base : base + ll]
    out_swap = io.put_core(n.outp.at[nc - 1 - at.c], n.oc_recv)
    for d in range(1, ny):
        forward_x(d)
    arrived(swap)
    pieces = 2
    piece = half // pieces
    sum_far = []
    for j in range(pieces):
        rows = slice(j * piece, (j + 1) * piece)
        total = n.part[pl.ds(pl.multiple_of(at.c * half + j * piece, 16), piece)]
        if nc > 1:
            total = total + n.c_recv[rows]
        n.y_send[rows] = total.astype(BF)
        sum_far.append([io.put(n.y_send.at[rows], n.y_recv.at[d - 1, rows], at.on_y(d)) for d in range(1, ny)])
    io.sent(swap)
    if t.by_rows:
        far_patches(1)
    arrived(out_swap)
    for y in range(ny):
        total = n.outp[at.c, y]
        if nc > 1:
            total = total + n.oc_recv[y]
        n.outp[at.c, y] = total
        n.oy_send[y] = total.astype(BF)
    for ref, out in ((n.keys, n.keys_o), (n.values, n.values_o), (n.query, n.query_o)):
        io.move(ref, out)

    def residual_back(ref, base, first, last):
        def step(from_rows, carry):
            rows = pl.ds(pl.multiple_of(base + from_rows.start, 16), 16)
            grad = ref[from_rows]
            hat, inv = n.hat[rows], n.inv[rows, 0:1]
            n.part[rows] = grad
            scaled = grad * n.vecs[4:5]
            first = jnp.mean(scaled, axis=-1, keepdims=True)
            second = jnp.mean(scaled * hat, axis=-1, keepdims=True)
            d_res = n.dout[rows].astype(F32) + inv * (scaled - first - hat * second)
            n.resid[rows] = d_res
            n.dattn[rows] = d_res.astype(BF)
            return carry

        sweep(first, last, step)

    n.own[0] = n.outp[at.c, at.y] + own_rows(n.resid)
    io.move(n.own.at[0], n.out_o)
    io.move(n.oy_send, n.out_send_o)
    share = []
    for j in range(pieces):
        rows = slice(j * piece, (j + 1) * piece)
        arrived(sum_far[j])
        total = n.y_send[rows].astype(F32)
        for d in range(1, ny):
            total = total + n.y_recv[d - 1, rows].astype(F32)
        n.share[rows] = total
        share.append(io.put_core(n.share.at[rows], n.s_recv.at[rows]))
        residual_back(n.share, at.c * half, j * piece, (j + 1) * piece)
    if nc > 1:
        for j in range(pieces):
            arrived(share[j])
            residual_back(n.s_recv, (nc - 1 - at.c) * half, j * piece, (j + 1) * piece)
    io.move(n.dattn, n.dattn_o)
    n.own[1] = own_rows(n.resid)
    io.move(n.own.at[1], n.dres_o)
    grad = own_rows(n.part)
    n.fvec[0:1] = jnp.sum(grad * own_rows(n.hat), axis=0, keepdims=True)
    n.fvec[1:2] = jnp.sum(grad, axis=0, keepdims=True)
    n.fvec[2:8] = jnp.zeros((6, D), F32)
    io.move(n.fvec, n.fvec_o)
    for d in range(ny):
        arrived(x_far[d])
    arrived(ffn_far)
    io.finish()


def call(kernel, s, name, ident, ins, outs, scratch, semaphores, places, limit, cost):
    names = list(ins) + list(outs) + list(scratch) + ["send", "recv", "local"]
    dma = [pltpu.SemaphoreType.DMA((count,)) for count in (semaphores, semaphores, 120)]
    result = pl.pallas_call(
        functools.partial(kernel, s, names),
        name=name,
        out_shape=[jax.ShapeDtypeStruct(*o) for o in outs.values()],
        in_specs=[places.get(k, ANY) for k in ins],
        out_specs=[ANY] * len(outs),
        scratch_shapes=[pltpu.VMEM(*v) for v in scratch.values()] + dma,
        compiler_params=pltpu.CompilerParams(collective_id=ident, has_side_effects=True, vmem_limit_bytes=limit << 20),
        cost_estimate=cost,
    )(*ins.values())
    return dict(zip(outs, result, strict=True))


def forward(s, ins):
    t = sizes_of(s)
    ny, nc, G, H, M, L, LR, GL, ML, D, E, F = t.ny, t.nc, t.G, t.H, t.M, t.L, t.LR, t.GL, t.ML, t.D, t.E, t.F
    half = GL // nc
    far, W = max(ny - 1, 1), t.W
    outs = dict(
        out_o=((L, D), F32), dres_o=((L, D), F32), fvec_o=((8, D), F32), key_norm_o=((H * ML, D), BF),
        keys_o=((G, t.KC, E), BF), values_o=((G, t.KC, E), BF), query_o=((G, LR, E), BF), mixed_o=((H, GL, E), BF),
        dattn_o=((GL, D), BF), ffn_o=((GL, D), BF), dout_o=((GL, D), BF), act_o=((GL, F), BF), dhid_o=((GL, F), BF),
        dall=((s.rows, ny * L, D), BF), fall=((t.nz, L, D), BF), out_send_o=((ny, L, D), BF),
    )
    scratch = dict(
        vecs=((8, D), F32), cot_v=((L, D), BF), wide_l=((L, D), F32), raw_m=((H, M, D), BF), raw_l=((H * L, D), BF), dslot=((ny, nc, L, D), BF),
        norm=((2, M, D), BF), lnorm=((H * L, D), BF), turn=((GL, W), F32), keys=((G, t.KC, E), BF), values=((G, t.KC, E), BF),
        query=((G, LR, E), BF), mix=((H, GL, E), BF), resid=((GL, D), F32), hat=((GL, D), F32), inv=((GL, 128), F32),
        ffn=((GL, D), BF), dout=((GL, D), BF), act=((GL, F), BF), dhid=((GL, F), BF), part=((GL, D), F32),
        outp=((nc, ny, L, D), F32), c_recv=((half, D), F32), oc_recv=((ny, L, D), F32), y_send=((half, D), BF),
        y_recv=((far, half, D), BF), oy_send=((ny, L, D), BF), share=((half, D), F32),
        s_recv=((half, D), F32), fq=((L, D), BF), own=((2, L, D), F32), dattn=((GL, D), BF),
        fvec=((8, D), F32), wq_v=((D, W), BF), wk_v=((D, W), BF), wv_v=((D, W), BF), wout_v=((D, D), BF),
        wup_v=((D, F), BF), wdown_v=((F, D), BF),
    )
    shape = (G, nc * (t.pr + t.ll), W) if t.by_rows else (1, 16, 128)
    rows = (GL, W) if t.by_rows else (16, 128)
    scratch.update(
        keys_w=(shape, BF), values_w=(shape, BF), query_w=((G, LR, W) if t.by_rows else shape, BF), o_send=(rows, BF),
        o_recv=(rows, BF), l_send=((rows[0], 128), BF), l_recv=((rows[0], 128), BF),
    )
    places = {"counts": SMEM}
    cost = pl.CostEstimate(flops=8 * 10**9, bytes_accessed=4 * 10**7, transcendentals=10**6)
    return call(forward_kernel, s, "forward", 1, ins, outs, scratch, 200, places, 62, cost)


def window_of(position, block, width):
    base = jnp.minimum(position * block // 128 * 128, width - 256)
    return pl.multiple_of(base, 128), position * block - base


def backward_kernel(s, names, *refs):
    n = types.SimpleNamespace(**dict(zip(names, refs, strict=True)))
    at = Place(s.rows, s.heads)
    t = sizes_of(s)
    ny, nc, nz, nx, G, H = t.ny, t.nc, t.nz, t.nx, t.G, t.H
    M, L, LR, GL, ML, D, E, F, ll, pr, B = t.M, t.L, t.LR, t.GL, t.ML, t.D, t.E, t.F, t.ll, t.pr, t.B
    here = at.r
    io = Copies(at, n.send, n.recv, n.local)

    def quarter(r, y):
        return r, pl.ds(pl.multiple_of((at.c * ny + y) * L, 16), L)

    aligned = t.aligned
    first_loads = [io.move(n.dattn, n.ffn_v.at[1]), io.move(n.mixed, n.mix_v)]
    first_loads.append(io.move(n.wout.at[pl.ds(pl.multiple_of(at.h * E, 16), E)], n.wout_v))
    if aligned:
        first_loads.append(io.move(n.dattn.at[:, pl.ds(pl.multiple_of(at.h * E, 128), E)], n.dcols_v))
    else:
        first_loads.append(io.move(n.dattn_cols, n.dcols_v))
    attend_loads = [io.move(getattr(n, k), getattr(n, k + "_v")) for k in ("keys", "values", "query")]
    norm_load = io.move(n.key_norm, n.norm_v)
    own_loads = [io.move(n.act, n.dout_v.at[1, :, 0:F]), io.move(n.ffn, n.ffn_v.at[0]), io.move(n.dout, n.dout_v.at[0])]
    ffn_loads = [io.move(n.wup.at[:, pl.ds(pl.multiple_of(at.h * F, 128), F)], n.wup_v)]
    ffn_loads.append(io.move(n.wdown.at[pl.ds(pl.multiple_of(at.h * F, 16), F)], n.wdown_v))
    if aligned:
        row_loads = []
        for head in range(H):
            for j, weight in enumerate((n.wk, n.wv)):
                lanes = slice((2 * head + j) * E, (2 * head + j + 1) * E)
                row_loads.append(io.move(weight.at[:, head * E : (head + 1) * E], n.w_v.at[:, lanes]))
    else:
        row_loads = [io.move(n.wkv, n.w_v)]
    row_loads += [io.move(n.media_gain, n.vecs.at[0]), io.move(n.latent_gain, n.vecs.at[1]), io.move(n.out_own, n.out_own_v)]
    row_loads += [io.move(n.media, n.media_v), io.move(n.lat, n.lat_v), io.move(n.dres, n.dres_v)]
    at.greet()

    x_quarters = []
    for dz in range(nz):
        source = n.fall.at[at.zs[dz]]
        x_quarters.append(io.put_x(source, n.fall_b.at[quarter(at.group(dz, 0), at.y)]))
    y_quarters = {}
    for dz in range(1, nz):
        source = n.fall.at[at.zs[dz]]
        y_quarters[dz, 0] = io.put_y(source, n.fall_b.at[quarter(at.group(dz, 0), at.y)])

    def core_rows(c):
        return pl.ds(pl.multiple_of(c * ny * L, 16), ny * L)

    for dx in range(1, nx):
        for dz in range(nz):
            block = n.fall_b.at[quarter(at.group(dz, nx - dx), at.y)]
            y_quarters[dz, nx - dx] = [io.plan(block, block, at.on_y(d)) for d in range(1, ny)]
    order = [(dz, 0) for dz in range(1, nz)] + [(dz, nx - dx) for dx in range(1, nx) for dz in range(nz)]
    near, count = nz - 1, len(order)
    to_core, fetched = [], []
    for index, (dz, dx) in enumerate(order):
        r = at.group(dz, dx)
        buf = (index + 1) % 2
        copies = [io.plan(n.dall.at[r], n.dall_b.at[r], at.partner)] if nc > 1 else []
        for d in range(ny):
            block = n.fall_b.at[quarter(r, at.ys[d])]
            source = n.fall.at[at.zs[dz]] if (d == 0 and dx == 0) else block
            copies += [io.plan(source, block, at.partner)] if nc > 1 else []
        to_core.append(copies)
        copies = []
        for c in range(nc):
            rows = core_rows(at.c if c == 0 else nc - 1 - at.c)
            source = n.dall if c == 0 else n.dall_b
            copies.append(io.plan_move(source.at[r], n.dout_v.at[buf, rows]))
        if dx > 0:
            copies.append(io.plan_move(n.fall_b.at[r], n.ffn_v.at[buf]))
        else:
            for slot in range(H):
                core = at.c if slot % nc == 0 else at.other
                rows = pl.ds(pl.multiple_of((core * ny + at.ys[slot // nc]) * L, 16), L)
                source = n.fall.at[at.zs[dz]] if slot == 0 else n.fall_b.at[r, rows]
                copies.append(io.plan_move(source, n.ffn_v.at[buf, rows]))
        fetched.append(copies)

    def spread(index):
        arrived(y_quarters[order[index]])
        begin(to_core[index])

    def fetch(index):
        if index < count:
            arrived(to_core[index])
            begin(fetched[index])

    io.moved(*first_loads)
    n.dmixed[...] = mt(n.ffn_v[1], n.wout_v[...]).astype(BF).reshape(G, LR, E)
    own_loads.append(io.move(n.dhid, n.ffn_v.at[1, :, 0:F]))
    span = nx * B
    if E == span:
        tiles = [tm(n.mix_v[z], n.dcols_v[...]) for z in range(nz)]
    else:
        whole = jnp.concatenate([n.mix_v[head] for head in range(H)], axis=-1)
        tiles = [tm(whole[:, z * span : (z + 1) * span], n.dcols_v[...]) for z in range(nz)]
    for z in range(nz):
        for x in range(nx):
            n.p_out[z, x] = tiles[z][x * B : (x + 1) * B].astype(BF)
    out_x = [io.plan(n.p_out.at[at.z, at.xs[d]], n.xr_out.at[d - 1], at.on_x(d)) for d in range(1, nx)]
    out_z = [io.put(n.p_out.at[at.zs[d]], n.zr_out.at[d - 1], at.on_z(d)) for d in range(1, nz)]

    def out_middle():
        arrived(out_z)
        total = n.p_out[at.z].astype(F32)
        for d in range(1, nz):
            total = total + n.zr_out[d - 1].astype(F32)
        n.p_out[at.z] = total.astype(BF)
        begin(out_x)

    def out_end():
        arrived(out_x)
        total = n.p_out[at.z, at.x].astype(F32)
        for d in range(1, nx):
            total = total + n.xr_out[d - 1].astype(F32)
        n.grad_v[0] = total
        io.move(n.grad_v.at[0], n.out_grad)

    parts = {"kv": (n.p_kv, n.xr_kv, n.zr_kv), "query": (n.p_query, n.xr_query, n.zr_query)}
    x_parts, z_parts = {}, {}
    z_order = list(range(1, nz)) + [0]

    def sum_start(w, rows, grads):
        part, x_recv = parts[w][:2]
        for dz in z_order:
            lanes = pl.ds(pl.multiple_of(at.zs[dz] * span, 128), span)
            tile = tm(rows(lanes), grads)
            for x in range(nx):
                part[dz, x] = tile[x * B : (x + 1) * B].astype(BF)
            z_parts[w, dz] = [io.plan(part.at[dz, at.x], parts[w][2].at[dz - 1], at.on_z(dz))] if dz else []
            x_parts[w, dz] = [
                io.put(part.at[dz, at.xs[d]], x_recv.at[dz, d - 1], at.on_x(d)) for d in range(1, nx)
            ]

    def sum_middle(w, dz):
        part, x_recv, _ = parts[w]
        arrived(x_parts[w, dz])
        total = part[dz, at.x].astype(F32)
        for d in range(1, nx):
            total = total + x_recv[dz, d - 1].astype(F32)
        part[dz, at.x] = total.astype(BF)
        begin(z_parts[w, dz])

    def sum_end(w, outs):
        part, _, z_recv = parts[w]
        total = part[0, at.x].astype(F32)
        for dz in range(1, nz):
            arrived(z_parts[w, dz])
            total = total + z_recv[dz - 1].astype(F32)
        for j, (ref, out) in enumerate(outs):
            ref[...] = total[:, j * E : (j + 1) * E]
            io.move(ref, out)

    io.moved(*attend_loads)
    mask = head_mask(t.heads_here, LR, E)
    mask_low = mask.astype(BF)
    scale = 1.0 / math.sqrt(HEAD_DIM)
    for i in range(G):
        q = spread_heads(n.query_v[i], mask_low)
        d = spread_heads(n.dmixed[i], mask_low)
        k, v = n.keys_v[i], n.values_v[i]
        probs = softmax(mt(q, k) * scale)
        d_probs = mt(d, v)
        inner = jnp.sum(probs * d_probs, axis=-1, keepdims=True)
        d_scores = (probs * (d_probs - inner)).astype(BF)
        d_query = gather_heads(mm(d_scores, k), mask, LR) * scale
        d_pair = jnp.concatenate([tm(d_scores, q) * scale, tm(probs.astype(BF), d)], axis=-1)
        for slot in range(H):
            rows = slice(slot * ML + i * pr, slot * ML + (i + 1) * pr)
            n.dkv[rows] = d_pair[slot * pr : (slot + 1) * pr].astype(BF)
        for head in range(H):
            rows = slice(H * pr + head * ll, H * pr + (head + 1) * ll)
            n.turn_kv[head, i * ll : (i + 1) * ll] = d_pair[rows]
            n.turn_q[head, i * ll : (i + 1) * ll, 0:E] = d_query[head * ll : (head + 1) * ll]
    if t.EP > E:
        n.turn_q[:, :, E : t.EP] = jnp.zeros((H, L, t.EP - E), F32)
    for slot in range(H):
        head = at.slots[slot]
        n.dkv[slot * ML + M : (slot + 1) * ML] = n.turn_kv[head].astype(BF)
        n.dq[slot * L : (slot + 1) * L] = n.turn_q[head].astype(BF)
    kv_lanes = pl.ds(pl.multiple_of(at.h * 2 * E, 128), 2 * E)
    q_lanes = pl.ds(pl.multiple_of(at.h * t.EP, 128), t.EP)
    turned = []
    for slot in range(1, H):
        peer = (at.r, at.slots[slot])
        turned.append(io.put(n.dkv.at[slot * ML : (slot + 1) * ML], n.dkv_full.at[:, kv_lanes], peer))
        turned.append(io.put(n.dq.at[slot * L : (slot + 1) * L], n.dq_full.at[:, q_lanes], peer))
    out_far = [io.plan(n.out_send.at[at.ys[d]], n.out_recv.at[d - 1], at.on_y(d)) for d in range(1, ny)]
    io.moved(norm_load)
    sum_start("kv", lambda lanes: n.norm_v[:, lanes], n.dkv[...])
    sum_start(
        "query",
        lambda lanes: jnp.concatenate([n.norm_v[slot * ML + M : (slot + 1) * ML, lanes] for slot in range(H)], axis=0),
        n.dq[:, 0:E],
    )
    base, offset = window_of(here, B, D)
    window = pl.ds(base, 256)
    io.moved(*own_loads)
    n.up_acc[...] = tm(n.ffn_v[0, :, window], n.ffn_v[1, :, 0:F])
    n.down_acc[...] = tm(n.dout_v[0, :, window], n.dout_v[1, :, 0:F])
    q_load = io.plan_move(n.wq, n.w_v.at[:, 0 : n.wq.shape[1]])
    media_out, lat_out = io.plan_move(n.drow.at[0:M], n.media_o), io.plan_move(n.drow.at[M:ML], n.lat_o)
    own_out = io.plan_move(n.out_own_v, n.out_o)
    vec_z = [io.plan(n.vec_sum.at[at.zs[d]], n.vec_z.at[d - 1], at.on_z(d)) for d in range(1, nz)]

    def back_slot(k):
        return (ny - k // nc) % ny * nc + k % nc

    vec_head = [io.plan(n.vec_own, n.vec_head.at[back_slot(k) - 1], (at.r, at.slots[k])) for k in range(1, H)]

    def norm_back_rows(raw, size, base, gain_row, extra):
        def step(rows, sums):
            grad_rows = pl.ds(pl.multiple_of(base + rows.start, 16), 16)
            hat, inv = norm_rows(raw[rows].astype(F32))
            grad = n.drow[grad_rows]
            product = grad * hat
            scaled = grad * n.vecs[gain_row : gain_row + 1]
            mean = jnp.mean(scaled, axis=-1, keepdims=True)
            second = jnp.mean(scaled * hat, axis=-1, keepdims=True)
            result = inv * (scaled - mean - hat * second)
            n.drow[grad_rows] = result if extra is None else result + extra[rows]
            return sums[0] + product[:8] + product[8:], sums[1] + grad[:8] + grad[8:]

        sums = sweep(0, size, step, (jnp.zeros((8, D), F32), jnp.zeros((8, D), F32)))
        return [jnp.sum(v, axis=0, keepdims=True) for v in sums]

    def own_gradients():
        n.dkv_full[:, kv_lanes] = n.dkv[0:ML]
        n.dq_full[:, q_lanes] = n.dq[0:L]
        io.moved(*row_loads)
        arrived(turned)
        n.drow[...] = mt(n.dkv_full[...], n.w_v[...])
        begin([q_load])
        n.vec_own[0:1], n.vec_own[1:2] = norm_back_rows(n.media_v, M, 0, 0, None)
        begin([media_out])
        io.moved(q_load)
        n.drow[M:ML] += mt(n.dq_full[...], n.w_v[:, 0 : n.wq.shape[1]])
        n.vec_own[2:3], n.vec_own[3:4] = norm_back_rows(n.lat_v, L, M, 1, n.dres_v)
        begin([lat_out])
        n.vec_own[4:6] = n.fvec[0:2]
        n.vec_own[6:8] = jnp.zeros((2, D), F32)
        begin(vec_head)
        begin(out_far)

    def vectors_middle():
        arrived(vec_head)
        total = n.vec_own[...]
        for k in range(1, H):
            total = total + n.vec_head[k - 1]
        for z in range(nz):
            n.vec_sum[z] = total[:, z * span : (z + 1) * span]
        begin(vec_z)

    def own_output():
        arrived(out_far)
        total = n.out_own_v[...]
        for d in range(1, ny):
            total = total + n.out_recv[d - 1].astype(F32)
        n.out_own_v[...] = total
        begin([own_out])

    before, middle, after = [{index: [] for index in range(count)} for _ in range(3)]

    def late_quarters():
        for dz, dx in order[near:]:
            arrived([x_quarters[dz][nx - dx - 1]])
            begin(y_quarters[dz, dx])

    for index in range(count):
        before[index] += [lambda index=index: io.moved(*fetched[index])]
        if index + 1 < count and index != near - 1:
            before[index] += [lambda index=index: spread(index + 1)]
            middle[index] += [lambda index=index: fetch(index + 1)]
    middle[0] += [late_quarters]
    after[near - 1] += [lambda: sum_middle("kv", z_order[0]), out_middle]
    after[near - 1] += [lambda dz=dz: sum_middle("kv", dz) for dz in z_order[1:2]]
    after[near - 1] += [own_gradients]
    after[near - 1] += [lambda dz=dz: sum_middle("kv", dz) for dz in z_order[2:]]
    after[near - 1] += [lambda: spread(near), lambda: fetch(near)]
    late = list(range(near, count))
    after[late[min(1, len(late) - 1)]] += [vectors_middle]
    for position, dz in enumerate(z_order):
        after[late[min(position + 1, len(late) - 1)]] += [lambda dz=dz: sum_middle("query", dz)]
    after[late[-1]] += [own_output]
    spread(0)
    fetch(0)
    io.moved(*ffn_loads)

    def at_index(index, actions):
        for k in range(count):
            if actions[k]:

                @pl.when(index == k)
                def _():
                    for action in actions[k]:
                        action()

    def group_step(index, carry):
        at_index(index, before)
        buf = lax.rem(index + 1, 2)
        value, slope = gelu_pair(mm(n.ffn_v[buf], n.wup_v[...]))
        n.down_acc[...] += tm(n.dout_v[buf, :, window], value.astype(BF))
        n.slope[...] = slope
        at_index(index, middle)
        d_hidden = (mt(n.dout_v[buf], n.wdown_v[...]) * n.slope[...]).astype(BF)
        n.up_acc[...] += tm(n.ffn_v[buf, :, window], d_hidden)
        at_index(index, after)
        return carry

    lax.fori_loop(0, count, group_step, 0)
    arrived(vec_z)
    total = n.vec_sum[at.z]
    for d in range(1, nz):
        total = total + n.vec_z[d - 1]
    n.vec_part[...] = total
    vec_x = [io.put(n.vec_part, n.vec_x.at[d - 1], at.on_x(d)) for d in range(1, nx)]
    own_rows = pl.ds(pl.multiple_of(offset, 8), B)
    io.move(n.up_acc.at[own_rows], n.up_grad)
    io.move(n.down_acc.at[own_rows], n.down_grad)
    out_end()
    sum_end("kv", [(n.grad_v.at[1], n.key_grad), (n.grad_v.at[2], n.value_grad)])
    arrived(vec_x)
    total = n.vec_part[...]
    for d in range(1, nx):
        total = total + n.vec_x[d - 1]
    n.vec_done[...] = total
    io.move(n.vec_done, n.vec_o)
    sum_end("query", [(n.grad_v.at[3], n.query_grad)])
    io.finish()


def backward(s, ins):
    t = sizes_of(s)
    ny, nc, nz, nx, G, H = t.ny, t.nc, t.nz, t.nx, t.G, t.H
    M, L, LR, GL, ML, D, E, F, B = t.M, t.L, t.LR, t.GL, t.ML, t.D, t.E, t.F, t.B
    fx, fz, fh = max(nx - 1, 1), max(nz - 1, 1), max(H - 1, 1)
    span = D // nz
    outs = dict(
        media_o=((M, D), F32), lat_o=((L, D), F32), query_grad=((B, E), F32), key_grad=((B, E), F32), value_grad=((B, E), F32),
        out_grad=((B, E), F32), up_grad=((B, F), F32), down_grad=((B, F), F32), vec_o=((8, span), F32), out_o=((L, D), F32),
        fall_b=((s.rows, GL, D), BF), dall_b=((s.rows, ny * L, D), BF),
    )
    scratch = dict(
        mix_v=((H, GL, E), BF), wout_v=((E, D), BF), dcols_v=((GL, E), BF), dmixed=((G, LR, E), BF),
        keys_v=((G, t.KC, E), BF), values_v=((G, t.KC, E), BF), query_v=((G, LR, E), BF), norm_v=((H * ML, D), BF),
        ffn_v=((2, GL, D), BF), dout_v=((2, GL, D), BF), wup_v=((D, F), BF),
        wdown_v=((F, D), BF), w_v=((D, max(2 * D, H * t.EP)), BF), media_v=((M, D), BF), lat_v=((L, D), BF), dres_v=((L, D), F32),
        dkv=((H * ML, 2 * E), BF), dq=((H * L, t.EP), BF), turn_kv=((H, L, 2 * E), F32), turn_q=((H, L, t.EP), F32),
        dkv_full=((ML, 2 * D), BF), dq_full=((L, H * t.EP), BF), grad_v=((4, B, E), F32), up_acc=((256, F), F32),
        down_acc=((256, F), F32), drow=((ML, D), F32), slope=((GL, F), F32), vec_own=((8, D), F32), vec_head=((fh, 8, D), F32),
        vec_sum=((nz, 8, span), F32), vec_z=((fz, 8, span), F32), vec_part=((8, span), F32), vec_x=((fx, 8, span), F32),
        vec_done=((8, span), F32), vecs=((8, D), F32), out_own_v=((L, D), F32), out_recv=((max(ny - 1, 1), L, D), BF),
        p_out=((nz, nx, B, E), BF), zr_out=((fz, nx, B, E), BF), xr_out=((fx, B, E), BF),
    )
    for w, lanes in (("kv", 2 * E), ("query", E)):
        scratch["p_" + w] = ((nz, nx, B, lanes), BF)
        scratch["xr_" + w] = ((nz, fx, B, lanes), BF)
        scratch["zr_" + w] = ((fz, B, lanes), BF)
    places = {"fvec": VMEM}
    cost = pl.CostEstimate(flops=30 * 10**9, bytes_accessed=8 * 10**7, transcendentals=10**6)
    return call(backward_kernel, s, "backward", 2, ins, outs, scratch, 300, places, 63, cost)


def finish_kernel(count, *refs):
    ins, outs, held = refs[:count], refs[count : 2 * count], refs[2 * count : 3 * count]
    read, write = refs[3 * count :]
    loads = [pltpu.make_async_copy(a, b, read.at[i]) for i, (a, b) in enumerate(zip(ins, held))]
    stores = [pltpu.make_async_copy(a, b, write.at[i]) for i, (a, b) in enumerate(zip(held, outs))]
    for copy in loads:
        copy.start()
    for load, store in zip(loads, stores):
        load.wait()
        store.start()
    for copy in stores:
        copy.wait()


def finish(arrays):
    count = len(arrays)
    return pl.pallas_call(
        functools.partial(finish_kernel, count),
        name="finish",
        out_shape=[jax.ShapeDtypeStruct(a.shape, a.dtype) for a in arrays],
        in_specs=[ANY] * count,
        out_specs=[ANY] * count,
        scratch_shapes=[pltpu.VMEM(a.shape, a.dtype) for a in arrays] + [pltpu.SemaphoreType.DMA((count,))] * 2,
        compiler_params=pltpu.CompilerParams(vmem_limit_bytes=62 << 20),
    )(*arrays)


def body(
    media, latents, counts, media_gain, media_shift, latent_gain, latent_shift, w_query, w_key, w_value, w_out,
    ffn_gain, ffn_shift, w_up, w_down, cotangent,
):
    rows, heads = lax.axis_size("rows"), lax.axis_size("head")
    at = Place(rows, heads)
    images, patch, width = media.shape
    lat = latents.shape[1]
    cols = width // heads
    s = types.SimpleNamespace(
        rows=rows, heads=heads, images=images, patch=patch, lat=lat, width=width, cols=cols, mine=w_up.shape[1] // heads
    )
    t = sizes_of(s)

    def columns(array):
        return array if t.aligned else lax.dynamic_slice_in_dim(array, at.h * cols, cols, 1)

    gains = dict(
        media_gain=media_gain, media_shift=media_shift, latent_gain=latent_gain, latent_shift=latent_shift,
        ffn_gain=ffn_gain, ffn_shift=ffn_shift,
    )
    rows_in = dict(media=media.reshape(-1, width), lat=latents.reshape(-1, width))
    a = forward(
        s,
        dict(
            rows_in, cot=cotangent.reshape(-1, width), counts=counts, **gains, wq=columns(w_query), wk=columns(w_key),
            wv=columns(w_value), wout=w_out, wup=w_up, wdown=w_down,
        ),
    )
    ins = dict(
        rows_in, media_gain=gains["media_gain"], latent_gain=gains["latent_gain"], fvec=a["fvec_o"], dres=a["dres_o"],
        key_norm=a["key_norm_o"], keys=a["keys_o"], values=a["values_o"], query=a["query_o"], mixed=a["mixed_o"],
        dattn=a["dattn_o"], ffn=a["ffn_o"], dout=a["dout_o"], act=a["act_o"], dhid=a["dhid_o"], dall=a["dall"], fall=a["fall"],
        wout=w_out, wup=w_up, wdown=w_down, out_own=a["out_o"], out_send=a["out_send_o"],
    )
    if t.aligned:
        ins.update(wk=w_key, wv=w_value, wq=w_query)
    else:
        pair = jnp.stack([w_key.reshape(width, heads, cols), w_value.reshape(width, heads, cols)], axis=2)
        padded = jnp.pad(w_query.reshape(width, heads, cols), ((0, 0), (0, 0), (0, t.EP - cols)))
        ins.update(wkv=pair.reshape(width, 2 * width), wq=padded.reshape(width, -1), dattn_cols=columns(a["dattn_o"]))
    b = backward(s, ins)
    share = width // (rows * heads)
    vector = lax.dynamic_slice_in_dim(b["vec_o"], (at.x * heads + at.h) * share, share, 1)
    names = ("out_o", "media_o", "lat_o", "query_grad", "key_grad", "value_grad", "out_grad", "up_grad", "down_grad")
    out, media_grad, latents_grad, query_grad, key_grad, value_grad, out_grad, up_grad, down_grad = finish([b[k] for k in names])
    return (
        out.reshape(latents.shape), media_grad.reshape(media.shape), latents_grad.reshape(latents.shape), vector[0], vector[1],
        vector[2], vector[3], query_grad, key_grad, value_grad, out_grad, vector[4], vector[5], up_grad, down_grad.T,
    )


def solution(mesh):
    row = P("rows", "head", None)
    whole = P()
    vector = P(("rows", "head"))
    grid = P("rows", "head")
    return jax.shard_map(
        body,
        mesh=mesh,
        in_specs=(row, row) + (whole,) * 13 + (row,),
        out_specs=(row, row, row, vector, vector, vector, vector, grid, grid, grid, grid, vector, vector, grid, P("head", "rows")),
        check_vma=False,
    )
```

```python
import functools
import math
import types

import jax
import jax.numpy as jnp
from jax import lax
from jax.experimental import pallas as pl
from jax.experimental.pallas import tpu as pltpu
from jax.sharding import PartitionSpec as P

HEAD_DIM = 96
MAX_IMG = 8
EPSILON = 1e-05
BF = jnp.bfloat16
F32 = jnp.float32
MESH = pl.DeviceIdType.MESH
ANY = pl.BlockSpec(memory_space=pl.ANY)
VMEM = pl.BlockSpec(memory_space=pltpu.VMEM)
SMEM = pl.BlockSpec(memory_space=pltpu.SMEM)


def factor_rows(count):
    nz = 4 if count % 4 == 0 else 1
    return nz, count // nz


def factor_head(count):
    nc = 2 if count % 2 == 0 else 1
    return count // nc, nc


def mm(a, b):
    return lax.dot_general(a, b, (((1,), (0,)), ((), ())), preferred_element_type=F32)


def mt(a, b):
    return lax.dot_general(a, b, (((1,), (1,)), ((), ())), preferred_element_type=F32)


def tm(a, b):
    return lax.dot_general(a, b, (((0,), (0,)), ((), ())), preferred_element_type=F32)


class Place:
    def __init__(self, rows, heads):
        self.rows, self.heads = rows, heads
        self.nz, self.nx = factor_rows(rows)
        self.ny, self.nc = factor_head(heads)
        self.r = lax.axis_index("rows")
        self.h = lax.axis_index("head")
        self.z, self.x = lax.div(self.r, self.nx), lax.rem(self.r, self.nx)
        self.y, self.c = lax.div(self.h, self.nc), lax.rem(self.h, self.nc)
        self.zs, self.xs, self.ys = [
            [self.turn(at, d, size) for d in range(size)]
            for at, size in ((self.z, self.nz), (self.x, self.nx), (self.y, self.ny))
        ]
        self.other = self.nc - 1 - self.c
        self.groups = [[z * self.nx + x for x in self.xs] for z in self.zs]
        self.slots = [y * self.nc + c for y in self.ys for c in (self.c, self.other)[: self.nc]]
        self.partner = (self.r, self.y * self.nc + self.other)

    @staticmethod
    def turn(at, d, size):
        if d == 0:
            return at
        there = at + d
        return jnp.where(there >= size, there - size, there)

    def group(self, dz, dx):
        return self.groups[dz % self.nz][dx % self.nx]

    def on_y(self, d):
        return self.r, self.slots[d * self.nc]

    def on_x(self, d):
        return self.group(0, d), self.h

    def on_z(self, d):
        return self.group(d, 0), self.h

    def greet(self):
        peers = [(self.r, head) for head in self.slots[1:]]
        peers += [self.on_x(d) for d in range(1, self.nx)] + [self.on_z(d) for d in range(1, self.nz)]
        barrier = pltpu.get_barrier_semaphore()
        for peer in peers:
            pl.semaphore_signal(barrier, inc=1, device_id=peer, device_id_type=MESH)
        pl.semaphore_wait(barrier, len(peers))


class Copies:
    def __init__(self, at, send, recv, local):
        self.at, self.send, self.recv, self.local = at, send, recv, local
        self.used, self.used_local = 0, 0
        self.unsent, self.open = [], []

    def plan(self, src, dst, peer):
        copy = pltpu.make_async_remote_copy(
            src_ref=src,
            dst_ref=dst,
            send_sem=self.send.at[self.used],
            recv_sem=self.recv.at[self.used],
            device_id=peer,
            device_id_type=MESH,
        )
        self.used += 1
        self.unsent.append(copy)
        return copy

    def put(self, src, dst, peer):
        copy = self.plan(src, dst, peer)
        copy.start()
        return copy

    def put_y(self, src, dst):
        return [self.put(src, dst, self.at.on_y(d)) for d in range(1, self.at.ny)]

    def put_x(self, src, dst):
        return [self.put(src, dst, self.at.on_x(d)) for d in range(1, self.at.nx)]

    def put_z(self, src, dst):
        return [self.put(src, dst, self.at.on_z(d)) for d in range(1, self.at.nz)]

    def put_core(self, src, dst):
        return [self.put(src, dst, self.at.partner)] if self.at.nc > 1 else []

    def sent(self, copies):
        for copy in copies:
            copy.wait_send()
        self.unsent = [c for c in self.unsent if all(c is not d for d in copies)]

    def plan_move(self, src, dst):
        copy = pltpu.make_async_copy(src, dst, self.local.at[self.used_local])
        self.used_local += 1
        self.open.append(copy)
        return copy

    def move(self, src, dst):
        copy = self.plan_move(src, dst)
        copy.start()
        return copy

    def moved(self, *copies):
        for copy in copies:
            copy.wait()
        self.open = [c for c in self.open if all(c is not d for d in copies)]

    def finish(self):
        for copy in self.unsent:
            copy.wait_send()
        for copy in self.open:
            copy.wait()


def begin(copies):
    for copy in copies:
        copy.start()


def arrived(copies):
    for copy in copies:
        copy.wait_recv()


def norm_rows(block):
    mean = jnp.mean(block, axis=-1, keepdims=True)
    centered = block - mean
    scale = lax.rsqrt(jnp.mean(centered * centered, axis=-1, keepdims=True) + EPSILON)
    return centered * scale, scale


def sweep(first, last, step, carry=0):
    together = next(k for k in (4, 2, 1) if (last - first) // 16 % k == 0)

    def turn(i, value):
        for j in range(together):
            start = first + i * (16 * together) + j * 16
            value = step(pl.ds(pl.multiple_of(start, 16), 16), value)
        return value

    return lax.fori_loop(0, (last - first) // (16 * together), turn, carry)


def gelu_pair(v):
    c = math.sqrt(2.0 / math.pi)
    square = v * v
    t = jnp.tanh(c * v * (1.0 + 0.044715 * square))
    half = 0.5 * (1.0 + t)
    slope = half + 0.5 * v * (1.0 - t * t) * (c * (1.0 + 3.0 * 0.044715 * square))
    return v * half, slope


def softmax(scores):
    powers = jnp.exp(scores - jnp.max(scores, axis=-1, keepdims=True))
    return powers * (1.0 / jnp.sum(powers, axis=-1, keepdims=True))


def head_mask(heads_here, rows, cols):
    col = lax.broadcasted_iota(jnp.int32, (rows, cols), 1)
    return jnp.concatenate(
        [((col >= j * HEAD_DIM) & (col < (j + 1) * HEAD_DIM)).astype(F32) for j in range(heads_here)], axis=0
    )


def spread_heads(block, mask):
    return jnp.concatenate([block] * (mask.shape[0] // block.shape[0]), axis=0) * mask


def gather_heads(block, mask, rows):
    block = block * mask
    return sum(block[j * rows : (j + 1) * rows] for j in range(block.shape[0] // rows))


def sizes_of(s):
    ny, nc = factor_head(s.heads)
    nz, nx = factor_rows(s.rows)
    t = types.SimpleNamespace(ny=ny, nc=nc, nz=nz, nx=nx, G=s.images, D=s.width, E=s.cols, F=s.mine, H=s.heads)
    t.pr, t.ll = s.patch, s.lat
    t.M, t.L, t.LR = t.G * t.pr, t.G * t.ll, t.H * t.ll
    t.GL, t.ML, t.KC = t.G * t.LR, t.M + t.L, t.H * t.pr + t.LR
    t.B = t.D // s.rows
    t.heads_here = t.E // HEAD_DIM
    t.aligned = t.E % 128 == 0
    t.EP = -(-t.E // 128) * 128
    t.by_rows = t.aligned and ny == 2 and nc == 2
    t.W = ny * t.E if t.by_rows else t.E
    t.wide_heads = t.W // HEAD_DIM
    return t


def forward_kernel(s, names, *refs):
    n = types.SimpleNamespace(**dict(zip(names, refs, strict=True)))
    at = Place(s.rows, s.heads)
    t = sizes_of(s)
    ny, nc, nz, nx, G, H = t.ny, t.nc, t.nz, t.nx, t.G, t.H
    M, L, LR, GL, ML, D, E, F, ll, pr = t.M, t.L, t.LR, t.GL, t.ML, t.D, t.E, t.F, t.ll, t.pr
    io = Copies(at, n.send, n.recv, n.local)
    here = at.r

    vectors = ("media_gain", "media_shift", "latent_gain", "latent_shift", "ffn_gain", "ffn_shift")
    load_vecs = [io.move(getattr(n, k), n.vecs.at[i]) for i, k in enumerate(vectors)]
    load_lat = io.move(n.lat, n.raw_l.at[0:L])
    load_cot = io.move(n.cot, n.cot_v)
    load_media = io.move(n.media, n.raw_m.at[0])

    def columns(weight):
        return weight.at[:, pl.ds(pl.multiple_of(at.h * E, 128), E)] if t.aligned else weight

    load_qkv = [io.move(columns(w), v.at[:, 0:E]) for w, v in ((n.wk, n.wk_v), (n.wv, n.wv_v), (n.wq, n.wq_v))]
    if t.by_rows:
        for w, v in ((n.wk, n.wk_v), (n.wv, n.wv_v), (n.wq, n.wq_v)):
            lanes = pl.ds(pl.multiple_of(at.slots[nc] * E, 128), E)
            load_qkv.append(io.move(w.at[:, lanes], v.at[:, E : 2 * E]))
    at.greet()

    bounds = [0, pr, M] if t.by_rows and G > 1 else [0, M // 2, M]
    chunks = len(bounds) - 1

    def far_slot(d):
        return (ny - d) % ny * nc

    def lat_rows(k):
        return n.raw_l.at[k * L : (k + 1) * L]

    lat_far = [io.put(n.lat, lat_rows(far_slot(d)), at.on_y(d)) for d in range(1, ny)]
    lat_near = io.put_core(n.lat, lat_rows(1 % H))
    media_far, media_near = [], []

    def send_patches(j):
        rows = slice(bounds[j], bounds[j + 1])
        media_far.append([io.put(n.media.at[rows], n.raw_m.at[far_slot(d), rows], at.on_y(d)) for d in range(1, ny)])

    for j in range(chunks):
        rows = slice(bounds[j], bounds[j + 1])
        media_near.append(io.put_core(n.media.at[rows], n.raw_m.at[1 % H, rows]))
    if not t.by_rows:
        for j in range(chunks):
            send_patches(j)

    io.moved(load_cot)
    for i in range(G):
        image = here * G + i
        limit = n.counts[lax.div(image, MAX_IMG)]
        live = jnp.where(lax.rem(image, MAX_IMG) < limit, 1.0, 0.0).astype(F32)
        rows = slice(i * ll, (i + 1) * ll)
        n.wide_l[rows] = n.cot_v[rows].astype(F32) * live
    n.dslot[at.y, at.c] = n.wide_l[...].astype(BF)
    own_d = n.dslot.at[at.y, at.c]

    def quarter(r, y):
        return r, pl.ds(pl.multiple_of(y * L, 16), L)

    def across(y, block):
        where = n.dall.at[quarter(here, y)]
        return io.put_z(block, where), io.put_x(block, where)

    z_far, x_far = {}, {}
    if t.by_rows:
        cot_far = io.put_y(own_d, own_d)
        cot_near = io.put_core(own_d, own_d)
        send_patches(0)
    z_far[0], x_far[0] = across(at.y, own_d)
    load_out = io.move(n.wout, n.wout_v)
    load_up = io.move(n.wup.at[:, pl.ds(pl.multiple_of(at.h * F, 128), F)], n.wup_v)
    load_down = io.move(n.wdown.at[pl.ds(pl.multiple_of(at.h * F, 16), F)], n.wdown_v)

    def forward_x(d, first=1, last=nz):
        for dz in range(first, last):
            z_far[d][dz - 1].wait_recv()
            block = n.dall.at[quarter(at.group(nz - dz, 0), at.ys[d])]
            x_far[d] += io.put_x(block, block)

    norm_busy = {}
    turn_count = [0]

    def patches(k, first, last):
        buf = turn_count[0] % 2
        turn_count[0] += 1
        if buf in norm_busy:
            io.moved(norm_busy[buf])

        def step(rows, carry):
            hat, _ = norm_rows(n.raw_m[k, rows].astype(F32))
            n.norm[buf, rows] = (hat * n.vecs[0:1] + n.vecs[1:2]).astype(BF)
            return carry

        sweep(first * 16, last * 16, step)
        rows = slice(first * 16, last * 16)
        for weight, result in ((n.wk_v, n.keys), (n.wv_v, n.values)):
            wide = mm(n.norm[buf, rows], weight[:, 0:E]).astype(BF)
            for i in range(first * 16 // pr, last * 16 // pr):
                base = i * pr - first * 16
                result[i, k * pr : (k + 1) * pr] = wide[base : base + pr]
        norm_busy[buf] = io.move(n.norm.at[buf, rows], n.key_norm_o.at[k * ML + first * 16 : k * ML + last * 16])

    io.moved(load_media, *load_qkv, *load_vecs)
    if t.by_rows:
        def near_patches(k, carry):
            @pl.when(k == 1)
            def _():
                for copies in media_near:
                    arrived(copies)

            def step(rows, value):
                hat, _ = norm_rows(n.raw_m[k, rows].astype(F32))
                n.norm[k, rows] = (hat * n.vecs[0:1] + n.vecs[1:2]).astype(BF)
                return value

            sweep(0, M, step)
            for weight, result, chip in ((n.wk_v, n.keys, n.keys_w), (n.wv_v, n.values, n.values_w)):
                wide = mm(n.norm[k], weight[...]).astype(BF)
                rows = pl.ds(pl.multiple_of(k * pr, 16), pr)
                for i in range(G):
                    result[i, rows] = wide[i * pr : (i + 1) * pr, 0:E]
                    chip[i, rows] = wide[i * pr : (i + 1) * pr]
            return carry

        lax.fori_loop(0, nc, near_patches, 0)
        for k in range(nc):
            norm_busy[k] = io.move(n.norm.at[k], n.key_norm_o.at[k * ML : k * ML + M])
    else:
        patches(0, 0, M // 16)
        if nc > 1:
            for copies in media_near:
                arrived(copies)
            patches(1, 0, M // 16)
    if not t.by_rows:
        cot_far = io.put_y(own_d, own_d)
        cot_near = io.put_core(own_d, own_d)
    relay = []
    for d, copy in zip(range(1, ny), lat_far):
        copy.wait_recv()
        k = far_slot(d)
        relay += io.put_core(lat_rows(k), lat_rows(k + 1)) if nc > 1 else []
    io.moved(load_lat)
    arrived(lat_near)
    arrived(relay)
    for k in range(H):
        wide = n.raw_l[k * L : (k + 1) * L].astype(F32)
        for i in range(G):
            n.resid[pl.ds(pl.multiple_of(i * LR + at.slots[k] * ll, 8), ll)] = wide[i * ll : (i + 1) * ll]

    def latent_step(rows, carry):
        hat, _ = norm_rows(n.raw_l[rows].astype(F32))
        n.lnorm[rows] = (hat * n.vecs[2:3] + n.vecs[3:4]).astype(BF)
        return carry

    sweep(0, H * L, latent_step)
    for k in range(H):
        io.move(n.lnorm.at[k * L : (k + 1) * L], n.key_norm_o.at[k * ML + M : (k + 1) * ML])
    for weight, result, chip in ((n.wq_v, n.query, n.query_w), (n.wk_v, n.keys, n.keys_w), (n.wv_v, n.values, n.values_w)):
        wide = mm(n.lnorm[...], weight[...])
        for k in range(H):
            for i in range(G):
                n.turn[pl.ds(pl.multiple_of(i * LR + at.slots[k] * ll, 8), ll)] = wide[k * L + i * ll : k * L + (i + 1) * ll]
        for i in range(G):
            block = n.turn[i * LR : (i + 1) * LR].astype(BF)
            if result is n.query:
                result[i] = block[:, 0:E]
                if t.by_rows:
                    chip[i] = block
            else:
                result[i, H * pr : t.KC] = block[:, 0:E]
                if t.by_rows:
                    pair = [wide[k * L + i * ll : k * L + (i + 1) * ll] for k in range(nc)]
                    chip[i, nc * pr : nc * (pr + ll)] = jnp.concatenate(pair, axis=0).astype(BF)

    def far_patches(j):
        relays = []
        rows = slice(bounds[j], bounds[j + 1])
        for d, copy in zip(range(1, ny), media_far[j]):
            copy.wait_recv()
            k = far_slot(d)
            relays.append(io.put_core(n.raw_m.at[k, rows], n.raw_m.at[k + 1, rows]) if nc > 1 else [])
        for d in range(1, ny):
            patches(far_slot(d), bounds[j] // 16, bounds[j + 1] // 16)
        for d in range(1, ny):
            if nc > 1:
                arrived(relays[d - 1])
                patches(far_slot(d) + 1, bounds[j] // 16, bounds[j + 1] // 16)

    cot_relay = []

    def far_cotangents():
        arrived(cot_far)
        for d in range(1, ny):
            block = n.dslot.at[at.ys[d], at.c]
            cot_relay.extend(io.put_core(block, block))

    def cross_cotangents():
        for d in range(1, ny):
            z_far[d], x_far[d] = across(at.ys[d], n.dslot.at[at.ys[d], at.c])

    def group_cotangents():
        arrived(cot_near)
        arrived(cot_relay)
        for y in range(ny):
            for c in range(nc):
                wide = n.dslot[y, c].astype(F32)
                for i in range(G):
                    n.part[i * LR + (y * nc + c) * ll : i * LR + (y * nc + c + 1) * ll] = wide[i * ll : (i + 1) * ll]
        n.dout[...] = n.part[...].astype(BF)
        io.move(n.dout, n.dout_o)

    def add_mixed(head):
        n.resid[...] += mm(n.mix[head], n.wout_v[pl.ds(pl.multiple_of(head * E, 16), E)])

    scale = 1.0 / math.sqrt(HEAD_DIM)
    mask = head_mask(t.wide_heads, LR, t.W)
    mask_low = mask.astype(BF)
    if t.by_rows:
        far_cotangents()
        lane = lax.broadcasted_iota(jnp.int32, (LR, 128), 1)
        for i in range(G):
            scores = mt(spread_heads(n.query_w[i], mask_low), n.keys_w[i]) * scale
            top = jnp.max(scores, axis=-1, keepdims=True)
            powers = jnp.exp(scores - top)
            total = jnp.sum(powers, axis=-1, keepdims=True)
            mixed = gather_heads(mm(powers.astype(BF), n.values_w[i]) * (1.0 / total), mask, LR)
            rows = slice(i * LR, (i + 1) * LR)
            n.o_send[rows] = mixed.astype(BF)
            log_total = top + jnp.log(total)
            stats = jnp.zeros((LR, 128), F32)
            for j in range(t.wide_heads):
                one = log_total[j * LR : (j + 1) * LR]
                high = one.astype(BF).astype(F32)
                stats = jnp.where(lane == j, high, stats)
                stats = jnp.where(lane == j + t.wide_heads, one - high, stats)
            n.l_send[rows] = stats.astype(BF)
        o_far = io.put_y(n.o_send, n.o_recv) + io.put_y(n.l_send, n.l_recv)
        send_patches(1)
        row = lax.broadcasted_iota(jnp.int32, (128, t.W), 0)
        col = lax.broadcasted_iota(jnp.int32, (128, t.W), 1)
        widen = jnp.zeros((128, t.W), F32)
        for j in range(t.wide_heads):
            inside = (col >= j * HEAD_DIM) & (col < (j + 1) * HEAD_DIM)
            widen = jnp.where(inside & ((row == j) | (row == j + t.wide_heads)), 1.0, widen)
        widen = widen.astype(BF)

        def other_chip(block):
            return jnp.concatenate([block[:, E : 2 * E], block[:, 0:E]], axis=-1)

        far_patches(0)
        group_cotangents()
        io.moved(load_out, load_up, load_down)
        forward_x(0)
        cross_cotangents()
        arrived(o_far)
        def merge(i, carry):
            rows = pl.ds(pl.multiple_of(i * LR, 16), LR)
            near_log, far_log = mm(n.l_send[rows], widen), other_chip(mm(n.l_recv[rows], widen))
            top = jnp.maximum(near_log, far_log)
            near_part, far_part = jnp.exp(near_log - top), jnp.exp(far_log - top)
            mixed = n.o_send[rows].astype(F32) * near_part + other_chip(n.o_recv[rows].astype(F32)) * far_part
            mixed = mixed * (1.0 / (near_part + far_part))
            for d in range(ny):
                n.mix[at.slots[d * nc], rows] = mixed[:, d * E : (d + 1) * E].astype(BF)
            return carry

        lax.fori_loop(0, G, merge, 0)
        mix_near = [io.put_core(n.mix.at[at.slots[d * nc]], n.mix.at[at.slots[d * nc]]) for d in range(ny)]
        def add_core(core, carry):
            @pl.when(core == 1)
            def _():
                for copies in mix_near:
                    arrived(copies)

            for d in range(ny):
                add_mixed(jnp.where(core == 0, at.slots[d * nc], at.slots[d * nc + 1]))
            return carry

        lax.fori_loop(0, nc, add_core, 0)
    else:
        for j in range(chunks):
            far_patches(j)
        far_cotangents()
        cross_cotangents()
        forward_x(0)
        for i in range(G):
            scores = mt(spread_heads(n.query[i], mask_low), n.keys[i]) * scale
            probs = softmax(scores).astype(BF)
            mixed = gather_heads(mm(probs, n.values[i]), mask, LR)
            n.mix[at.h, i * LR : (i + 1) * LR] = mixed.astype(BF)
        mix_far = io.put_y(n.mix.at[at.h], n.mix.at[at.h])
        mix_near = io.put_core(n.mix.at[at.h], n.mix.at[at.h])
        io.moved(load_out, load_up, load_down)
        add_mixed(at.h)
        arrived(mix_near)
        if nc > 1:
            add_mixed(at.slots[1])
        group_cotangents()
        mix_relay = []
        for d, copy in zip(range(1, ny), mix_far):
            copy.wait_recv()
            block = n.mix.at[at.slots[far_slot(d)]]
            mix_relay.append(io.put_core(block, block))
        for d in range(1, ny):
            add_mixed(at.slots[far_slot(d)])
        for d in range(1, ny):
            if nc > 1:
                arrived(mix_relay[d - 1])
                add_mixed(at.slots[far_slot(d) + 1])
    io.move(n.mix, n.mixed_o)
    gain, shift = n.vecs[4:5], n.vecs[5:6]

    def ffn_step(rows, carry):
        hat, inv = norm_rows(n.resid[rows])
        n.hat[rows] = hat
        n.inv[rows] = jnp.broadcast_to(inv, (16, 128))
        n.ffn[rows] = (hat * n.vecs[4:5] + n.vecs[5:6]).astype(BF)
        return carry

    sweep(0, GL, ffn_step)
    io.move(n.ffn, n.ffn_o)

    def own_rows(ref):
        return jnp.concatenate([ref[pl.ds(pl.multiple_of(i * LR + at.h * ll, 8), ll)] for i in range(G)], axis=0)

    n.fq[...] = (own_rows(n.hat) * gain + shift).astype(BF)
    own_f = n.fall.at[at.z]
    ffn_far = io.put_z(n.fq, own_f)
    io.move(n.fq, own_f)
    value, slope = gelu_pair(mm(n.ffn[...], n.wup_v[...]))
    n.act[...] = value.astype(BF)
    n.dhid[...] = (mt(n.dout[...], n.wdown_v[...]) * slope).astype(BF)
    n.part[...] = mt(n.dhid[...], n.wup_v[...])
    half = GL // nc
    theirs = pl.ds(pl.multiple_of((nc - 1 - at.c) * half, 16), half)
    swap = io.put_core(n.part.at[theirs], n.c_recv)
    io.move(n.act, n.act_o)
    io.move(n.dhid, n.dhid_o)
    out_part = mm(n.act[...], n.wdown_v[...])
    for i in range(G):
        for head in range(H):
            base = i * LR + head * ll
            n.outp[head % nc, head // nc, i * ll : (i + 1) * ll] = out_part[base : base + ll]
    out_swap = io.put_core(n.outp.at[nc - 1 - at.c], n.oc_recv)
    for d in range(1, ny):
        forward_x(d)
    arrived(swap)
    pieces = 2
    piece = half // pieces
    sum_far = []
    for j in range(pieces):
        rows = slice(j * piece, (j + 1) * piece)
        total = n.part[pl.ds(pl.multiple_of(at.c * half + j * piece, 16), piece)]
        if nc > 1:
            total = total + n.c_recv[rows]
        n.y_send[rows] = total.astype(BF)
        sum_far.append([io.put(n.y_send.at[rows], n.y_recv.at[d - 1, rows], at.on_y(d)) for d in range(1, ny)])
    io.sent(swap)
    if t.by_rows:
        far_patches(1)
    arrived(out_swap)
    for y in range(ny):
        total = n.outp[at.c, y]
        if nc > 1:
            total = total + n.oc_recv[y]
        n.outp[at.c, y] = total
        n.oy_send[y] = total.astype(BF)
    for ref, out in ((n.keys, n.keys_o), (n.values, n.values_o), (n.query, n.query_o)):
        io.move(ref, out)

    def residual_back(ref, base, first, last):
        def step(from_rows, carry):
            rows = pl.ds(pl.multiple_of(base + from_rows.start, 16), 16)
            grad = ref[from_rows]
            hat, inv = n.hat[rows], n.inv[rows, 0:1]
            n.part[rows] = grad
            scaled = grad * n.vecs[4:5]
            first = jnp.mean(scaled, axis=-1, keepdims=True)
            second = jnp.mean(scaled * hat, axis=-1, keepdims=True)
            d_res = n.dout[rows].astype(F32) + inv * (scaled - first - hat * second)
            n.resid[rows] = d_res
            n.dattn[rows] = d_res.astype(BF)
            return carry

        sweep(first, last, step)

    n.own[0] = n.outp[at.c, at.y] + own_rows(n.resid)
    io.move(n.own.at[0], n.out_o)
    io.move(n.oy_send, n.out_send_o)
    share = []
    for j in range(pieces):
        rows = slice(j * piece, (j + 1) * piece)
        arrived(sum_far[j])
        total = n.y_send[rows].astype(F32)
        for d in range(1, ny):
            total = total + n.y_recv[d - 1, rows].astype(F32)
        n.share[rows] = total
        share.append(io.put_core(n.share.at[rows], n.s_recv.at[rows]))
        residual_back(n.share, at.c * half, j * piece, (j + 1) * piece)
    if nc > 1:
        for j in range(pieces):
            arrived(share[j])
            residual_back(n.s_recv, (nc - 1 - at.c) * half, j * piece, (j + 1) * piece)
    io.move(n.dattn, n.dattn_o)
    n.own[1] = own_rows(n.resid)
    io.move(n.own.at[1], n.dres_o)
    grad = own_rows(n.part)
    n.fvec[0:1] = jnp.sum(grad * own_rows(n.hat), axis=0, keepdims=True)
    n.fvec[1:2] = jnp.sum(grad, axis=0, keepdims=True)
    n.fvec[2:8] = jnp.zeros((6, D), F32)
    io.move(n.fvec, n.fvec_o)
    for d in range(ny):
        arrived(x_far[d])
    arrived(ffn_far)
    io.finish()


def call(kernel, s, name, ident, ins, outs, scratch, semaphores, places, limit, cost):
    names = list(ins) + list(outs) + list(scratch) + ["send", "recv", "local"]
    dma = [pltpu.SemaphoreType.DMA((count,)) for count in (semaphores, semaphores, 120)]
    result = pl.pallas_call(
        functools.partial(kernel, s, names),
        name=name,
        out_shape=[jax.ShapeDtypeStruct(*o) for o in outs.values()],
        in_specs=[places.get(k, ANY) for k in ins],
        out_specs=[ANY] * len(outs),
        scratch_shapes=[pltpu.VMEM(*v) for v in scratch.values()] + dma,
        compiler_params=pltpu.CompilerParams(collective_id=ident, has_side_effects=True, vmem_limit_bytes=limit << 20),
        cost_estimate=cost,
    )(*ins.values())
    return dict(zip(outs, result, strict=True))


def forward(s, ins):
    t = sizes_of(s)
    ny, nc, G, H, M, L, LR, GL, ML, D, E, F = t.ny, t.nc, t.G, t.H, t.M, t.L, t.LR, t.GL, t.ML, t.D, t.E, t.F
    half = GL // nc
    far, W = max(ny - 1, 1), t.W
    outs = dict(
        out_o=((L, D), F32), dres_o=((L, D), F32), fvec_o=((8, D), F32), key_norm_o=((H * ML, D), BF),
        keys_o=((G, t.KC, E), BF), values_o=((G, t.KC, E), BF), query_o=((G, LR, E), BF), mixed_o=((H, GL, E), BF),
        dattn_o=((GL, D), BF), ffn_o=((GL, D), BF), dout_o=((GL, D), BF), act_o=((GL, F), BF), dhid_o=((GL, F), BF),
        dall=((s.rows, ny * L, D), BF), fall=((t.nz, L, D), BF), out_send_o=((ny, L, D), BF),
    )
    scratch = dict(
        vecs=((8, D), F32), cot_v=((L, D), BF), wide_l=((L, D), F32), raw_m=((H, M, D), BF), raw_l=((H * L, D), BF), dslot=((ny, nc, L, D), BF),
        norm=((2, M, D), BF), lnorm=((H * L, D), BF), turn=((GL, W), F32), keys=((G, t.KC, E), BF), values=((G, t.KC, E), BF),
        query=((G, LR, E), BF), mix=((H, GL, E), BF), resid=((GL, D), F32), hat=((GL, D), F32), inv=((GL, 128), F32),
        ffn=((GL, D), BF), dout=((GL, D), BF), act=((GL, F), BF), dhid=((GL, F), BF), part=((GL, D), F32),
        outp=((nc, ny, L, D), F32), c_recv=((half, D), F32), oc_recv=((ny, L, D), F32), y_send=((half, D), BF),
        y_recv=((far, half, D), BF), oy_send=((ny, L, D), BF), share=((half, D), F32),
        s_recv=((half, D), F32), fq=((L, D), BF), own=((2, L, D), F32), dattn=((GL, D), BF),
        fvec=((8, D), F32), wq_v=((D, W), BF), wk_v=((D, W), BF), wv_v=((D, W), BF), wout_v=((D, D), BF),
        wup_v=((D, F), BF), wdown_v=((F, D), BF),
    )
    shape = (G, nc * (t.pr + t.ll), W) if t.by_rows else (1, 16, 128)
    rows = (GL, W) if t.by_rows else (16, 128)
    scratch.update(
        keys_w=(shape, BF), values_w=(shape, BF), query_w=((G, LR, W) if t.by_rows else shape, BF), o_send=(rows, BF),
        o_recv=(rows, BF), l_send=((rows[0], 128), BF), l_recv=((rows[0], 128), BF),
    )
    places = {"counts": SMEM}
    cost = pl.CostEstimate(flops=8 * 10**9, bytes_accessed=4 * 10**7, transcendentals=10**6)
    return call(forward_kernel, s, "forward", 1, ins, outs, scratch, 200, places, 62, cost)


def window_of(position, block, width):
    base = jnp.minimum(position * block // 128 * 128, width - 256)
    return pl.multiple_of(base, 128), position * block - base


def backward_kernel(s, names, *refs):
    n = types.SimpleNamespace(**dict(zip(names, refs, strict=True)))
    at = Place(s.rows, s.heads)
    t = sizes_of(s)
    ny, nc, nz, nx, G, H = t.ny, t.nc, t.nz, t.nx, t.G, t.H
    M, L, LR, GL, ML, D, E, F, ll, pr, B = t.M, t.L, t.LR, t.GL, t.ML, t.D, t.E, t.F, t.ll, t.pr, t.B
    here = at.r
    io = Copies(at, n.send, n.recv, n.local)

    def quarter(r, y):
        return r, pl.ds(pl.multiple_of((at.c * ny + y) * L, 16), L)

    aligned = t.aligned
    first_loads = [io.move(n.dattn, n.ffn_v.at[1]), io.move(n.mixed, n.mix_v)]
    first_loads.append(io.move(n.wout.at[pl.ds(pl.multiple_of(at.h * E, 16), E)], n.wout_v))
    if aligned:
        first_loads.append(io.move(n.dattn.at[:, pl.ds(pl.multiple_of(at.h * E, 128), E)], n.dcols_v))
    else:
        first_loads.append(io.move(n.dattn_cols, n.dcols_v))
    attend_loads = [io.move(getattr(n, k), getattr(n, k + "_v")) for k in ("keys", "values", "query")]
    norm_load = io.move(n.key_norm, n.norm_v)
    own_loads = [io.move(n.act, n.dout_v.at[1, :, 0:F]), io.move(n.ffn, n.ffn_v.at[0]), io.move(n.dout, n.dout_v.at[0])]
    ffn_loads = [io.move(n.wup.at[:, pl.ds(pl.multiple_of(at.h * F, 128), F)], n.wup_v)]
    ffn_loads.append(io.move(n.wdown.at[pl.ds(pl.multiple_of(at.h * F, 16), F)], n.wdown_v))
    if aligned:
        row_loads = []
        for head in range(H):
            for j, weight in enumerate((n.wk, n.wv)):
                lanes = slice((2 * head + j) * E, (2 * head + j + 1) * E)
                row_loads.append(io.move(weight.at[:, head * E : (head + 1) * E], n.w_v.at[:, lanes]))
    else:
        row_loads = [io.move(n.wkv, n.w_v)]
    row_loads += [io.move(n.media_gain, n.vecs.at[0]), io.move(n.latent_gain, n.vecs.at[1]), io.move(n.out_own, n.out_own_v)]
    row_loads += [io.move(n.media, n.media_v), io.move(n.lat, n.lat_v), io.move(n.dres, n.dres_v)]
    at.greet()

    x_quarters = []
    for dz in range(nz):
        source = n.fall.at[at.zs[dz]]
        x_quarters.append(io.put_x(source, n.fall_b.at[quarter(at.group(dz, 0), at.y)]))
    y_quarters = {}
    for dz in range(1, nz):
        source = n.fall.at[at.zs[dz]]
        y_quarters[dz, 0] = io.put_y(source, n.fall_b.at[quarter(at.group(dz, 0), at.y)])

    def core_rows(c):
        return pl.ds(pl.multiple_of(c * ny * L, 16), ny * L)

    for dx in range(1, nx):
        for dz in range(nz):
            block = n.fall_b.at[quarter(at.group(dz, nx - dx), at.y)]
            y_quarters[dz, nx - dx] = [io.plan(block, block, at.on_y(d)) for d in range(1, ny)]
    order = [(dz, 0) for dz in range(1, nz)] + [(dz, nx - dx) for dx in range(1, nx) for dz in range(nz)]
    near, count = nz - 1, len(order)
    to_core, fetched = [], []
    for index, (dz, dx) in enumerate(order):
        r = at.group(dz, dx)
        buf = (index + 1) % 2
        copies = [io.plan(n.dall.at[r], n.dall_b.at[r], at.partner)] if nc > 1 else []
        for d in range(ny):
            block = n.fall_b.at[quarter(r, at.ys[d])]
            source = n.fall.at[at.zs[dz]] if (d == 0 and dx == 0) else block
            copies += [io.plan(source, block, at.partner)] if nc > 1 else []
        to_core.append(copies)
        copies = []
        for c in range(nc):
            rows = core_rows(at.c if c == 0 else nc - 1 - at.c)
            source = n.dall if c == 0 else n.dall_b
            copies.append(io.plan_move(source.at[r], n.dout_v.at[buf, rows]))
        if dx > 0:
            copies.append(io.plan_move(n.fall_b.at[r], n.ffn_v.at[buf]))
        else:
            for slot in range(H):
                core = at.c if slot % nc == 0 else at.other
                rows = pl.ds(pl.multiple_of((core * ny + at.ys[slot // nc]) * L, 16), L)
                source = n.fall.at[at.zs[dz]] if slot == 0 else n.fall_b.at[r, rows]
                copies.append(io.plan_move(source, n.ffn_v.at[buf, rows]))
        fetched.append(copies)

    def spread(index):
        arrived(y_quarters[order[index]])
        begin(to_core[index])

    def fetch(index):
        if index < count:
            arrived(to_core[index])
            begin(fetched[index])

    io.moved(*first_loads)
    n.dmixed[...] = mt(n.ffn_v[1], n.wout_v[...]).astype(BF).reshape(G, LR, E)
    own_loads.append(io.move(n.dhid, n.ffn_v.at[1, :, 0:F]))
    span = nx * B
    if E == span:
        tiles = [tm(n.mix_v[z], n.dcols_v[...]) for z in range(nz)]
    else:
        whole = jnp.concatenate([n.mix_v[head] for head in range(H)], axis=-1)
        tiles = [tm(whole[:, z * span : (z + 1) * span], n.dcols_v[...]) for z in range(nz)]
    for z in range(nz):
        for x in range(nx):
            n.p_out[z, x] = tiles[z][x * B : (x + 1) * B].astype(BF)
    out_x = [io.plan(n.p_out.at[at.z, at.xs[d]], n.xr_out.at[d - 1], at.on_x(d)) for d in range(1, nx)]
    out_z = [io.put(n.p_out.at[at.zs[d]], n.zr_out.at[d - 1], at.on_z(d)) for d in range(1, nz)]

    def out_middle():
        arrived(out_z)
        total = n.p_out[at.z].astype(F32)
        for d in range(1, nz):
            total = total + n.zr_out[d - 1].astype(F32)
        n.p_out[at.z] = total.astype(BF)
        begin(out_x)

    def out_end():
        arrived(out_x)
        total = n.p_out[at.z, at.x].astype(F32)
        for d in range(1, nx):
            total = total + n.xr_out[d - 1].astype(F32)
        n.grad_v[0] = total
        io.move(n.grad_v.at[0], n.out_grad)

    parts = {"kv": (n.p_kv, n.xr_kv, n.zr_kv), "query": (n.p_query, n.xr_query, n.zr_query)}
    x_parts, z_parts = {}, {}
    z_order = list(range(1, nz)) + [0]

    def sum_start(w, rows, grads):
        part, x_recv = parts[w][:2]
        for dz in z_order:
            lanes = pl.ds(pl.multiple_of(at.zs[dz] * span, 128), span)
            tile = tm(rows(lanes), grads)
            for x in range(nx):
                part[dz, x] = tile[x * B : (x + 1) * B].astype(BF)
            z_parts[w, dz] = [io.plan(part.at[dz, at.x], parts[w][2].at[dz - 1], at.on_z(dz))] if dz else []
            x_parts[w, dz] = [
                io.put(part.at[dz, at.xs[d]], x_recv.at[dz, d - 1], at.on_x(d)) for d in range(1, nx)
            ]

    def sum_middle(w, dz):
        part, x_recv, _ = parts[w]
        arrived(x_parts[w, dz])
        total = part[dz, at.x].astype(F32)
        for d in range(1, nx):
            total = total + x_recv[dz, d - 1].astype(F32)
        part[dz, at.x] = total.astype(BF)
        begin(z_parts[w, dz])

    def sum_end(w, outs):
        part, _, z_recv = parts[w]
        total = part[0, at.x].astype(F32)
        for dz in range(1, nz):
            arrived(z_parts[w, dz])
            total = total + z_recv[dz - 1].astype(F32)
        for j, (ref, out) in enumerate(outs):
            ref[...] = total[:, j * E : (j + 1) * E]
            io.move(ref, out)

    io.moved(*attend_loads)
    mask = head_mask(t.heads_here, LR, E)
    mask_low = mask.astype(BF)
    scale = 1.0 / math.sqrt(HEAD_DIM)
    for i in range(G):
        q = spread_heads(n.query_v[i], mask_low)
        d = spread_heads(n.dmixed[i], mask_low)
        k, v = n.keys_v[i], n.values_v[i]
        probs = softmax(mt(q, k) * scale)
        d_probs = mt(d, v)
        inner = jnp.sum(probs * d_probs, axis=-1, keepdims=True)
        d_scores = (probs * (d_probs - inner)).astype(BF)
        d_query = gather_heads(mm(d_scores, k), mask, LR) * scale
        d_pair = jnp.concatenate([tm(d_scores, q) * scale, tm(probs.astype(BF), d)], axis=-1)
        for slot in range(H):
            rows = slice(slot * ML + i * pr, slot * ML + (i + 1) * pr)
            n.dkv[rows] = d_pair[slot * pr : (slot + 1) * pr].astype(BF)
        for head in range(H):
            rows = slice(H * pr + head * ll, H * pr + (head + 1) * ll)
            n.turn_kv[head, i * ll : (i + 1) * ll] = d_pair[rows]
            n.turn_q[head, i * ll : (i + 1) * ll, 0:E] = d_query[head * ll : (head + 1) * ll]
    if t.EP > E:
        n.turn_q[:, :, E : t.EP] = jnp.zeros((H, L, t.EP - E), F32)
    for slot in range(H):
        head = at.slots[slot]
        n.dkv[slot * ML + M : (slot + 1) * ML] = n.turn_kv[head].astype(BF)
        n.dq[slot * L : (slot + 1) * L] = n.turn_q[head].astype(BF)
    kv_lanes = pl.ds(pl.multiple_of(at.h * 2 * E, 128), 2 * E)
    q_lanes = pl.ds(pl.multiple_of(at.h * t.EP, 128), t.EP)
    turned = []
    for slot in range(1, H):
        peer = (at.r, at.slots[slot])
        turned.append(io.put(n.dkv.at[slot * ML : (slot + 1) * ML], n.dkv_full.at[:, kv_lanes], peer))
        turned.append(io.put(n.dq.at[slot * L : (slot + 1) * L], n.dq_full.at[:, q_lanes], peer))
    out_far = [io.plan(n.out_send.at[at.ys[d]], n.out_recv.at[d - 1], at.on_y(d)) for d in range(1, ny)]
    io.moved(norm_load)
    sum_start("kv", lambda lanes: n.norm_v[:, lanes], n.dkv[...])
    sum_start(
        "query",
        lambda lanes: jnp.concatenate([n.norm_v[slot * ML + M : (slot + 1) * ML, lanes] for slot in range(H)], axis=0),
        n.dq[:, 0:E],
    )
    base, offset = window_of(here, B, D)
    window = pl.ds(base, 256)
    io.moved(*own_loads)
    n.up_acc[...] = tm(n.ffn_v[0, :, window], n.ffn_v[1, :, 0:F])
    n.down_acc[...] = tm(n.dout_v[0, :, window], n.dout_v[1, :, 0:F])
    q_load = io.plan_move(n.wq, n.w_v.at[:, 0 : n.wq.shape[1]])
    media_out, lat_out = io.plan_move(n.drow.at[0:M], n.media_o), io.plan_move(n.drow.at[M:ML], n.lat_o)
    own_out = io.plan_move(n.out_own_v, n.out_o)
    vec_z = [io.plan(n.vec_sum.at[at.zs[d]], n.vec_z.at[d - 1], at.on_z(d)) for d in range(1, nz)]

    def back_slot(k):
        return (ny - k // nc) % ny * nc + k % nc

    vec_head = [io.plan(n.vec_own, n.vec_head.at[back_slot(k) - 1], (at.r, at.slots[k])) for k in range(1, H)]

    def norm_back_rows(raw, size, base, gain_row, extra):
        def step(rows, sums):
            grad_rows = pl.ds(pl.multiple_of(base + rows.start, 16), 16)
            hat, inv = norm_rows(raw[rows].astype(F32))
            grad = n.drow[grad_rows]
            product = grad * hat
            scaled = grad * n.vecs[gain_row : gain_row + 1]
            mean = jnp.mean(scaled, axis=-1, keepdims=True)
            second = jnp.mean(scaled * hat, axis=-1, keepdims=True)
            result = inv * (scaled - mean - hat * second)
            n.drow[grad_rows] = result if extra is None else result + extra[rows]
            return sums[0] + product[:8] + product[8:], sums[1] + grad[:8] + grad[8:]

        sums = sweep(0, size, step, (jnp.zeros((8, D), F32), jnp.zeros((8, D), F32)))
        return [jnp.sum(v, axis=0, keepdims=True) for v in sums]

    def own_gradients():
        n.dkv_full[:, kv_lanes] = n.dkv[0:ML]
        n.dq_full[:, q_lanes] = n.dq[0:L]
        io.moved(*row_loads)
        arrived(turned)
        n.drow[...] = mt(n.dkv_full[...], n.w_v[...])
        begin([q_load])
        n.vec_own[0:1], n.vec_own[1:2] = norm_back_rows(n.media_v, M, 0, 0, None)
        begin([media_out])
        io.moved(q_load)
        n.drow[M:ML] += mt(n.dq_full[...], n.w_v[:, 0 : n.wq.shape[1]])
        n.vec_own[2:3], n.vec_own[3:4] = norm_back_rows(n.lat_v, L, M, 1, n.dres_v)
        begin([lat_out])
        n.vec_own[4:6] = n.fvec[0:2]
        n.vec_own[6:8] = jnp.zeros((2, D), F32)
        begin(vec_head)
        begin(out_far)

    def vectors_middle():
        arrived(vec_head)
        total = n.vec_own[...]
        for k in range(1, H):
            total = total + n.vec_head[k - 1]
        for z in range(nz):
            n.vec_sum[z] = total[:, z * span : (z + 1) * span]
        begin(vec_z)

    def own_output():
        arrived(out_far)
        total = n.out_own_v[...]
        for d in range(1, ny):
            total = total + n.out_recv[d - 1].astype(F32)
        n.out_own_v[...] = total
        begin([own_out])

    before, middle, after = [{index: [] for index in range(count)} for _ in range(3)]

    def late_quarters():
        for dz, dx in order[near:]:
            arrived([x_quarters[dz][nx - dx - 1]])
            begin(y_quarters[dz, dx])

    for index in range(count):
        before[index] += [lambda index=index: io.moved(*fetched[index])]
        if index + 1 < count and index != near - 1:
            before[index] += [lambda index=index: spread(index + 1)]
            middle[index] += [lambda index=index: fetch(index + 1)]
    middle[0] += [late_quarters]
    after[near - 1] += [lambda: sum_middle("kv", z_order[0]), out_middle]
    after[near - 1] += [lambda dz=dz: sum_middle("kv", dz) for dz in z_order[1:2]]
    after[near - 1] += [own_gradients]
    after[near - 1] += [lambda dz=dz: sum_middle("kv", dz) for dz in z_order[2:]]
    after[near - 1] += [lambda: spread(near), lambda: fetch(near)]
    late = list(range(near, count))
    after[late[min(1, len(late) - 1)]] += [vectors_middle]
    for position, dz in enumerate(z_order):
        after[late[min(position + 1, len(late) - 1)]] += [lambda dz=dz: sum_middle("query", dz)]
    after[late[-1]] += [own_output]
    spread(0)
    fetch(0)
    io.moved(*ffn_loads)

    def at_index(index, actions):
        for k in range(count):
            if actions[k]:

                @pl.when(index == k)
                def _():
                    for action in actions[k]:
                        action()

    def group_step(index, carry):
        at_index(index, before)
        buf = lax.rem(index + 1, 2)
        value, slope = gelu_pair(mm(n.ffn_v[buf], n.wup_v[...]))
        n.down_acc[...] += tm(n.dout_v[buf, :, window], value.astype(BF))
        n.slope[...] = slope
        at_index(index, middle)
        d_hidden = (mt(n.dout_v[buf], n.wdown_v[...]) * n.slope[...]).astype(BF)
        n.up_acc[...] += tm(n.ffn_v[buf, :, window], d_hidden)
        at_index(index, after)
        return carry

    lax.fori_loop(0, count, group_step, 0)
    arrived(vec_z)
    total = n.vec_sum[at.z]
    for d in range(1, nz):
        total = total + n.vec_z[d - 1]
    n.vec_part[...] = total
    vec_x = [io.put(n.vec_part, n.vec_x.at[d - 1], at.on_x(d)) for d in range(1, nx)]
    own_rows = pl.ds(pl.multiple_of(offset, 8), B)
    io.move(n.up_acc.at[own_rows], n.up_grad)
    io.move(n.down_acc.at[own_rows], n.down_grad)
    out_end()
    sum_end("kv", [(n.grad_v.at[1], n.key_grad), (n.grad_v.at[2], n.value_grad)])
    arrived(vec_x)
    total = n.vec_part[...]
    for d in range(1, nx):
        total = total + n.vec_x[d - 1]
    n.vec_done[...] = total
    io.move(n.vec_done, n.vec_o)
    sum_end("query", [(n.grad_v.at[3], n.query_grad)])
    io.finish()


def backward(s, ins):
    t = sizes_of(s)
    ny, nc, nz, nx, G, H = t.ny, t.nc, t.nz, t.nx, t.G, t.H
    M, L, LR, GL, ML, D, E, F, B = t.M, t.L, t.LR, t.GL, t.ML, t.D, t.E, t.F, t.B
    fx, fz, fh = max(nx - 1, 1), max(nz - 1, 1), max(H - 1, 1)
    span = D // nz
    outs = dict(
        media_o=((M, D), F32), lat_o=((L, D), F32), query_grad=((B, E), F32), key_grad=((B, E), F32), value_grad=((B, E), F32),
        out_grad=((B, E), F32), up_grad=((B, F), F32), down_grad=((B, F), F32), vec_o=((8, span), F32), out_o=((L, D), F32),
        fall_b=((s.rows, GL, D), BF), dall_b=((s.rows, ny * L, D), BF),
    )
    scratch = dict(
        mix_v=((H, GL, E), BF), wout_v=((E, D), BF), dcols_v=((GL, E), BF), dmixed=((G, LR, E), BF),
        keys_v=((G, t.KC, E), BF), values_v=((G, t.KC, E), BF), query_v=((G, LR, E), BF), norm_v=((H * ML, D), BF),
        ffn_v=((2, GL, D), BF), dout_v=((2, GL, D), BF), wup_v=((D, F), BF),
        wdown_v=((F, D), BF), w_v=((D, max(2 * D, H * t.EP)), BF), media_v=((M, D), BF), lat_v=((L, D), BF), dres_v=((L, D), F32),
        dkv=((H * ML, 2 * E), BF), dq=((H * L, t.EP), BF), turn_kv=((H, L, 2 * E), F32), turn_q=((H, L, t.EP), F32),
        dkv_full=((ML, 2 * D), BF), dq_full=((L, H * t.EP), BF), grad_v=((4, B, E), F32), up_acc=((256, F), F32),
        down_acc=((256, F), F32), drow=((ML, D), F32), slope=((GL, F), F32), vec_own=((8, D), F32), vec_head=((fh, 8, D), F32),
        vec_sum=((nz, 8, span), F32), vec_z=((fz, 8, span), F32), vec_part=((8, span), F32), vec_x=((fx, 8, span), F32),
        vec_done=((8, span), F32), vecs=((8, D), F32), out_own_v=((L, D), F32), out_recv=((max(ny - 1, 1), L, D), BF),
        p_out=((nz, nx, B, E), BF), zr_out=((fz, nx, B, E), BF), xr_out=((fx, B, E), BF),
    )
    for w, lanes in (("kv", 2 * E), ("query", E)):
        scratch["p_" + w] = ((nz, nx, B, lanes), BF)
        scratch["xr_" + w] = ((nz, fx, B, lanes), BF)
        scratch["zr_" + w] = ((fz, B, lanes), BF)
    places = {"fvec": VMEM}
    cost = pl.CostEstimate(flops=30 * 10**9, bytes_accessed=8 * 10**7, transcendentals=10**6)
    return call(backward_kernel, s, "backward", 2, ins, outs, scratch, 300, places, 63, cost)


def finish_kernel(count, *refs):
    ins, outs, held = refs[:count], refs[count : 2 * count], refs[2 * count : 3 * count]
    read, write = refs[3 * count :]
    loads = [pltpu.make_async_copy(a, b, read.at[i]) for i, (a, b) in enumerate(zip(ins, held))]
    stores = [pltpu.make_async_copy(a, b, write.at[i]) for i, (a, b) in enumerate(zip(held, outs))]
    for copy in loads:
        copy.start()
    for load, store in zip(loads, stores):
        load.wait()
        store.start()
    for copy in stores:
        copy.wait()


def finish(arrays):
    count = len(arrays)
    return pl.pallas_call(
        functools.partial(finish_kernel, count),
        name="finish",
        out_shape=[jax.ShapeDtypeStruct(a.shape, a.dtype) for a in arrays],
        in_specs=[ANY] * count,
        out_specs=[ANY] * count,
        scratch_shapes=[pltpu.VMEM(a.shape, a.dtype) for a in arrays] + [pltpu.SemaphoreType.DMA((count,))] * 2,
        compiler_params=pltpu.CompilerParams(vmem_limit_bytes=62 << 20),
    )(*arrays)


def body(
    media, latents, counts, media_gain, media_shift, latent_gain, latent_shift, w_query, w_key, w_value, w_out,
    ffn_gain, ffn_shift, w_up, w_down, cotangent,
):
    rows, heads = lax.axis_size("rows"), lax.axis_size("head")
    at = Place(rows, heads)
    images, patch, width = media.shape
    lat = latents.shape[1]
    cols = width // heads
    s = types.SimpleNamespace(
        rows=rows, heads=heads, images=images, patch=patch, lat=lat, width=width, cols=cols, mine=w_up.shape[1] // heads
    )
    t = sizes_of(s)

    def columns(array):
        return array if t.aligned else lax.dynamic_slice_in_dim(array, at.h * cols, cols, 1)

    gains = dict(
        media_gain=media_gain, media_shift=media_shift, latent_gain=latent_gain, latent_shift=latent_shift,
        ffn_gain=ffn_gain, ffn_shift=ffn_shift,
    )
    rows_in = dict(media=media.reshape(-1, width), lat=latents.reshape(-1, width))
    a = forward(
        s,
        dict(
            rows_in, cot=cotangent.reshape(-1, width), counts=counts, **gains, wq=columns(w_query), wk=columns(w_key),
            wv=columns(w_value), wout=w_out, wup=w_up, wdown=w_down,
        ),
    )
    ins = dict(
        rows_in, media_gain=gains["media_gain"], latent_gain=gains["latent_gain"], fvec=a["fvec_o"], dres=a["dres_o"],
        key_norm=a["key_norm_o"], keys=a["keys_o"], values=a["values_o"], query=a["query_o"], mixed=a["mixed_o"],
        dattn=a["dattn_o"], ffn=a["ffn_o"], dout=a["dout_o"], act=a["act_o"], dhid=a["dhid_o"], dall=a["dall"], fall=a["fall"],
        wout=w_out, wup=w_up, wdown=w_down, out_own=a["out_o"], out_send=a["out_send_o"],
    )
    if t.aligned:
        ins.update(wk=w_key, wv=w_value, wq=w_query)
    else:
        pair = jnp.stack([w_key.reshape(width, heads, cols), w_value.reshape(width, heads, cols)], axis=2)
        padded = jnp.pad(w_query.reshape(width, heads, cols), ((0, 0), (0, 0), (0, t.EP - cols)))
        ins.update(wkv=pair.reshape(width, 2 * width), wq=padded.reshape(width, -1), dattn_cols=columns(a["dattn_o"]))
    b = backward(s, ins)
    share = width // (rows * heads)
    vector = lax.dynamic_slice_in_dim(b["vec_o"], (at.x * heads + at.h) * share, share, 1)
    names = ("out_o", "media_o", "lat_o", "query_grad", "key_grad", "value_grad", "out_grad", "up_grad", "down_grad")
    out, media_grad, latents_grad, query_grad, key_grad, value_grad, out_grad, up_grad, down_grad = finish([b[k] for k in names])
    return (
        out.reshape(latents.shape), media_grad.reshape(media.shape), latents_grad.reshape(latents.shape), vector[0], vector[1],
        vector[2], vector[3], query_grad, key_grad, value_grad, out_grad, vector[4], vector[5], up_grad, down_grad.T,
    )


def solution(mesh):
    row = P("rows", "head", None)
    whole = P()
    vector = P(("rows", "head"))
    grid = P("rows", "head")
    return jax.shard_map(
        body,
        mesh=mesh,
        in_specs=(row, row) + (whole,) * 13 + (row,),
        out_specs=(row, row, row, vector, vector, vector, vector, grid, grid, grid, grid, vector, vector, grid, P("head", "rows")),
        check_vma=False,
    )
```

```python
import functools
import math
import types

import jax
import jax.numpy as jnp
from jax import lax
from jax.experimental import pallas as pl
from jax.experimental.pallas import tpu as pltpu
from jax.sharding import PartitionSpec as P

HEAD_DIM = 96
MAX_IMG = 8
EPSILON = 1e-05
BF = jnp.bfloat16
F32 = jnp.float32
MESH = pl.DeviceIdType.MESH
ANY = pl.BlockSpec(memory_space=pl.ANY)
VMEM = pl.BlockSpec(memory_space=pltpu.VMEM)
SMEM = pl.BlockSpec(memory_space=pltpu.SMEM)


def factor_rows(count):
    nz = 4 if count % 4 == 0 else 1
    return nz, count // nz


def factor_head(count):
    nc = 2 if count % 2 == 0 else 1
    return count // nc, nc


def mm(a, b):
    return lax.dot_general(a, b, (((1,), (0,)), ((), ())), preferred_element_type=F32)


def mt(a, b):
    return lax.dot_general(a, b, (((1,), (1,)), ((), ())), preferred_element_type=F32)


def tm(a, b):
    return lax.dot_general(a, b, (((0,), (0,)), ((), ())), preferred_element_type=F32)


class Place:
    def __init__(self, rows, heads):
        self.rows, self.heads = rows, heads
        self.nz, self.nx = factor_rows(rows)
        self.ny, self.nc = factor_head(heads)
        self.r = lax.axis_index("rows")
        self.h = lax.axis_index("head")
        self.z, self.x = lax.div(self.r, self.nx), lax.rem(self.r, self.nx)
        self.y, self.c = lax.div(self.h, self.nc), lax.rem(self.h, self.nc)
        self.zs, self.xs, self.ys = [
            [self.turn(at, d, size) for d in range(size)]
            for at, size in ((self.z, self.nz), (self.x, self.nx), (self.y, self.ny))
        ]
        self.other = self.nc - 1 - self.c
        self.groups = [[z * self.nx + x for x in self.xs] for z in self.zs]
        self.slots = [y * self.nc + c for y in self.ys for c in (self.c, self.other)[: self.nc]]
        self.partner = (self.r, self.y * self.nc + self.other)

    @staticmethod
    def turn(at, d, size):
        if d == 0:
            return at
        there = at + d
        return jnp.where(there >= size, there - size, there)

    def group(self, dz, dx):
        return self.groups[dz % self.nz][dx % self.nx]

    def on_y(self, d):
        return self.r, self.slots[d * self.nc]

    def on_x(self, d):
        return self.group(0, d), self.h

    def on_z(self, d):
        return self.group(d, 0), self.h

    def greet(self):
        peers = [(self.r, head) for head in self.slots[1:]]
        peers += [self.on_x(d) for d in range(1, self.nx)] + [self.on_z(d) for d in range(1, self.nz)]
        barrier = pltpu.get_barrier_semaphore()
        for peer in peers:
            pl.semaphore_signal(barrier, inc=1, device_id=peer, device_id_type=MESH)
        pl.semaphore_wait(barrier, len(peers))


class Copies:
    def __init__(self, at, send, recv, local):
        self.at, self.send, self.recv, self.local = at, send, recv, local
        self.used, self.used_local = 0, 0
        self.unsent, self.open = [], []

    def plan(self, src, dst, peer):
        copy = pltpu.make_async_remote_copy(
            src_ref=src,
            dst_ref=dst,
            send_sem=self.send.at[self.used],
            recv_sem=self.recv.at[self.used],
            device_id=peer,
            device_id_type=MESH,
        )
        self.used += 1
        self.unsent.append(copy)
        return copy

    def put(self, src, dst, peer):
        copy = self.plan(src, dst, peer)
        copy.start()
        return copy

    def put_y(self, src, dst):
        return [self.put(src, dst, self.at.on_y(d)) for d in range(1, self.at.ny)]

    def put_x(self, src, dst):
        return [self.put(src, dst, self.at.on_x(d)) for d in range(1, self.at.nx)]

    def put_z(self, src, dst):
        return [self.put(src, dst, self.at.on_z(d)) for d in range(1, self.at.nz)]

    def put_core(self, src, dst):
        return [self.put(src, dst, self.at.partner)] if self.at.nc > 1 else []

    def sent(self, copies):
        for copy in copies:
            copy.wait_send()
        self.unsent = [c for c in self.unsent if all(c is not d for d in copies)]

    def plan_move(self, src, dst):
        copy = pltpu.make_async_copy(src, dst, self.local.at[self.used_local])
        self.used_local += 1
        self.open.append(copy)
        return copy

    def move(self, src, dst):
        copy = self.plan_move(src, dst)
        copy.start()
        return copy

    def moved(self, *copies):
        for copy in copies:
            copy.wait()
        self.open = [c for c in self.open if all(c is not d for d in copies)]

    def finish(self):
        for copy in self.unsent:
            copy.wait_send()
        for copy in self.open:
            copy.wait()


def begin(copies):
    for copy in copies:
        copy.start()


def arrived(copies):
    for copy in copies:
        copy.wait_recv()


def norm_rows(block):
    mean = jnp.mean(block, axis=-1, keepdims=True)
    centered = block - mean
    scale = lax.rsqrt(jnp.mean(centered * centered, axis=-1, keepdims=True) + EPSILON)
    return centered * scale, scale


def sweep(first, last, step, carry=0):
    together = next(k for k in (4, 2, 1) if (last - first) // 16 % k == 0)

    def turn(i, value):
        for j in range(together):
            start = first + i * (16 * together) + j * 16
            value = step(pl.ds(pl.multiple_of(start, 16), 16), value)
        return value

    return lax.fori_loop(0, (last - first) // (16 * together), turn, carry)


def gelu_pair(v):
    c = math.sqrt(2.0 / math.pi)
    square = v * v
    t = jnp.tanh(c * v * (1.0 + 0.044715 * square))
    half = 0.5 * (1.0 + t)
    slope = half + 0.5 * v * (1.0 - t * t) * (c * (1.0 + 3.0 * 0.044715 * square))
    return v * half, slope


def softmax(scores):
    powers = jnp.exp(scores - jnp.max(scores, axis=-1, keepdims=True))
    return powers * (1.0 / jnp.sum(powers, axis=-1, keepdims=True))


def head_mask(heads_here, rows, cols):
    col = lax.broadcasted_iota(jnp.int32, (rows, cols), 1)
    return jnp.concatenate(
        [((col >= j * HEAD_DIM) & (col < (j + 1) * HEAD_DIM)).astype(F32) for j in range(heads_here)], axis=0
    )


def spread_heads(block, mask):
    return jnp.concatenate([block] * (mask.shape[0] // block.shape[0]), axis=0) * mask


def gather_heads(block, mask, rows):
    block = block * mask
    return sum(block[j * rows : (j + 1) * rows] for j in range(block.shape[0] // rows))


def sizes_of(s):
    ny, nc = factor_head(s.heads)
    nz, nx = factor_rows(s.rows)
    t = types.SimpleNamespace(ny=ny, nc=nc, nz=nz, nx=nx, G=s.images, D=s.width, E=s.cols, F=s.mine, H=s.heads)
    t.pr, t.ll = s.patch, s.lat
    t.M, t.L, t.LR = t.G * t.pr, t.G * t.ll, t.H * t.ll
    t.GL, t.ML, t.KC = t.G * t.LR, t.M + t.L, t.H * t.pr + t.LR
    t.B = t.D // s.rows
    t.heads_here = t.E // HEAD_DIM
    t.aligned = t.E % 128 == 0
    t.EP = -(-t.E // 128) * 128
    t.by_rows = t.aligned and ny == 2 and nc == 2
    t.W = ny * t.E if t.by_rows else t.E
    t.wide_heads = t.W // HEAD_DIM
    return t


def forward_kernel(s, names, *refs):
    n = types.SimpleNamespace(**dict(zip(names, refs, strict=True)))
    at = Place(s.rows, s.heads)
    t = sizes_of(s)
    ny, nc, nz, nx, G, H = t.ny, t.nc, t.nz, t.nx, t.G, t.H
    M, L, LR, GL, ML, D, E, F, ll, pr = t.M, t.L, t.LR, t.GL, t.ML, t.D, t.E, t.F, t.ll, t.pr
    io = Copies(at, n.send, n.recv, n.local)
    here = at.r

    vectors = ("media_gain", "media_shift", "latent_gain", "latent_shift", "ffn_gain", "ffn_shift")
    load_vecs = [io.move(getattr(n, k), n.vecs.at[i]) for i, k in enumerate(vectors)]
    load_lat = io.move(n.lat, n.raw_l.at[0:L])
    load_cot = io.move(n.cot, n.cot_v)
    load_media = io.move(n.media, n.raw_m.at[0])

    def columns(weight):
        return weight.at[:, pl.ds(pl.multiple_of(at.h * E, 128), E)] if t.aligned else weight

    load_qkv = [io.move(columns(w), v.at[:, 0:E]) for w, v in ((n.wk, n.wk_v), (n.wv, n.wv_v), (n.wq, n.wq_v))]
    if t.by_rows:
        for w, v in ((n.wk, n.wk_v), (n.wv, n.wv_v), (n.wq, n.wq_v)):
            lanes = pl.ds(pl.multiple_of(at.slots[nc] * E, 128), E)
            load_qkv.append(io.move(w.at[:, lanes], v.at[:, E : 2 * E]))
    at.greet()

    bounds = [0, pr, M] if t.by_rows and G > 1 else [0, M // 2, M]
    chunks = len(bounds) - 1

    def far_slot(d):
        return (ny - d) % ny * nc

    def lat_rows(k):
        return n.raw_l.at[k * L : (k + 1) * L]

    lat_far = [io.put(n.lat, lat_rows(far_slot(d)), at.on_y(d)) for d in range(1, ny)]
    lat_near = io.put_core(n.lat, lat_rows(1 % H))
    media_far, media_near = [], []

    def send_patches(j):
        rows = slice(bounds[j], bounds[j + 1])
        media_far.append([io.put(n.media.at[rows], n.raw_m.at[far_slot(d), rows], at.on_y(d)) for d in range(1, ny)])

    for j in range(chunks):
        rows = slice(bounds[j], bounds[j + 1])
        media_near.append(io.put_core(n.media.at[rows], n.raw_m.at[1 % H, rows]))
    if not t.by_rows:
        for j in range(chunks):
            send_patches(j)

    io.moved(load_cot)
    for i in range(G):
        image = here * G + i
        limit = n.counts[lax.div(image, MAX_IMG)]
        live = jnp.where(lax.rem(image, MAX_IMG) < limit, 1.0, 0.0).astype(F32)
        rows = slice(i * ll, (i + 1) * ll)
        n.wide_l[rows] = n.cot_v[rows].astype(F32) * live
    n.dslot[at.y, at.c] = n.wide_l[...].astype(BF)
    own_d = n.dslot.at[at.y, at.c]

    def quarter(r, y):
        return r, pl.ds(pl.multiple_of(y * L, 16), L)

    def across(y, block):
        where = n.dall.at[quarter(here, y)]
        return io.put_z(block, where), io.put_x(block, where)

    z_far, x_far = {}, {}
    if t.by_rows:
        cot_far = io.put_y(own_d, own_d)
        cot_near = io.put_core(own_d, own_d)
        send_patches(0)
    z_far[0], x_far[0] = across(at.y, own_d)
    load_out = io.move(n.wout, n.wout_v)
    load_up = io.move(n.wup.at[:, pl.ds(pl.multiple_of(at.h * F, 128), F)], n.wup_v)
    load_down = io.move(n.wdown.at[pl.ds(pl.multiple_of(at.h * F, 16), F)], n.wdown_v)

    def forward_x(d, first=1, last=nz):
        for dz in range(first, last):
            z_far[d][dz - 1].wait_recv()
            block = n.dall.at[quarter(at.group(nz - dz, 0), at.ys[d])]
            x_far[d] += io.put_x(block, block)

    norm_busy = {}
    turn_count = [0]

    def patches(k, first, last):
        buf = turn_count[0] % 2
        turn_count[0] += 1
        if buf in norm_busy:
            io.moved(norm_busy[buf])

        def step(rows, carry):
            hat, _ = norm_rows(n.raw_m[k, rows].astype(F32))
            n.norm[buf, rows] = (hat * n.vecs[0:1] + n.vecs[1:2]).astype(BF)
            return carry

        sweep(first * 16, last * 16, step)
        rows = slice(first * 16, last * 16)
        for weight, result in ((n.wk_v, n.keys), (n.wv_v, n.values)):
            wide = mm(n.norm[buf, rows], weight[:, 0:E]).astype(BF)
            for i in range(first * 16 // pr, last * 16 // pr):
                base = i * pr - first * 16
                result[i, k * pr : (k + 1) * pr] = wide[base : base + pr]
        norm_busy[buf] = io.move(n.norm.at[buf, rows], n.key_norm_o.at[k * ML + first * 16 : k * ML + last * 16])

    io.moved(load_media, *load_qkv, *load_vecs)
    if t.by_rows:
        def near_patches(k, carry):
            @pl.when(k == 1)
            def _():
                for copies in media_near:
                    arrived(copies)

            def step(rows, value):
                hat, _ = norm_rows(n.raw_m[k, rows].astype(F32))
                n.norm[k, rows] = (hat * n.vecs[0:1] + n.vecs[1:2]).astype(BF)
                return value

            sweep(0, M, step)
            for weight, result, chip in ((n.wk_v, n.keys, n.keys_w), (n.wv_v, n.values, n.values_w)):
                wide = mm(n.norm[k], weight[...]).astype(BF)
                rows = pl.ds(pl.multiple_of(k * pr, 16), pr)
                for i in range(G):
                    result[i, rows] = wide[i * pr : (i + 1) * pr, 0:E]
                    chip[i, rows] = wide[i * pr : (i + 1) * pr]
            return carry

        lax.fori_loop(0, nc, near_patches, 0)
        for k in range(nc):
            norm_busy[k] = io.move(n.norm.at[k], n.key_norm_o.at[k * ML : k * ML + M])
    else:
        patches(0, 0, M // 16)
        if nc > 1:
            for copies in media_near:
                arrived(copies)
            patches(1, 0, M // 16)
    if not t.by_rows:
        cot_far = io.put_y(own_d, own_d)
        cot_near = io.put_core(own_d, own_d)
    relay = []
    for d, copy in zip(range(1, ny), lat_far):
        copy.wait_recv()
        k = far_slot(d)
        relay += io.put_core(lat_rows(k), lat_rows(k + 1)) if nc > 1 else []
    io.moved(load_lat)
    arrived(lat_near)
    arrived(relay)
    for k in range(H):
        wide = n.raw_l[k * L : (k + 1) * L].astype(F32)
        for i in range(G):
            n.resid[pl.ds(pl.multiple_of(i * LR + at.slots[k] * ll, 8), ll)] = wide[i * ll : (i + 1) * ll]

    def latent_step(rows, carry):
        hat, _ = norm_rows(n.raw_l[rows].astype(F32))
        n.lnorm[rows] = (hat * n.vecs[2:3] + n.vecs[3:4]).astype(BF)
        return carry

    sweep(0, H * L, latent_step)
    for k in range(H):
        io.move(n.lnorm.at[k * L : (k + 1) * L], n.key_norm_o.at[k * ML + M : (k + 1) * ML])
    for weight, result, chip in ((n.wq_v, n.query, n.query_w), (n.wk_v, n.keys, n.keys_w), (n.wv_v, n.values, n.values_w)):
        wide = mm(n.lnorm[...], weight[...])
        for k in range(H):
            for i in range(G):
                n.turn[pl.ds(pl.multiple_of(i * LR + at.slots[k] * ll, 8), ll)] = wide[k * L + i * ll : k * L + (i + 1) * ll]
        for i in range(G):
            block = n.turn[i * LR : (i + 1) * LR].astype(BF)
            if result is n.query:
                result[i] = block[:, 0:E]
                if t.by_rows:
                    chip[i] = block
            else:
                result[i, H * pr : t.KC] = block[:, 0:E]
                if t.by_rows:
                    pair = [wide[k * L + i * ll : k * L + (i + 1) * ll] for k in range(nc)]
                    chip[i, nc * pr : nc * (pr + ll)] = jnp.concatenate(pair, axis=0).astype(BF)

    def far_patches(j):
        relays = []
        rows = slice(bounds[j], bounds[j + 1])
        for d, copy in zip(range(1, ny), media_far[j]):
            copy.wait_recv()
            k = far_slot(d)
            relays.append(io.put_core(n.raw_m.at[k, rows], n.raw_m.at[k + 1, rows]) if nc > 1 else [])
        for d in range(1, ny):
            patches(far_slot(d), bounds[j] // 16, bounds[j + 1] // 16)
        for d in range(1, ny):
            if nc > 1:
                arrived(relays[d - 1])
                patches(far_slot(d) + 1, bounds[j] // 16, bounds[j + 1] // 16)

    cot_relay = []

    def far_cotangents():
        arrived(cot_far)
        for d in range(1, ny):
            block = n.dslot.at[at.ys[d], at.c]
            cot_relay.extend(io.put_core(block, block))

    def cross_cotangents():
        for d in range(1, ny):
            z_far[d], x_far[d] = across(at.ys[d], n.dslot.at[at.ys[d], at.c])

    def group_cotangents():
        arrived(cot_near)
        arrived(cot_relay)
        for y in range(ny):
            for c in range(nc):
                wide = n.dslot[y, c].astype(F32)
                for i in range(G):
                    n.part[i * LR + (y * nc + c) * ll : i * LR + (y * nc + c + 1) * ll] = wide[i * ll : (i + 1) * ll]
        n.dout[...] = n.part[...].astype(BF)
        io.move(n.dout, n.dout_o)

    def add_mixed(head):
        n.resid[...] += mm(n.mix[head], n.wout_v[pl.ds(pl.multiple_of(head * E, 16), E)])

    scale = 1.0 / math.sqrt(HEAD_DIM)
    mask = head_mask(t.wide_heads, LR, t.W)
    mask_low = mask.astype(BF)
    if t.by_rows:
        far_cotangents()
        lane = lax.broadcasted_iota(jnp.int32, (LR, 128), 1)
        for i in range(G):
            scores = mt(spread_heads(n.query_w[i], mask_low), n.keys_w[i]) * scale
            top = jnp.max(scores, axis=-1, keepdims=True)
            powers = jnp.exp(scores - top)
            total = jnp.sum(powers, axis=-1, keepdims=True)
            mixed = gather_heads(mm(powers.astype(BF), n.values_w[i]) * (1.0 / total), mask, LR)
            rows = slice(i * LR, (i + 1) * LR)
            n.o_send[rows] = mixed.astype(BF)
            log_total = top + jnp.log(total)
            stats = jnp.zeros((LR, 128), F32)
            for j in range(t.wide_heads):
                one = log_total[j * LR : (j + 1) * LR]
                high = one.astype(BF).astype(F32)
                stats = jnp.where(lane == j, high, stats)
                stats = jnp.where(lane == j + t.wide_heads, one - high, stats)
            n.l_send[rows] = stats.astype(BF)
        o_far = io.put_y(n.o_send, n.o_recv) + io.put_y(n.l_send, n.l_recv)
        send_patches(1)
        row = lax.broadcasted_iota(jnp.int32, (128, t.W), 0)
        col = lax.broadcasted_iota(jnp.int32, (128, t.W), 1)
        widen = jnp.zeros((128, t.W), F32)
        for j in range(t.wide_heads):
            inside = (col >= j * HEAD_DIM) & (col < (j + 1) * HEAD_DIM)
            widen = jnp.where(inside & ((row == j) | (row == j + t.wide_heads)), 1.0, widen)
        widen = widen.astype(BF)

        def other_chip(block):
            return jnp.concatenate([block[:, E : 2 * E], block[:, 0:E]], axis=-1)

        far_patches(0)
        group_cotangents()
        io.moved(load_out, load_up, load_down)
        forward_x(0)
        cross_cotangents()
        arrived(o_far)
        def merge(i, carry):
            rows = pl.ds(pl.multiple_of(i * LR, 16), LR)
            near_log, far_log = mm(n.l_send[rows], widen), other_chip(mm(n.l_recv[rows], widen))
            top = jnp.maximum(near_log, far_log)
            near_part, far_part = jnp.exp(near_log - top), jnp.exp(far_log - top)
            mixed = n.o_send[rows].astype(F32) * near_part + other_chip(n.o_recv[rows].astype(F32)) * far_part
            mixed = mixed * (1.0 / (near_part + far_part))
            for d in range(ny):
                n.mix[at.slots[d * nc], rows] = mixed[:, d * E : (d + 1) * E].astype(BF)
            return carry

        lax.fori_loop(0, G, merge, 0)
        mix_near = [io.put_core(n.mix.at[at.slots[d * nc]], n.mix.at[at.slots[d * nc]]) for d in range(ny)]
        def add_core(core, carry):
            @pl.when(core == 1)
            def _():
                for copies in mix_near:
                    arrived(copies)

            for d in range(ny):
                add_mixed(jnp.where(core == 0, at.slots[d * nc], at.slots[d * nc + 1]))
            return carry

        lax.fori_loop(0, nc, add_core, 0)
    else:
        for j in range(chunks):
            far_patches(j)
        far_cotangents()
        cross_cotangents()
        forward_x(0)
        for i in range(G):
            scores = mt(spread_heads(n.query[i], mask_low), n.keys[i]) * scale
            probs = softmax(scores).astype(BF)
            mixed = gather_heads(mm(probs, n.values[i]), mask, LR)
            n.mix[at.h, i * LR : (i + 1) * LR] = mixed.astype(BF)
        mix_far = io.put_y(n.mix.at[at.h], n.mix.at[at.h])
        mix_near = io.put_core(n.mix.at[at.h], n.mix.at[at.h])
        io.moved(load_out, load_up, load_down)
        add_mixed(at.h)
        arrived(mix_near)
        if nc > 1:
            add_mixed(at.slots[1])
        group_cotangents()
        mix_relay = []
        for d, copy in zip(range(1, ny), mix_far):
            copy.wait_recv()
            block = n.mix.at[at.slots[far_slot(d)]]
            mix_relay.append(io.put_core(block, block))
        for d in range(1, ny):
            add_mixed(at.slots[far_slot(d)])
        for d in range(1, ny):
            if nc > 1:
                arrived(mix_relay[d - 1])
                add_mixed(at.slots[far_slot(d) + 1])
    io.move(n.mix, n.mixed_o)
    gain, shift = n.vecs[4:5], n.vecs[5:6]

    def ffn_step(rows, carry):
        hat, inv = norm_rows(n.resid[rows])
        n.hat[rows] = hat
        n.inv[rows] = jnp.broadcast_to(inv, (16, 128))
        n.ffn[rows] = (hat * n.vecs[4:5] + n.vecs[5:6]).astype(BF)
        return carry

    sweep(0, GL, ffn_step)
    io.move(n.ffn, n.ffn_o)

    def own_rows(ref):
        return jnp.concatenate([ref[pl.ds(pl.multiple_of(i * LR + at.h * ll, 8), ll)] for i in range(G)], axis=0)

    n.fq[...] = (own_rows(n.hat) * gain + shift).astype(BF)
    own_f = n.fall.at[at.z]
    ffn_far = io.put_z(n.fq, own_f)
    io.move(n.fq, own_f)
    value, slope = gelu_pair(mm(n.ffn[...], n.wup_v[...]))
    n.act[...] = value.astype(BF)
    n.dhid[...] = (mt(n.dout[...], n.wdown_v[...]) * slope).astype(BF)
    n.part[...] = mt(n.dhid[...], n.wup_v[...])
    half = GL // nc
    theirs = pl.ds(pl.multiple_of((nc - 1 - at.c) * half, 16), half)
    swap = io.put_core(n.part.at[theirs], n.c_recv)
    io.move(n.act, n.act_o)
    io.move(n.dhid, n.dhid_o)
    out_part = mm(n.act[...], n.wdown_v[...])
    for i in range(G):
        for head in range(H):
            base = i * LR + head * ll
            n.outp[head % nc, head // nc, i * ll : (i + 1) * ll] = out_part[base : base + ll]
    out_swap = io.put_core(n.outp.at[nc - 1 - at.c], n.oc_recv)
    for d in range(1, ny):
        forward_x(d, 1, nz - 1)
    arrived(swap)
    pieces = 2
    piece = half // pieces
    sum_far = []
    for j in range(pieces):
        rows = slice(j * piece, (j + 1) * piece)
        total = n.part[pl.ds(pl.multiple_of(at.c * half + j * piece, 16), piece)]
        if nc > 1:
            total = total + n.c_recv[rows]
        n.y_send[rows] = total.astype(BF)
        sum_far.append([io.put(n.y_send.at[rows], n.y_recv.at[d - 1, rows], at.on_y(d)) for d in range(1, ny)])
    io.sent(swap)
    if t.by_rows:
        far_patches(1)
    for d in range(1, ny):
        forward_x(d, max(nz - 1, 1), nz)
    arrived(out_swap)
    for y in range(ny):
        total = n.outp[at.c, y]
        if nc > 1:
            total = total + n.oc_recv[y]
        n.outp[at.c, y] = total
        n.oy_send[y] = total.astype(BF)
    for ref, out in ((n.keys, n.keys_o), (n.values, n.values_o), (n.query, n.query_o)):
        io.move(ref, out)

    def residual_back(ref, base, first, last):
        def step(from_rows, carry):
            rows = pl.ds(pl.multiple_of(base + from_rows.start, 16), 16)
            grad = ref[from_rows]
            hat, inv = n.hat[rows], n.inv[rows, 0:1]
            n.part[rows] = grad
            scaled = grad * n.vecs[4:5]
            first = jnp.mean(scaled, axis=-1, keepdims=True)
            second = jnp.mean(scaled * hat, axis=-1, keepdims=True)
            d_res = n.dout[rows].astype(F32) + inv * (scaled - first - hat * second)
            n.resid[rows] = d_res
            n.dattn[rows] = d_res.astype(BF)
            return carry

        sweep(first, last, step)

    n.own[0] = n.outp[at.c, at.y] + own_rows(n.resid)
    io.move(n.own.at[0], n.out_o)
    io.move(n.oy_send, n.out_send_o)
    share = []
    for j in range(pieces):
        rows = slice(j * piece, (j + 1) * piece)
        arrived(sum_far[j])
        total = n.y_send[rows].astype(F32)
        for d in range(1, ny):
            total = total + n.y_recv[d - 1, rows].astype(F32)
        n.share[rows] = total
        share.append(io.put_core(n.share.at[rows], n.s_recv.at[rows]))
        residual_back(n.share, at.c * half, j * piece, (j + 1) * piece)
    if nc > 1:
        for j in range(pieces):
            arrived(share[j])
            residual_back(n.s_recv, (nc - 1 - at.c) * half, j * piece, (j + 1) * piece)
    io.move(n.dattn, n.dattn_o)
    n.own[1] = own_rows(n.resid)
    io.move(n.own.at[1], n.dres_o)
    grad = own_rows(n.part)
    n.fvec[0:1] = jnp.sum(grad * own_rows(n.hat), axis=0, keepdims=True)
    n.fvec[1:2] = jnp.sum(grad, axis=0, keepdims=True)
    n.fvec[2:8] = jnp.zeros((6, D), F32)
    io.move(n.fvec, n.fvec_o)
    for d in range(ny):
        arrived(x_far[d])
    arrived(ffn_far)
    io.finish()


def call(kernel, s, name, ident, ins, outs, scratch, semaphores, places, limit, cost):
    names = list(ins) + list(outs) + list(scratch) + ["send", "recv", "local"]
    dma = [pltpu.SemaphoreType.DMA((count,)) for count in (semaphores, semaphores, 120)]
    result = pl.pallas_call(
        functools.partial(kernel, s, names),
        name=name,
        out_shape=[jax.ShapeDtypeStruct(*o) for o in outs.values()],
        in_specs=[places.get(k, ANY) for k in ins],
        out_specs=[ANY] * len(outs),
        scratch_shapes=[pltpu.VMEM(*v) for v in scratch.values()] + dma,
        compiler_params=pltpu.CompilerParams(collective_id=ident, has_side_effects=True, vmem_limit_bytes=limit << 20),
        cost_estimate=cost,
    )(*ins.values())
    return dict(zip(outs, result, strict=True))


def forward(s, ins):
    t = sizes_of(s)
    ny, nc, G, H, M, L, LR, GL, ML, D, E, F = t.ny, t.nc, t.G, t.H, t.M, t.L, t.LR, t.GL, t.ML, t.D, t.E, t.F
    half = GL // nc
    far, W = max(ny - 1, 1), t.W
    outs = dict(
        out_o=((L, D), F32), dres_o=((L, D), F32), fvec_o=((8, D), F32), key_norm_o=((H * ML, D), BF),
        keys_o=((G, t.KC, E), BF), values_o=((G, t.KC, E), BF), query_o=((G, LR, E), BF), mixed_o=((H, GL, E), BF),
        dattn_o=((GL, D), BF), ffn_o=((GL, D), BF), dout_o=((GL, D), BF), act_o=((GL, F), BF), dhid_o=((GL, F), BF),
        dall=((s.rows, ny * L, D), BF), fall=((t.nz, L, D), BF), out_send_o=((ny, L, D), BF),
    )
    scratch = dict(
        vecs=((8, D), F32), cot_v=((L, D), BF), wide_l=((L, D), F32), raw_m=((H, M, D), BF), raw_l=((H * L, D), BF), dslot=((ny, nc, L, D), BF),
        norm=((2, M, D), BF), lnorm=((H * L, D), BF), turn=((GL, W), F32), keys=((G, t.KC, E), BF), values=((G, t.KC, E), BF),
        query=((G, LR, E), BF), mix=((H, GL, E), BF), resid=((GL, D), F32), hat=((GL, D), F32), inv=((GL, 128), F32),
        ffn=((GL, D), BF), dout=((GL, D), BF), act=((GL, F), BF), dhid=((GL, F), BF), part=((GL, D), F32),
        outp=((nc, ny, L, D), F32), c_recv=((half, D), F32), oc_recv=((ny, L, D), F32), y_send=((half, D), BF),
        y_recv=((far, half, D), BF), oy_send=((ny, L, D), BF), share=((half, D), F32),
        s_recv=((half, D), F32), fq=((L, D), BF), own=((2, L, D), F32), dattn=((GL, D), BF),
        fvec=((8, D), F32), wq_v=((D, W), BF), wk_v=((D, W), BF), wv_v=((D, W), BF), wout_v=((D, D), BF),
        wup_v=((D, F), BF), wdown_v=((F, D), BF),
    )
    shape = (G, nc * (t.pr + t.ll), W) if t.by_rows else (1, 16, 128)
    rows = (GL, W) if t.by_rows else (16, 128)
    scratch.update(
        keys_w=(shape, BF), values_w=(shape, BF), query_w=((G, LR, W) if t.by_rows else shape, BF), o_send=(rows, BF),
        o_recv=(rows, BF), l_send=((rows[0], 128), BF), l_recv=((rows[0], 128), BF),
    )
    places = {"counts": SMEM}
    cost = pl.CostEstimate(flops=8 * 10**9, bytes_accessed=4 * 10**7, transcendentals=10**6)
    return call(forward_kernel, s, "forward", 1, ins, outs, scratch, 200, places, 62, cost)


def window_of(position, block, width):
    base = jnp.minimum(position * block // 128 * 128, width - 256)
    return pl.multiple_of(base, 128), position * block - base


def backward_kernel(s, names, *refs):
    n = types.SimpleNamespace(**dict(zip(names, refs, strict=True)))
    at = Place(s.rows, s.heads)
    t = sizes_of(s)
    ny, nc, nz, nx, G, H = t.ny, t.nc, t.nz, t.nx, t.G, t.H
    M, L, LR, GL, ML, D, E, F, ll, pr, B = t.M, t.L, t.LR, t.GL, t.ML, t.D, t.E, t.F, t.ll, t.pr, t.B
    here = at.r
    io = Copies(at, n.send, n.recv, n.local)

    def quarter(r, y):
        return r, pl.ds(pl.multiple_of((at.c * ny + y) * L, 16), L)

    aligned = t.aligned
    first_loads = [io.move(n.dattn, n.ffn_v.at[1]), io.move(n.mixed, n.mix_v)]
    first_loads.append(io.move(n.wout.at[pl.ds(pl.multiple_of(at.h * E, 16), E)], n.wout_v))
    if aligned:
        first_loads.append(io.move(n.dattn.at[:, pl.ds(pl.multiple_of(at.h * E, 128), E)], n.dcols_v))
    else:
        first_loads.append(io.move(n.dattn_cols, n.dcols_v))
    attend_loads = [io.move(getattr(n, k), getattr(n, k + "_v")) for k in ("keys", "values", "query")]
    norm_load = io.move(n.key_norm, n.norm_v)
    own_loads = [io.move(n.act, n.dout_v.at[1, :, 0:F]), io.move(n.ffn, n.ffn_v.at[0]), io.move(n.dout, n.dout_v.at[0])]
    ffn_loads = [io.move(n.wup.at[:, pl.ds(pl.multiple_of(at.h * F, 128), F)], n.wup_v)]
    ffn_loads.append(io.move(n.wdown.at[pl.ds(pl.multiple_of(at.h * F, 16), F)], n.wdown_v))
    if aligned:
        row_loads = []
        for head in range(H):
            for j, weight in enumerate((n.wk, n.wv)):
                lanes = slice((2 * head + j) * E, (2 * head + j + 1) * E)
                row_loads.append(io.move(weight.at[:, head * E : (head + 1) * E], n.w_v.at[:, lanes]))
    else:
        row_loads = [io.move(n.wkv, n.w_v)]
    row_loads += [io.move(n.media_gain, n.vecs.at[0]), io.move(n.latent_gain, n.vecs.at[1]), io.move(n.out_own, n.out_own_v)]
    row_loads += [io.move(n.media, n.media_v), io.move(n.lat, n.lat_v), io.move(n.dres, n.dres_v)]
    at.greet()

    x_quarters = []
    for dz in range(nz):
        source = n.fall.at[at.zs[dz]]
        x_quarters.append(io.put_x(source, n.fall_b.at[quarter(at.group(dz, 0), at.y)]))
    y_quarters = {}
    for dz in range(1, nz):
        source = n.fall.at[at.zs[dz]]
        y_quarters[dz, 0] = io.put_y(source, n.fall_b.at[quarter(at.group(dz, 0), at.y)])

    def core_rows(c):
        return pl.ds(pl.multiple_of(c * ny * L, 16), ny * L)

    for dx in range(1, nx):
        for dz in range(nz):
            block = n.fall_b.at[quarter(at.group(dz, nx - dx), at.y)]
            y_quarters[dz, nx - dx] = [io.plan(block, block, at.on_y(d)) for d in range(1, ny)]
    order = [(dz, 0) for dz in range(1, nz)] + [(dz, nx - dx) for dx in range(1, nx) for dz in range(nz)]
    near, count = nz - 1, len(order)
    to_core, fetched = [], []
    for index, (dz, dx) in enumerate(order):
        r = at.group(dz, dx)
        buf = (index + 1) % 2
        copies = [io.plan(n.dall.at[r], n.dall_b.at[r], at.partner)] if nc > 1 else []
        for d in range(ny):
            block = n.fall_b.at[quarter(r, at.ys[d])]
            source = n.fall.at[at.zs[dz]] if (d == 0 and dx == 0) else block
            copies += [io.plan(source, block, at.partner)] if nc > 1 else []
        to_core.append(copies)
        copies = []
        for c in range(nc):
            rows = core_rows(at.c if c == 0 else nc - 1 - at.c)
            source = n.dall if c == 0 else n.dall_b
            copies.append(io.plan_move(source.at[r], n.dout_v.at[buf, rows]))
        if dx > 0:
            copies.append(io.plan_move(n.fall_b.at[r], n.ffn_v.at[buf]))
        else:
            for slot in range(H):
                core = at.c if slot % nc == 0 else at.other
                rows = pl.ds(pl.multiple_of((core * ny + at.ys[slot // nc]) * L, 16), L)
                source = n.fall.at[at.zs[dz]] if slot == 0 else n.fall_b.at[r, rows]
                copies.append(io.plan_move(source, n.ffn_v.at[buf, rows]))
        fetched.append(copies)

    def spread(index):
        arrived(y_quarters[order[index]])
        begin(to_core[index])

    def fetch(index):
        if index < count:
            arrived(to_core[index])
            begin(fetched[index])

    io.moved(*first_loads)
    n.dmixed[...] = mt(n.ffn_v[1], n.wout_v[...]).astype(BF).reshape(G, LR, E)
    own_loads.append(io.move(n.dhid, n.ffn_v.at[1, :, 0:F]))
    span = nx * B
    if E == span:
        tiles = [tm(n.mix_v[z], n.dcols_v[...]) for z in range(nz)]
    else:
        whole = jnp.concatenate([n.mix_v[head] for head in range(H)], axis=-1)
        tiles = [tm(whole[:, z * span : (z + 1) * span], n.dcols_v[...]) for z in range(nz)]
    for z in range(nz):
        for x in range(nx):
            n.p_out[z, x] = tiles[z][x * B : (x + 1) * B].astype(BF)
    out_x = [io.plan(n.p_out.at[at.z, at.xs[d]], n.xr_out.at[d - 1], at.on_x(d)) for d in range(1, nx)]
    out_z = [io.put(n.p_out.at[at.zs[d]], n.zr_out.at[d - 1], at.on_z(d)) for d in range(1, nz)]

    def out_middle():
        arrived(out_z)
        total = n.p_out[at.z].astype(F32)
        for d in range(1, nz):
            total = total + n.zr_out[d - 1].astype(F32)
        n.p_out[at.z] = total.astype(BF)
        begin(out_x)

    def out_end():
        arrived(out_x)
        total = n.p_out[at.z, at.x].astype(F32)
        for d in range(1, nx):
            total = total + n.xr_out[d - 1].astype(F32)
        n.grad_v[0] = total
        io.move(n.grad_v.at[0], n.out_grad)

    parts = {"kv": (n.p_kv, n.xr_kv, n.zr_kv), "query": (n.p_query, n.xr_query, n.zr_query)}
    x_parts, z_parts = {}, {}
    z_order = list(range(1, nz)) + [0]

    def sum_start(w, rows, grads):
        part, x_recv = parts[w][:2]
        for dz in z_order:
            lanes = pl.ds(pl.multiple_of(at.zs[dz] * span, 128), span)
            tile = tm(rows(lanes), grads)
            for x in range(nx):
                part[dz, x] = tile[x * B : (x + 1) * B].astype(BF)
            z_parts[w, dz] = [io.plan(part.at[dz, at.x], parts[w][2].at[dz - 1], at.on_z(dz))] if dz else []
            x_parts[w, dz] = [
                io.put(part.at[dz, at.xs[d]], x_recv.at[dz, d - 1], at.on_x(d)) for d in range(1, nx)
            ]

    def sum_middle(w, dz):
        part, x_recv, _ = parts[w]
        arrived(x_parts[w, dz])
        total = part[dz, at.x].astype(F32)
        for d in range(1, nx):
            total = total + x_recv[dz, d - 1].astype(F32)
        part[dz, at.x] = total.astype(BF)
        begin(z_parts[w, dz])

    def sum_end(w, outs):
        part, _, z_recv = parts[w]
        total = part[0, at.x].astype(F32)
        for dz in range(1, nz):
            arrived(z_parts[w, dz])
            total = total + z_recv[dz - 1].astype(F32)
        for j, (ref, out) in enumerate(outs):
            ref[...] = total[:, j * E : (j + 1) * E]
            io.move(ref, out)

    io.moved(*attend_loads)
    mask = head_mask(t.heads_here, LR, E)
    mask_low = mask.astype(BF)
    scale = 1.0 / math.sqrt(HEAD_DIM)
    for i in range(G):
        q = spread_heads(n.query_v[i], mask_low)
        d = spread_heads(n.dmixed[i], mask_low)
        k, v = n.keys_v[i], n.values_v[i]
        probs = softmax(mt(q, k) * scale)
        d_probs = mt(d, v)
        inner = jnp.sum(probs * d_probs, axis=-1, keepdims=True)
        d_scores = (probs * (d_probs - inner)).astype(BF)
        d_query = gather_heads(mm(d_scores, k), mask, LR) * scale
        d_pair = jnp.concatenate([tm(d_scores, q) * scale, tm(probs.astype(BF), d)], axis=-1)
        for slot in range(H):
            rows = slice(slot * ML + i * pr, slot * ML + (i + 1) * pr)
            n.dkv[rows] = d_pair[slot * pr : (slot + 1) * pr].astype(BF)
        for head in range(H):
            rows = slice(H * pr + head * ll, H * pr + (head + 1) * ll)
            n.turn_kv[head, i * ll : (i + 1) * ll] = d_pair[rows]
            n.turn_q[head, i * ll : (i + 1) * ll, 0:E] = d_query[head * ll : (head + 1) * ll]
    if t.EP > E:
        n.turn_q[:, :, E : t.EP] = jnp.zeros((H, L, t.EP - E), F32)
    for slot in range(H):
        head = at.slots[slot]
        n.dkv[slot * ML + M : (slot + 1) * ML] = n.turn_kv[head].astype(BF)
        n.dq[slot * L : (slot + 1) * L] = n.turn_q[head].astype(BF)
    kv_lanes = pl.ds(pl.multiple_of(at.h * 2 * E, 128), 2 * E)
    q_lanes = pl.ds(pl.multiple_of(at.h * t.EP, 128), t.EP)
    turned = []
    for slot in range(1, H):
        peer = (at.r, at.slots[slot])
        turned.append(io.put(n.dkv.at[slot * ML : (slot + 1) * ML], n.dkv_full.at[:, kv_lanes], peer))
        turned.append(io.put(n.dq.at[slot * L : (slot + 1) * L], n.dq_full.at[:, q_lanes], peer))
    out_far = [io.plan(n.out_send.at[at.ys[d]], n.out_recv.at[d - 1], at.on_y(d)) for d in range(1, ny)]
    io.moved(norm_load)
    sum_start("kv", lambda lanes: n.norm_v[:, lanes], n.dkv[...])
    sum_start(
        "query",
        lambda lanes: jnp.concatenate([n.norm_v[slot * ML + M : (slot + 1) * ML, lanes] for slot in range(H)], axis=0),
        n.dq[:, 0:E],
    )
    base, offset = window_of(here, B, D)
    window = pl.ds(base, 256)
    io.moved(*own_loads)
    n.up_acc[...] = tm(n.ffn_v[0, :, window], n.ffn_v[1, :, 0:F])
    n.down_acc[...] = tm(n.dout_v[0, :, window], n.dout_v[1, :, 0:F])
    q_load = io.plan_move(n.wq, n.w_v.at[:, 0 : n.wq.shape[1]])
    media_out, lat_out = io.plan_move(n.drow.at[0:M], n.media_o), io.plan_move(n.drow.at[M:ML], n.lat_o)
    own_out = io.plan_move(n.out_own_v, n.out_o)
    vec_z = [io.plan(n.vec_sum.at[at.zs[d]], n.vec_z.at[d - 1], at.on_z(d)) for d in range(1, nz)]

    def back_slot(k):
        return (ny - k // nc) % ny * nc + k % nc

    vec_head = [io.plan(n.vec_own, n.vec_head.at[back_slot(k) - 1], (at.r, at.slots[k])) for k in range(1, H)]

    def norm_back_rows(raw, size, base, gain_row, extra):
        def step(rows, sums):
            grad_rows = pl.ds(pl.multiple_of(base + rows.start, 16), 16)
            hat, inv = norm_rows(raw[rows].astype(F32))
            grad = n.drow[grad_rows]
            product = grad * hat
            scaled = grad * n.vecs[gain_row : gain_row + 1]
            mean = jnp.mean(scaled, axis=-1, keepdims=True)
            second = jnp.mean(scaled * hat, axis=-1, keepdims=True)
            result = inv * (scaled - mean - hat * second)
            n.drow[grad_rows] = result if extra is None else result + extra[rows]
            return sums[0] + product[:8] + product[8:], sums[1] + grad[:8] + grad[8:]

        sums = sweep(0, size, step, (jnp.zeros((8, D), F32), jnp.zeros((8, D), F32)))
        return [jnp.sum(v, axis=0, keepdims=True) for v in sums]

    def own_gradients():
        n.dkv_full[:, kv_lanes] = n.dkv[0:ML]
        n.dq_full[:, q_lanes] = n.dq[0:L]
        io.moved(*row_loads)
        arrived(turned)
        n.drow[...] = mt(n.dkv_full[...], n.w_v[...])
        begin([q_load])
        spread(near)
        n.vec_own[0:1], n.vec_own[1:2] = norm_back_rows(n.media_v, M, 0, 0, None)
        begin([media_out])
        fetch(near)
        io.moved(q_load)
        n.drow[M:ML] += mt(n.dq_full[...], n.w_v[:, 0 : n.wq.shape[1]])
        n.vec_own[2:3], n.vec_own[3:4] = norm_back_rows(n.lat_v, L, M, 1, n.dres_v)
        begin([lat_out])
        n.vec_own[4:6] = n.fvec[0:2]
        n.vec_own[6:8] = jnp.zeros((2, D), F32)
        begin(vec_head)
        begin(out_far)

    def vectors_middle():
        arrived(vec_head)
        total = n.vec_own[...]
        for k in range(1, H):
            total = total + n.vec_head[k - 1]
        for z in range(nz):
            n.vec_sum[z] = total[:, z * span : (z + 1) * span]
        begin(vec_z)

    def own_output():
        arrived(out_far)
        total = n.out_own_v[...]
        for d in range(1, ny):
            total = total + n.out_recv[d - 1].astype(F32)
        n.out_own_v[...] = total
        begin([own_out])

    before, middle, after = [{index: [] for index in range(count)} for _ in range(3)]

    def late_quarters():
        for dz, dx in order[near:]:
            arrived([x_quarters[dz][nx - dx - 1]])
            begin(y_quarters[dz, dx])

    for index in range(count):
        before[index] += [lambda index=index: io.moved(*fetched[index])]
        if index + 1 < count and index != near - 1:
            before[index] += [lambda index=index: spread(index + 1)]
            middle[index] += [lambda index=index: fetch(index + 1)]
    middle[0] += [late_quarters]
    after[near - 1] += [lambda: sum_middle("kv", z_order[0]), out_middle]
    after[near - 1] += [lambda dz=dz: sum_middle("kv", dz) for dz in z_order[1:2]]
    after[near - 1] += [own_gradients]
    after[near - 1] += [lambda dz=dz: sum_middle("kv", dz) for dz in z_order[2:]]
    late = list(range(near, count))
    after[late[min(1, len(late) - 1)]] += [vectors_middle]
    after[late[0]] += [lambda dz=dz: sum_middle("query", dz) for dz in z_order[:-1]]
    middle[late[min(1, len(late) - 1)]] += [lambda: sum_middle("query", z_order[-1])]
    after[late[-1]] += [own_output]
    spread(0)
    fetch(0)
    io.moved(*ffn_loads)

    def at_index(index, actions):
        for k in range(count):
            if actions[k]:

                @pl.when(index == k)
                def _():
                    for action in actions[k]:
                        action()

    def group_step(index, carry):
        at_index(index, before)
        buf = lax.rem(index + 1, 2)
        value, slope = gelu_pair(mm(n.ffn_v[buf], n.wup_v[...]))
        n.down_acc[...] += tm(n.dout_v[buf, :, window], value.astype(BF))
        n.slope[...] = slope
        at_index(index, middle)
        d_hidden = (mt(n.dout_v[buf], n.wdown_v[...]) * n.slope[...]).astype(BF)
        n.up_acc[...] += tm(n.ffn_v[buf, :, window], d_hidden)
        at_index(index, after)
        return carry

    lax.fori_loop(0, count, group_step, 0)
    arrived(vec_z)
    total = n.vec_sum[at.z]
    for d in range(1, nz):
        total = total + n.vec_z[d - 1]
    n.vec_part[...] = total
    vec_x = [io.put(n.vec_part, n.vec_x.at[d - 1], at.on_x(d)) for d in range(1, nx)]
    own_rows = pl.ds(pl.multiple_of(offset, 8), B)
    io.move(n.up_acc.at[own_rows], n.up_grad)
    io.move(n.down_acc.at[own_rows], n.down_grad)
    out_end()
    sum_end("kv", [(n.grad_v.at[1], n.key_grad), (n.grad_v.at[2], n.value_grad)])
    arrived(vec_x)
    total = n.vec_part[...]
    for d in range(1, nx):
        total = total + n.vec_x[d - 1]
    n.vec_done[...] = total
    io.move(n.vec_done, n.vec_o)
    sum_end("query", [(n.grad_v.at[3], n.query_grad)])
    io.finish()


def backward(s, ins):
    t = sizes_of(s)
    ny, nc, nz, nx, G, H = t.ny, t.nc, t.nz, t.nx, t.G, t.H
    M, L, LR, GL, ML, D, E, F, B = t.M, t.L, t.LR, t.GL, t.ML, t.D, t.E, t.F, t.B
    fx, fz, fh = max(nx - 1, 1), max(nz - 1, 1), max(H - 1, 1)
    span = D // nz
    outs = dict(
        media_o=((M, D), F32), lat_o=((L, D), F32), query_grad=((B, E), F32), key_grad=((B, E), F32), value_grad=((B, E), F32),
        out_grad=((B, E), F32), up_grad=((B, F), F32), down_grad=((B, F), F32), vec_o=((8, span), F32), out_o=((L, D), F32),
        fall_b=((s.rows, GL, D), BF), dall_b=((s.rows, ny * L, D), BF),
    )
    scratch = dict(
        mix_v=((H, GL, E), BF), wout_v=((E, D), BF), dcols_v=((GL, E), BF), dmixed=((G, LR, E), BF),
        keys_v=((G, t.KC, E), BF), values_v=((G, t.KC, E), BF), query_v=((G, LR, E), BF), norm_v=((H * ML, D), BF),
        ffn_v=((2, GL, D), BF), dout_v=((2, GL, D), BF), wup_v=((D, F), BF),
        wdown_v=((F, D), BF), w_v=((D, max(2 * D, H * t.EP)), BF), media_v=((M, D), BF), lat_v=((L, D), BF), dres_v=((L, D), F32),
        dkv=((H * ML, 2 * E), BF), dq=((H * L, t.EP), BF), turn_kv=((H, L, 2 * E), F32), turn_q=((H, L, t.EP), F32),
        dkv_full=((ML, 2 * D), BF), dq_full=((L, H * t.EP), BF), grad_v=((4, B, E), F32), up_acc=((256, F), F32),
        down_acc=((256, F), F32), drow=((ML, D), F32), slope=((GL, F), F32), vec_own=((8, D), F32), vec_head=((fh, 8, D), F32),
        vec_sum=((nz, 8, span), F32), vec_z=((fz, 8, span), F32), vec_part=((8, span), F32), vec_x=((fx, 8, span), F32),
        vec_done=((8, span), F32), vecs=((8, D), F32), out_own_v=((L, D), F32), out_recv=((max(ny - 1, 1), L, D), BF),
        p_out=((nz, nx, B, E), BF), zr_out=((fz, nx, B, E), BF), xr_out=((fx, B, E), BF),
    )
    for w, lanes in (("kv", 2 * E), ("query", E)):
        scratch["p_" + w] = ((nz, nx, B, lanes), BF)
        scratch["xr_" + w] = ((nz, fx, B, lanes), BF)
        scratch["zr_" + w] = ((fz, B, lanes), BF)
    places = {"fvec": VMEM}
    cost = pl.CostEstimate(flops=30 * 10**9, bytes_accessed=8 * 10**7, transcendentals=10**6)
    return call(backward_kernel, s, "backward", 2, ins, outs, scratch, 300, places, 63, cost)


def finish_kernel(count, *refs):
    ins, outs, held = refs[:count], refs[count : 2 * count], refs[2 * count : 3 * count]
    read, write = refs[3 * count :]
    loads = [pltpu.make_async_copy(a, b, read.at[i]) for i, (a, b) in enumerate(zip(ins, held))]
    stores = [pltpu.make_async_copy(a, b, write.at[i]) for i, (a, b) in enumerate(zip(held, outs))]
    for copy in loads:
        copy.start()
    for load, store in zip(loads, stores):
        load.wait()
        store.start()
    for copy in stores:
        copy.wait()


def finish(arrays):
    count = len(arrays)
    return pl.pallas_call(
        functools.partial(finish_kernel, count),
        name="finish",
        out_shape=[jax.ShapeDtypeStruct(a.shape, a.dtype) for a in arrays],
        in_specs=[ANY] * count,
        out_specs=[ANY] * count,
        scratch_shapes=[pltpu.VMEM(a.shape, a.dtype) for a in arrays] + [pltpu.SemaphoreType.DMA((count,))] * 2,
        compiler_params=pltpu.CompilerParams(vmem_limit_bytes=62 << 20),
    )(*arrays)


def body(
    media, latents, counts, media_gain, media_shift, latent_gain, latent_shift, w_query, w_key, w_value, w_out,
    ffn_gain, ffn_shift, w_up, w_down, cotangent,
):
    rows, heads = lax.axis_size("rows"), lax.axis_size("head")
    at = Place(rows, heads)
    images, patch, width = media.shape
    lat = latents.shape[1]
    cols = width // heads
    s = types.SimpleNamespace(
        rows=rows, heads=heads, images=images, patch=patch, lat=lat, width=width, cols=cols, mine=w_up.shape[1] // heads
    )
    t = sizes_of(s)

    def columns(array):
        return array if t.aligned else lax.dynamic_slice_in_dim(array, at.h * cols, cols, 1)

    gains = dict(
        media_gain=media_gain, media_shift=media_shift, latent_gain=latent_gain, latent_shift=latent_shift,
        ffn_gain=ffn_gain, ffn_shift=ffn_shift,
    )
    rows_in = dict(media=media.reshape(-1, width), lat=latents.reshape(-1, width))
    a = forward(
        s,
        dict(
            rows_in, cot=cotangent.reshape(-1, width), counts=counts, **gains, wq=columns(w_query), wk=columns(w_key),
            wv=columns(w_value), wout=w_out, wup=w_up, wdown=w_down,
        ),
    )
    ins = dict(
        rows_in, media_gain=gains["media_gain"], latent_gain=gains["latent_gain"], fvec=a["fvec_o"], dres=a["dres_o"],
        key_norm=a["key_norm_o"], keys=a["keys_o"], values=a["values_o"], query=a["query_o"], mixed=a["mixed_o"],
        dattn=a["dattn_o"], ffn=a["ffn_o"], dout=a["dout_o"], act=a["act_o"], dhid=a["dhid_o"], dall=a["dall"], fall=a["fall"],
        wout=w_out, wup=w_up, wdown=w_down, out_own=a["out_o"], out_send=a["out_send_o"],
    )
    if t.aligned:
        ins.update(wk=w_key, wv=w_value, wq=w_query)
    else:
        pair = jnp.stack([w_key.reshape(width, heads, cols), w_value.reshape(width, heads, cols)], axis=2)
        padded = jnp.pad(w_query.reshape(width, heads, cols), ((0, 0), (0, 0), (0, t.EP - cols)))
        ins.update(wkv=pair.reshape(width, 2 * width), wq=padded.reshape(width, -1), dattn_cols=columns(a["dattn_o"]))
    b = backward(s, ins)
    share = width // (rows * heads)
    vector = lax.dynamic_slice_in_dim(b["vec_o"], (at.x * heads + at.h) * share, share, 1)
    names = ("out_o", "media_o", "lat_o", "query_grad", "key_grad", "value_grad", "out_grad", "up_grad", "down_grad")
    out, media_grad, latents_grad, query_grad, key_grad, value_grad, out_grad, up_grad, down_grad = finish([b[k] for k in names])
    return (
        out.reshape(latents.shape), media_grad.reshape(media.shape), latents_grad.reshape(latents.shape), vector[0], vector[1],
        vector[2], vector[3], query_grad, key_grad, value_grad, out_grad, vector[4], vector[5], up_grad, down_grad.T,
    )


def solution(mesh):
    row = P("rows", "head", None)
    whole = P()
    vector = P(("rows", "head"))
    grid = P("rows", "head")
    return jax.shard_map(
        body,
        mesh=mesh,
        in_specs=(row, row) + (whole,) * 13 + (row,),
        out_specs=(row, row, row, vector, vector, vector, vector, grid, grid, grid, grid, vector, vector, grid, P("head", "rows")),
        check_vma=False,
    )
```
